32 devices in a mesh: row: 16 (over z, y, x), col: 2 (over core).
Axes of the slice: x: 2, y: 2, z: 4, core: 2. Of those that a mesh axis runs over, the one named last changes fastest.
Arguments:
- inverse_block: bfloat16 [1280, 1280], P('row', 'col')
- factor_cols: bfloat16 [3, 1280, 512], P(None, 'col', 'row'), may hold values from -6 to 6
- occupancy: int32 [3, 10], replicated, may hold values 0 or 1
- row_block: int32 [3, 10], replicated, may hold values from 0 to 9, each once within a row
- coupling: bfloat16 [2, 512, 512], replicated, may hold values from -0.25 to 0.25
- diag_inverse: float32 [3, 512, 512], P(None, None, 'col'), may hold values from -6 to 6
Outputs:
- columns: float32 [3, 1280, 512], P(None, ('row', 'col'))
- diagonals: float32 [3, 512, 512], P(None, None, 'col')
The draws below stay inside these ranges and needn't reach their ends.
Inputs may be any that keep to these rules, and one draw needn't show every extreme that they name: `row_block`: each row names every one of the 10 row blocks exactly once.
All inputs are finite; a program needn't handle non-finite values.
Results may differ from the reference program's by a relative error of at most 0.0003.
Values may be sent and summed in bfloat16 or wider, within the bound.
No kernel may reach another device: no remote copies, remote signals or barrier semaphores. Data moves between devices by JAX's collectives and lax.ppermute only.
A program may use at most 64 MiB of HBM per device.

```python
import jax
import jax.numpy as jnp
from jax import lax

W = 512
SUPER = 3
ROWS = 1280
NB = 10


def draw_inverse_block(key, part):
    first_key, second_key = jax.random.split(jax.random.fold_in(key, 7))
    spread = jax.random.normal(first_key, (ROWS, ROWS), jnp.float32)
    leading = jax.random.uniform(second_key, (ROWS,), jnp.float32, 1.0, 3.0)
    spread = spread * ROWS ** (-0.5)
    steps = jnp.arange(ROWS, dtype=jnp.int32)
    return spread.at[steps, steps].add(leading).astype(jnp.bfloat16)


def plant(entries, stream_key, least, high):
    extent = entries.shape
    index_at = [jax.random.randint(jax.random.fold_in(stream_key, axis), (), 0, extent[axis]) for axis in range(len(extent))]
    entries = entries.at[tuple(index_at)].set(least)
    longest = extent.index(max(extent))
    index_at[longest] = (index_at[longest] + 1) % extent[longest]
    return entries.at[tuple(index_at)].set(high)


def steps_of(own_key, extent, cuts, low, high):
    level, own = 1.0, jax.random.fold_in(own_key, 6)
    for dim, blocks in cuts:
        steps = jnp.exp(jax.random.uniform(jax.random.fold_in(own, dim), (blocks,), jnp.float32, low / len(cuts), high / len(cuts)))
        level = level * jnp.repeat(steps, extent[dim] // blocks).reshape([-1 if axis == dim else 1 for axis in range(len(extent))])
    return level


def normal_values(own_key, shape, scale, most, shards=(), kind=jnp.bfloat16):
    factor_of = steps_of(own_key, shape, shards, -0.22, 0.18) if shards else 1.0
    array = jax.random.normal(own_key, shape, jnp.float32) * scale * factor_of
    return jnp.minimum(jnp.maximum(array, -most), most).astype(kind)


def setup_inputs(seed: int = 0) -> dict:
    streams_of = jax.random.split(jax.random.key(seed), 7)
    inverse_block = draw_inverse_block(jax.random.fold_in(streams_of[6], 71), 0)
    factor_cols = normal_values(streams_of[1], (SUPER, ROWS, W), 1.0, 6.0, ((1, 2), (2, 16)))
    occupancy = plant((jax.random.randint(streams_of[2], (SUPER, NB), 0, 20) < 17).astype(jnp.int32), jax.random.fold_in(streams_of[2], 1), 0, 1)
    row_block = jax.vmap(lambda own: jax.random.permutation(own, NB))(jax.random.split(streams_of[3], SUPER)).reshape((SUPER, NB)).astype(jnp.int32)
    coupling = normal_values(streams_of[4], (SUPER - 1, W, W), W ** -0.5, 0.25)
    diag_inverse = normal_values(streams_of[5], (SUPER, W, W), 1.0, 6.0, ((2, 2),), jnp.float32)
    return {"inverse_block": inverse_block, "factor_cols": factor_cols, "occupancy": occupancy, "row_block": row_block, "coupling": coupling, "diag_inverse": diag_inverse}


def reference(inverse_block, factor_cols, occupancy, row_block, coupling, diag_inverse):
    highest = lax.Precision.HIGHEST
    nblocks = ROWS // 128
    previous = None
    chain_prev = None
    column_list = []
    diag_list = []
    for position in range(SUPER):
        blocks = factor_cols[position].reshape(nblocks, 128, W) * occupancy[position][:, None, None].astype(jnp.bfloat16)
        placed = jnp.zeros_like(blocks).at[row_block[position]].set(blocks).reshape(ROWS, W)
        product = jnp.dot(inverse_block, placed, preferred_element_type=jnp.float32)
        if position == 0:
            coupled = jnp.zeros((ROWS, W), jnp.float32)
        else:
            coupled = jnp.dot(previous, coupling[position - 1].astype(jnp.float32), precision=highest)
        current = -(product + coupled)
        own = placed.astype(jnp.float32)
        inner = jnp.dot(own.T, current, precision=highest) - jnp.dot(coupled.T, own, precision=highest)
        diag_now = diag_inverse[position] - inner / ROWS
        if position > 0:
            link = coupling[position - 1].astype(jnp.float32)
            diag_now = diag_now + jnp.dot(link.T, jnp.dot(chain_prev, link, precision=highest), precision=highest)
        column_list.append(current)
        diag_list.append(diag_now)
        previous = current
        chain_prev = diag_now
    return jnp.stack(column_list), jnp.stack(diag_list)
```

```python
import functools

import jax
import jax.numpy as jnp
from jax import lax
from jax.experimental import pallas as pl
from jax.experimental.pallas import tpu as pltpu
from jax.sharding import PartitionSpec as P

highest = lax.Precision.HIGHEST
f32 = jnp.float32
bf16 = jnp.bfloat16

REPLICATE_BYTES = 12 * 2**20


def routed(gathered, occupancy, row_block, nblocks):
    count = gathered.shape[0]
    width_part = gathered.shape[1] // (nblocks * 128)
    blocks = gathered.reshape(count, nblocks, 128, width_part)
    levels = lax.broadcasted_iota(jnp.int32, (count, nblocks, nblocks), 1)
    picks = ((row_block[:, None, :] == levels) & (occupancy[:, None, :] > 0)).astype(jnp.bfloat16)
    placed = jnp.einsum("kqb,kbtx->kxqt", picks, blocks, preferred_element_type=jnp.float32)
    return placed.astype(jnp.bfloat16).reshape(count, width_part, nblocks * 128)


def split_rows(placed, column, row_parts, col_parts, tile):
    count, width_part, total = placed.shape
    span = total // col_parts
    column_part = lax.dynamic_slice_in_dim(placed, column * span, span, 2)
    grid = placed.reshape(count, width_part, row_parts, col_parts, tile)
    mine = lax.dynamic_index_in_dim(grid, column, 3, keepdims=False)
    return (column_part, jnp.transpose(mine, (0, 2, 1, 3)))


def make_term(inverse_block, column_full):
    return lax.dot_general(
        inverse_block, column_full, (((1,), (2,)), ((), ())), preferred_element_type=jnp.float32
    )


def local_step(summed, own_rows, previous, link, diag_part, column, row_first, rows_total):
    if link is None:
        coupled = jnp.zeros_like(summed)
    else:
        coupled = jnp.dot(previous, link.astype(jnp.float32), precision=highest)
    current = -(summed + coupled)
    own = own_rows.astype(jnp.float32)
    inner = jnp.dot(own, current, precision=highest) - jnp.dot(coupled.T, own.T, precision=highest)
    width = summed.shape[1]
    diag_cols = diag_part.shape[1]
    embedded = lax.dynamic_update_slice(
        jnp.zeros((width, width), jnp.float32), diag_part, (0, column * diag_cols)
    )
    return (current, row_first * embedded - inner / rows_total)


def chain_diag(total, chain_prev, link):
    if link is None:
        return total
    link_wide = link.astype(jnp.float32)
    return total + jnp.dot(
        link_wide.T, jnp.dot(chain_prev, link_wide, precision=highest), precision=highest
    )


def grid_plan(inverse_block, factor_cols, occupancy, row_block, coupling, diag_inverse):
    column = lax.axis_index("col")
    row_first = (lax.axis_index("row") == 0).astype(jnp.float32)
    row_parts = lax.axis_size("row")
    col_parts = lax.axis_size("col")
    local_rows = inverse_block.shape[0]
    rows_total = local_rows * row_parts
    supers, span, width_part = factor_cols.shape
    width = width_part * row_parts
    tile = local_rows // col_parts
    nblocks = occupancy.shape[1]
    diag_cols = diag_inverse.shape[2]
    flat = factor_cols.reshape(supers, span * width_part)
    column_list = []
    partial_list = []
    previous = None
    gathered = lax.all_gather(flat, "col", axis=1, tiled=True)
    placed = routed(gathered, occupancy, row_block, nblocks)
    column_part, outgoing = split_rows(placed, column, row_parts, col_parts, tile)
    column_full = lax.all_gather(column_part, "row", axis=1, tiled=True)
    arrived = lax.all_to_all(outgoing, "row", split_axis=1, concat_axis=1, tiled=True)
    own_all = arrived.reshape(supers, width, tile)
    summed = lax.psum_scatter(
        make_term(inverse_block, column_full), "col", scatter_dimension=0, tiled=True
    )
    for position in range(supers):
        link = None if position == 0 else coupling[position - 1]
        current, partial_value = local_step(
            summed[:, position, :],
            own_all[position],
            previous,
            link,
            diag_inverse[position],
            column,
            row_first,
            rows_total,
        )
        column_list.append(current)
        partial_list.append(partial_value)
        previous = current
    diag_list = []
    totals = lax.psum(jnp.stack(partial_list), ("row", "col"))
    chain_prev = None
    for position in range(supers):
        link = None if position == 0 else coupling[position - 1]
        diag_now = chain_diag(totals[position], chain_prev, link)
        diag_list.append(lax.dynamic_slice_in_dim(diag_now, column * diag_cols, diag_cols, 1))
        chain_prev = diag_now
    diagonals = jnp.stack(diag_list)
    return (jnp.stack(column_list), diagonals)


def swap(value, axis, bit, parts):
    return lax.ppermute(value, axis, [(i, i ^ bit) for i in range(parts)])


def spread(own, row_parts):
    outer = row_parts // 4
    line = jnp.stack([own] + [swap(own, "row", 4 * k, row_parts) for k in range(1, outer)])
    over_x = swap(line, "row", 1, row_parts)
    over_y = swap(line, "row", 2, row_parts)
    half = outer // 2
    far_a = swap(over_y[:half], "row", 1, row_parts)
    far_b = swap(over_x[half:], "row", 2, row_parts)
    return [(0, 0, line), (1, 0, over_x), (2, 0, over_y), (3, 0, far_a), (3, half, far_b)]


def split2(value):
    high = value.astype(bf16)
    return high, (value - high.astype(f32)).astype(bf16)


def nn(a, b):
    return lax.dot_general(a, b, (((1,), (0,)), ((), ())), preferred_element_type=f32)


def nt(a, b):
    return lax.dot_general(a, b, (((1,), (1,)), ((), ())), preferred_element_type=f32)


def nn2(pair, b):
    return nn(pair[0], b) + nn(pair[1], b)


def nn2r(a, pair):
    return nn(a, pair[0]) + nn(a, pair[1])


def local_kernel(groups, dims, *refs):
    supers, width, rows, span, chunk = dims
    n = len(groups)
    place_ref, occ_ref, block_ref = refs[:3]
    f_refs = refs[3 : 3 + 2 * n]
    z_refs = refs[3 + 2 * n : 3 + 4 * n]
    link_ref, link_t_ref, diag_ref, diag_other_ref = refs[3 + 4 * n : 7 + 4 * n]
    col_out, diag_out = refs[7 + 4 * n : 9 + 4 * n]
    (f_all, z_all, pt, c0h, c0l, c1h, c1l, p1h, p1l, c2h, c2l, tmp, f_sem, z_sem) = refs[9 + 4 * n :]
    row = place_ref[0]
    col = place_ref[1]
    local_rows = z_refs[0].shape[1]
    part = f_refs[0].shape[3]
    half_w = width // 2
    f_copies, z_copies = [], []
    for side in range(2):
        target = col if side == 0 else 1 - col
        for g, (plane, first, count) in enumerate(groups):
            for k in range(count):
                owner = row ^ (4 * (first + k) + plane)
                f_copies.append(pltpu.make_async_copy(f_refs[side * n + g].at[k], f_all.at[target, owner], f_sem))
                z_copies.append(
                    pltpu.make_async_copy(
                        z_refs[side * n + g].at[k],
                        z_all.at[
                            pl.ds(pl.multiple_of(owner * local_rows, local_rows), local_rows),
                            pl.ds(pl.multiple_of(target * span, span), span),
                        ],
                        z_sem,
                    )
                )
    for copy in f_copies + z_copies:
        copy.start()
    for copy in f_copies:
        copy.wait()
    per_side = span // 128
    for s in range(supers):
        for b in range(2 * per_side):
            lane = (b % per_side) * 128
            blk = f_all[b // per_side, :, s, :, lane : lane + 128].reshape(width, 128)
            keep = jnp.where(occ_ref[s * 2 * per_side + b] > 0, blk, jnp.zeros_like(blk))
            pt[s, :, pl.ds(pl.multiple_of(block_ref[s * 2 * per_side + b] * 128, 128), 128)] = keep
    for copy in z_copies:
        copy.wait()
    c_rows = pl.ds(pl.multiple_of(col * half_w, half_w), half_w)

    def step(m, carry):
        at = pl.ds(pl.multiple_of(m * chunk, chunk), chunk)
        zm = z_all[at, :]
        cols0 = split2(-nt(zm, pt[0]))
        c0h[at, :], c0l[at, :] = cols0
        tmp[...] = nn2(cols0, link_ref[0])
        p1h[at, :], p1l[at, :] = split2(tmp[...])
        tmp[...] += nt(zm, pt[1])
        cols1 = split2(-tmp[...])
        c1h[at, :], c1l[at, :] = cols1
        cols2 = -(nt(zm, pt[2, c_rows, :]) + nn2(cols1, link_ref[1, :, c_rows]))
        c2h[at, :], c2l[at, :] = split2(cols2)
        return carry

    lax.fori_loop(0, rows // chunk, step, 0)

    own = pl.ds(pl.multiple_of(row * local_rows, local_rows), local_rows)
    tile = local_rows // 2
    o1 = (c1h[own, :], c1l[own, :])
    mine = [
        c0h[own, :].astype(f32) + c0l[own, :].astype(f32),
        o1[0].astype(f32) + o1[1].astype(f32),
        -(nt(z_all[own, :], pt[2]) + nn2(o1, link_ref[1])),
    ]
    for s in range(supers):
        col_out[s] = jnp.where(col == 0, mine[s][:tile], mine[s][tile:])

    scale = 1.0 / rows
    whole = lambda s: (
        jnp.where(col == 0, diag_ref[s], diag_other_ref[s]),
        jnp.where(col == 0, diag_other_ref[s], diag_ref[s]),
    )
    d0 = jnp.concatenate(whole(0), axis=1) - nn2r(pt[0], (c0h[...], c0l[...])) * scale
    u1 = nn2r(pt[1], (p1h[...], p1l[...]))
    i1 = nn2r(pt[1], (c1h[...], c1l[...])) - u1.T
    d1 = jnp.concatenate(whole(1), axis=1) - i1 * scale + nn2r(link_t_ref[0], split2(nn2(split2(d0), link_ref[0])))
    n2 = nn2r(pt[2, c_rows, :], (c1h[...], c1l[...]))
    i2 = nn2r(pt[2], (c2h[...], c2l[...])) - nn2(split2(n2), link_ref[1]).T
    d2 = diag_ref[2] - i2 * scale + nn2r(link_t_ref[1], split2(nn2(split2(d1), link_ref[1, :, c_rows])))
    diag_out[0] = jnp.where(col == 0, d0[:, :half_w], d0[:, half_w:])
    diag_out[1] = jnp.where(col == 0, d1[:, :half_w], d1[:, half_w:])
    diag_out[2] = d2


def replicated_plan(inverse_block, factor_cols, occupancy, row_block, coupling, diag_inverse):
    row_parts = lax.axis_size("row")
    row = lax.axis_index("row")
    col = lax.axis_index("col")
    supers, span, part = factor_cols.shape
    width = part * row_parts
    local_rows = inverse_block.shape[0]
    rows = local_rows * row_parts
    f_groups = spread(jnp.transpose(factor_cols, (0, 2, 1)), row_parts)
    z_groups = spread(inverse_block, row_parts)
    across = lambda value: lax.ppermute(value, "col", [(0, 1), (1, 0)])
    diag_other = across(diag_inverse[: supers - 1])
    f_values = [v for _, _, v in f_groups]
    z_values = [v for _, _, v in z_groups]
    f_values = f_values + [across(v) for v in f_values]
    z_values = z_values + [across(v) for v in z_values]
    groups = tuple((plane, first, v.shape[0]) for plane, first, v in f_groups)
    chunk = 256
    any_spec = pl.BlockSpec(memory_space=pl.ANY)
    smem = pl.BlockSpec(memory_space=pltpu.SMEM)
    vmem = pl.BlockSpec(memory_space=pltpu.VMEM)
    wide = lambda cols: pltpu.VMEM((rows, cols), bf16)
    return pl.pallas_call(
        functools.partial(local_kernel, groups, (supers, width, rows, span, chunk)),
        out_shape=(
            jax.ShapeDtypeStruct((supers, local_rows // 2, width), f32),
            jax.ShapeDtypeStruct((supers, width, width // 2), f32),
        ),
        in_specs=[smem] * 3 + [any_spec] * (4 * len(groups)) + [vmem] * 4,
        out_specs=(vmem, vmem),
        scratch_shapes=[
            pltpu.VMEM((2, row_parts, supers, part, span), bf16),
            pltpu.VMEM((rows, 2 * span), bf16),
            pltpu.VMEM((supers, width, rows), bf16),
            wide(width), wide(width), wide(width), wide(width), wide(width), wide(width),
            wide(width // 2), wide(width // 2),
            pltpu.VMEM((chunk, width), f32),
            pltpu.SemaphoreType.DMA,
            pltpu.SemaphoreType.DMA,
        ],
        compiler_params=pltpu.CompilerParams(vmem_limit_bytes=56 * 2**20),
        name="selected_inverse",
    )(
        jnp.stack([row, col]).astype(jnp.int32), occupancy.reshape(-1), row_block.reshape(-1),
        *f_values, *z_values,
        coupling, jnp.transpose(coupling, (0, 2, 1)), diag_inverse, diag_other,
    )


def solution(mesh):
    row_parts, col_parts = mesh.shape["row"], mesh.shape["col"]
    in_specs = (P("row", "col"), P(None, "col", "row"), P(), P(), P(), P(None, None, "col"))
    out_specs = (P(None, ("row", "col"), None), P(None, None, "col"))

    def per_device(inverse_block, factor_cols, *rest):
        held = (inverse_block.size + factor_cols.size) * 2 * row_parts * col_parts
        fits = held <= REPLICATE_BYTES and col_parts == 2 and row_parts in (8, 16, 32)
        plan = replicated_plan if fits else grid_plan
        return plan(inverse_block, factor_cols, *rest)

    return jax.shard_map(
        per_device, mesh=mesh, in_specs=in_specs, out_specs=out_specs, check_vma=False
    )
```

```python
import functools

import jax
import jax.numpy as jnp
from jax import lax
from jax.experimental import pallas as pl
from jax.experimental.pallas import tpu as pltpu
from jax.sharding import PartitionSpec as P

highest = lax.Precision.HIGHEST
f32 = jnp.float32
bf16 = jnp.bfloat16

REPLICATE_BYTES = 12 * 2**20


def routed(gathered, occupancy, row_block, nblocks):
    count = gathered.shape[0]
    width_part = gathered.shape[1] // (nblocks * 128)
    blocks = gathered.reshape(count, nblocks, 128, width_part)
    levels = lax.broadcasted_iota(jnp.int32, (count, nblocks, nblocks), 1)
    picks = ((row_block[:, None, :] == levels) & (occupancy[:, None, :] > 0)).astype(jnp.bfloat16)
    placed = jnp.einsum("kqb,kbtx->kxqt", picks, blocks, preferred_element_type=jnp.float32)
    return placed.astype(jnp.bfloat16).reshape(count, width_part, nblocks * 128)


def split_rows(placed, column, row_parts, col_parts, tile):
    count, width_part, total = placed.shape
    span = total // col_parts
    column_part = lax.dynamic_slice_in_dim(placed, column * span, span, 2)
    grid = placed.reshape(count, width_part, row_parts, col_parts, tile)
    mine = lax.dynamic_index_in_dim(grid, column, 3, keepdims=False)
    return (column_part, jnp.transpose(mine, (0, 2, 1, 3)))


def make_term(inverse_block, column_full):
    return lax.dot_general(
        inverse_block, column_full, (((1,), (2,)), ((), ())), preferred_element_type=jnp.float32
    )


def local_step(summed, own_rows, previous, link, diag_part, column, row_first, rows_total):
    if link is None:
        coupled = jnp.zeros_like(summed)
    else:
        coupled = jnp.dot(previous, link.astype(jnp.float32), precision=highest)
    current = -(summed + coupled)
    own = own_rows.astype(jnp.float32)
    inner = jnp.dot(own, current, precision=highest) - jnp.dot(coupled.T, own.T, precision=highest)
    width = summed.shape[1]
    diag_cols = diag_part.shape[1]
    embedded = lax.dynamic_update_slice(
        jnp.zeros((width, width), jnp.float32), diag_part, (0, column * diag_cols)
    )
    return (current, row_first * embedded - inner / rows_total)


def chain_diag(total, chain_prev, link):
    if link is None:
        return total
    link_wide = link.astype(jnp.float32)
    return total + jnp.dot(
        link_wide.T, jnp.dot(chain_prev, link_wide, precision=highest), precision=highest
    )


def grid_plan(inverse_block, factor_cols, occupancy, row_block, coupling, diag_inverse):
    column = lax.axis_index("col")
    row_first = (lax.axis_index("row") == 0).astype(jnp.float32)
    row_parts = lax.axis_size("row")
    col_parts = lax.axis_size("col")
    local_rows = inverse_block.shape[0]
    rows_total = local_rows * row_parts
    supers, span, width_part = factor_cols.shape
    width = width_part * row_parts
    tile = local_rows // col_parts
    nblocks = occupancy.shape[1]
    diag_cols = diag_inverse.shape[2]
    flat = factor_cols.reshape(supers, span * width_part)
    column_list = []
    partial_list = []
    previous = None
    gathered = lax.all_gather(flat, "col", axis=1, tiled=True)
    placed = routed(gathered, occupancy, row_block, nblocks)
    column_part, outgoing = split_rows(placed, column, row_parts, col_parts, tile)
    column_full = lax.all_gather(column_part, "row", axis=1, tiled=True)
    arrived = lax.all_to_all(outgoing, "row", split_axis=1, concat_axis=1, tiled=True)
    own_all = arrived.reshape(supers, width, tile)
    summed = lax.psum_scatter(
        make_term(inverse_block, column_full), "col", scatter_dimension=0, tiled=True
    )
    for position in range(supers):
        link = None if position == 0 else coupling[position - 1]
        current, partial_value = local_step(
            summed[:, position, :],
            own_all[position],
            previous,
            link,
            diag_inverse[position],
            column,
            row_first,
            rows_total,
        )
        column_list.append(current)
        partial_list.append(partial_value)
        previous = current
    diag_list = []
    totals = lax.psum(jnp.stack(partial_list), ("row", "col"))
    chain_prev = None
    for position in range(supers):
        link = None if position == 0 else coupling[position - 1]
        diag_now = chain_diag(totals[position], chain_prev, link)
        diag_list.append(lax.dynamic_slice_in_dim(diag_now, column * diag_cols, diag_cols, 1))
        chain_prev = diag_now
    diagonals = jnp.stack(diag_list)
    return (jnp.stack(column_list), diagonals)


def swap(value, axis, bit, parts):
    return lax.ppermute(value, axis, [(i, i ^ bit) for i in range(parts)])


def along_line(own, row_parts):
    outer = row_parts // 4
    parts = [own] + [swap(own, "row", 4 * k, row_parts) for k in range(1, outer)]
    return jnp.stack(parts[: outer // 2]), jnp.stack(parts[outer // 2 :])


def over_plane(low, high, row_parts):
    x_high = swap(high, "row", 1, row_parts)
    y_low = swap(low, "row", 2, row_parts)
    x_low = swap(low, "row", 1, row_parts)
    y_high = swap(high, "row", 2, row_parts)
    far_low = swap(y_low, "row", 1, row_parts)
    far_high = swap(x_high, "row", 2, row_parts)
    return [x_low, x_high, y_low, y_high, far_low, far_high]


def split2(value):
    high = value.astype(bf16)
    return high, (value - high.astype(f32)).astype(bf16)


def nn(a, b):
    return lax.dot_general(a, b, (((1,), (0,)), ((), ())), preferred_element_type=f32)


def nt(a, b):
    return lax.dot_general(a, b, (((1,), (1,)), ((), ())), preferred_element_type=f32)


def nn2(pair, b):
    return nn(pair[0], b) + nn(pair[1], b)


def nn2r(a, pair):
    return nn(a, pair[0]) + nn(a, pair[1])


def local_kernel(groups, dims, *refs):
    supers, width, rows, span, chunk = dims
    n = len(groups)
    occ_ref, block_ref = refs[:2]
    f_refs = refs[2 : 2 + 2 * n]
    z_refs = refs[2 + 2 * n : 2 + 4 * n]
    link_ref, diag_ref, diag_other_ref = refs[2 + 4 * n : 5 + 4 * n]
    col_out, diag_out = refs[5 + 4 * n : 7 + 4 * n]
    (f_all, z_all, pt, c0h, c0l, c1h, c1l, p1h, p1l, c2h, c2l, tmp, f_sem, z_sem) = refs[7 + 4 * n :]
    row = lax.axis_index("row")
    col = lax.axis_index("col")
    local_rows = z_refs[0].shape[1]
    part = f_refs[0].shape[3]
    half_w = width // 2
    f_copies, z_copies = [], []
    for side in range(2):
        target = col if side == 0 else 1 - col
        for g, (plane, first, count) in enumerate(groups):
            for k in range(count):
                owner = row ^ (4 * (first + k) + plane)
                f_copies.append(pltpu.make_async_copy(f_refs[side * n + g].at[k], f_all.at[target, owner], f_sem))
                z_copies.append(
                    pltpu.make_async_copy(
                        z_refs[side * n + g].at[k],
                        z_all.at[
                            pl.ds(pl.multiple_of(owner * local_rows, local_rows), local_rows),
                            pl.ds(pl.multiple_of(target * span, span), span),
                        ],
                        z_sem,
                    )
                )
    for copy in f_copies + z_copies:
        copy.start()
    for copy in f_copies:
        copy.wait()
    per_side = span // 128
    for s in range(supers):
        for b in range(2 * per_side):
            lane = (b % per_side) * 128
            blk = f_all[b // per_side, :, s, :, lane : lane + 128].reshape(width, 128)
            keep = jnp.where(occ_ref[s, b] > 0, blk, jnp.zeros_like(blk))
            pt[s, :, pl.ds(pl.multiple_of(block_ref[s, b] * 128, 128), 128)] = keep
    for copy in z_copies:
        copy.wait()
    c_rows = pl.ds(pl.multiple_of(col * half_w, half_w), half_w)

    def step(m, carry):
        at = pl.ds(pl.multiple_of(m * chunk, chunk), chunk)
        zm = z_all[at, :]
        cols0 = split2(-nt(zm, pt[0]))
        c0h[at, :], c0l[at, :] = cols0
        tmp[...] = nn2(cols0, link_ref[0])
        p1h[at, :], p1l[at, :] = split2(tmp[...])
        tmp[...] += nt(zm, pt[1])
        cols1 = split2(-tmp[...])
        c1h[at, :], c1l[at, :] = cols1
        cols2 = -(nt(zm, pt[2, c_rows, :]) + nn2(cols1, link_ref[1, :, c_rows]))
        c2h[at, :], c2l[at, :] = split2(cols2)
        return carry

    lax.fori_loop(0, rows // chunk, step, 0)

    own = pl.ds(pl.multiple_of(row * local_rows, local_rows), local_rows)
    tile = local_rows // 2
    o1 = (c1h[own, :], c1l[own, :])
    mine = [
        c0h[own, :].astype(f32) + c0l[own, :].astype(f32),
        o1[0].astype(f32) + o1[1].astype(f32),
        -(nt(z_all[own, :], pt[2]) + nn2(o1, link_ref[1])),
    ]
    for s in range(supers):
        col_out[s] = jnp.where(col == 0, mine[s][:tile], mine[s][tile:])

    scale = 1.0 / rows
    whole = lambda s: (
        jnp.where(col == 0, diag_ref[s], diag_other_ref[s]),
        jnp.where(col == 0, diag_other_ref[s], diag_ref[s]),
    )
    d0 = jnp.concatenate(whole(0), axis=1) - nn2r(pt[0], (c0h[...], c0l[...])) * scale
    u1 = nn2r(pt[1], (p1h[...], p1l[...]))
    i1 = nn2r(pt[1], (c1h[...], c1l[...])) - u1.T
    d1 = jnp.concatenate(whole(1), axis=1) - i1 * scale + nn2r(link_ref[0].T, split2(nn2(split2(d0), link_ref[0])))
    n2 = nn2r(pt[2, c_rows, :], (c1h[...], c1l[...]))
    i2 = nn2r(pt[2], (c2h[...], c2l[...])) - nn2(split2(n2), link_ref[1]).T
    d2 = diag_ref[2] - i2 * scale + nn2r(link_ref[1].T, split2(nn2(split2(d1), link_ref[1, :, c_rows])))
    diag_out[0] = jnp.where(col == 0, d0[:, :half_w], d0[:, half_w:])
    diag_out[1] = jnp.where(col == 0, d1[:, :half_w], d1[:, half_w:])
    diag_out[2] = d2


def replicated_plan(inverse_block, factor_cols, occupancy, row_block, coupling, diag_inverse):
    row_parts = lax.axis_size("row")
    supers, span, part = factor_cols.shape
    width = part * row_parts
    local_rows = inverse_block.shape[0]
    rows = local_rows * row_parts
    f_low, f_high = along_line(jnp.transpose(factor_cols, (0, 2, 1)), row_parts)
    f_low, f_high, own_block = lax.optimization_barrier((f_low, f_high, inverse_block))
    f_plane = over_plane(f_low, f_high, row_parts)
    z_low, z_high = along_line(own_block, row_parts)
    z_low, z_high, *f_plane[:4] = lax.optimization_barrier((z_low, z_high, *f_plane[:4]))
    z_plane = over_plane(z_low, z_high, row_parts)
    across = lambda value: lax.ppermute(value, "col", [(0, 1), (1, 0)])
    diag_other = across(diag_inverse)
    f_values = [f_low, f_high] + f_plane
    z_values = [z_low, z_high] + z_plane
    f_values = f_values + [across(v) for v in f_values]
    z_values = z_values + [across(v) for v in z_values]
    half = row_parts // 8
    groups = tuple((plane, first, half) for plane in range(4) for first in (0, half))
    chunk = rows // 2
    any_spec = pl.BlockSpec(memory_space=pl.ANY)
    smem = pl.BlockSpec(memory_space=pltpu.SMEM)
    vmem = pl.BlockSpec(memory_space=pltpu.VMEM)
    wide = lambda cols: pltpu.VMEM((rows, cols), bf16)
    return pl.pallas_call(
        functools.partial(local_kernel, groups, (supers, width, rows, span, chunk)),
        out_shape=(
            jax.ShapeDtypeStruct((supers, local_rows // 2, width), f32),
            jax.ShapeDtypeStruct((supers, width, width // 2), f32),
        ),
        in_specs=[smem] * 2 + [any_spec] * (4 * len(groups)) + [vmem] * 3,
        out_specs=(vmem, vmem),
        scratch_shapes=[
            pltpu.VMEM((2, row_parts, supers, part, span), bf16),
            pltpu.VMEM((rows, 2 * span), bf16),
            pltpu.VMEM((supers, width, rows), bf16),
            wide(width), wide(width), wide(width), wide(width), wide(width), wide(width),
            wide(width // 2), wide(width // 2),
            pltpu.VMEM((chunk, width), f32),
            pltpu.SemaphoreType.DMA,
            pltpu.SemaphoreType.DMA,
        ],
        compiler_params=pltpu.CompilerParams(vmem_limit_bytes=40 * 2**20),
        name="selected_inverse",
    )(
        occupancy, row_block,
        *f_values, *z_values,
        coupling, diag_inverse, diag_other,
    )


def solution(mesh):
    row_parts, col_parts = mesh.shape["row"], mesh.shape["col"]
    in_specs = (P("row", "col"), P(None, "col", "row"), P(), P(), P(), P(None, None, "col"))
    out_specs = (P(None, ("row", "col"), None), P(None, None, "col"))

    def per_device(inverse_block, factor_cols, *rest):
        held = (inverse_block.size + factor_cols.size) * 2 * row_parts * col_parts
        fits = held <= REPLICATE_BYTES and col_parts == 2 and row_parts in (8, 16, 32)
        plan = replicated_plan if fits else grid_plan
        return plan(inverse_block, factor_cols, *rest)

    return jax.shard_map(
        per_device, mesh=mesh, in_specs=in_specs, out_specs=out_specs, check_vma=False
    )
```

```python
import functools

import jax
import jax.numpy as jnp
from jax import lax
from jax.experimental import pallas as pl
from jax.experimental.pallas import tpu as pltpu
from jax.sharding import PartitionSpec as P

highest = lax.Precision.HIGHEST
f32 = jnp.float32
bf16 = jnp.bfloat16

REPLICATE_BYTES = 12 * 2**20


def routed(gathered, occupancy, row_block, nblocks):
    count = gathered.shape[0]
    width_part = gathered.shape[1] // (nblocks * 128)
    blocks = gathered.reshape(count, nblocks, 128, width_part)
    levels = lax.broadcasted_iota(jnp.int32, (count, nblocks, nblocks), 1)
    picks = ((row_block[:, None, :] == levels) & (occupancy[:, None, :] > 0)).astype(jnp.bfloat16)
    placed = jnp.einsum("kqb,kbtx->kxqt", picks, blocks, preferred_element_type=jnp.float32)
    return placed.astype(jnp.bfloat16).reshape(count, width_part, nblocks * 128)


def split_rows(placed, column, row_parts, col_parts, tile):
    count, width_part, total = placed.shape
    span = total // col_parts
    column_part = lax.dynamic_slice_in_dim(placed, column * span, span, 2)
    grid = placed.reshape(count, width_part, row_parts, col_parts, tile)
    mine = lax.dynamic_index_in_dim(grid, column, 3, keepdims=False)
    return (column_part, jnp.transpose(mine, (0, 2, 1, 3)))


def make_term(inverse_block, column_full):
    return lax.dot_general(
        inverse_block, column_full, (((1,), (2,)), ((), ())), preferred_element_type=jnp.float32
    )


def local_step(summed, own_rows, previous, link, diag_part, column, row_first, rows_total):
    if link is None:
        coupled = jnp.zeros_like(summed)
    else:
        coupled = jnp.dot(previous, link.astype(jnp.float32), precision=highest)
    current = -(summed + coupled)
    own = own_rows.astype(jnp.float32)
    inner = jnp.dot(own, current, precision=highest) - jnp.dot(coupled.T, own.T, precision=highest)
    width = summed.shape[1]
    diag_cols = diag_part.shape[1]
    embedded = lax.dynamic_update_slice(
        jnp.zeros((width, width), jnp.float32), diag_part, (0, column * diag_cols)
    )
    return (current, row_first * embedded - inner / rows_total)


def chain_diag(total, chain_prev, link):
    if link is None:
        return total
    link_wide = link.astype(jnp.float32)
    return total + jnp.dot(
        link_wide.T, jnp.dot(chain_prev, link_wide, precision=highest), precision=highest
    )


def grid_plan(inverse_block, factor_cols, occupancy, row_block, coupling, diag_inverse):
    column = lax.axis_index("col")
    row_first = (lax.axis_index("row") == 0).astype(jnp.float32)
    row_parts = lax.axis_size("row")
    col_parts = lax.axis_size("col")
    local_rows = inverse_block.shape[0]
    rows_total = local_rows * row_parts
    supers, span, width_part = factor_cols.shape
    width = width_part * row_parts
    tile = local_rows // col_parts
    nblocks = occupancy.shape[1]
    diag_cols = diag_inverse.shape[2]
    flat = factor_cols.reshape(supers, span * width_part)
    column_list = []
    partial_list = []
    previous = None
    gathered = lax.all_gather(flat, "col", axis=1, tiled=True)
    placed = routed(gathered, occupancy, row_block, nblocks)
    column_part, outgoing = split_rows(placed, column, row_parts, col_parts, tile)
    column_full = lax.all_gather(column_part, "row", axis=1, tiled=True)
    arrived = lax.all_to_all(outgoing, "row", split_axis=1, concat_axis=1, tiled=True)
    own_all = arrived.reshape(supers, width, tile)
    summed = lax.psum_scatter(
        make_term(inverse_block, column_full), "col", scatter_dimension=0, tiled=True
    )
    for position in range(supers):
        link = None if position == 0 else coupling[position - 1]
        current, partial_value = local_step(
            summed[:, position, :],
            own_all[position],
            previous,
            link,
            diag_inverse[position],
            column,
            row_first,
            rows_total,
        )
        column_list.append(current)
        partial_list.append(partial_value)
        previous = current
    diag_list = []
    totals = lax.psum(jnp.stack(partial_list), ("row", "col"))
    chain_prev = None
    for position in range(supers):
        link = None if position == 0 else coupling[position - 1]
        diag_now = chain_diag(totals[position], chain_prev, link)
        diag_list.append(lax.dynamic_slice_in_dim(diag_now, column * diag_cols, diag_cols, 1))
        chain_prev = diag_now
    diagonals = jnp.stack(diag_list)
    return (jnp.stack(column_list), diagonals)


def swap(value, axis, bit, parts):
    return lax.ppermute(value, axis, [(i, i ^ bit) for i in range(parts)])


def split2(value):
    high = value.astype(bf16)
    return high, (value - high.astype(f32)).astype(bf16)


def nn(a, b):
    return lax.dot_general(a, b, (((1,), (0,)), ((), ())), preferred_element_type=f32)


def nt(a, b):
    return lax.dot_general(a, b, (((1,), (1,)), ((), ())), preferred_element_type=f32)


def nn2(pair, b):
    return nn(pair[0], b) + nn(pair[1], b)


def nn2r(a, pair):
    return nn(a, pair[0]) + nn(a, pair[1])


def local_kernel(outer, dims, *refs):
    supers, width, rows, span, part, chunk = dims
    n = 2 * outer
    occ_ref, block_ref = refs[:2]
    held = refs[2 : 2 + n]
    link_ref, diag_ref, diag_other_ref = refs[2 + n : 5 + n]
    col_out, diag_out = refs[5 + n : 7 + n]
    (f_all, z_all, pt, c0h, c0l, c1h, c1l, p1h, p1l, c2h, c2l, tmp, f_sem, z_sem) = refs[7 + n :]
    row = lax.axis_index("row")
    col = lax.axis_index("col")
    f_rows = supers * part
    local_rows = held[0].shape[1] - f_rows
    half_w = width // 2
    f_copies, z_copies = [], []
    for side in range(2):
        target = col if side == 0 else 1 - col
        for k in range(outer):
            plane = (row // 4) ^ k
            for j in range(4):
                source = held[side * outer + k].at[j]
                owner = plane * 4 + j
                f_copies.append(pltpu.make_async_copy(source.at[pl.ds(0, f_rows)], f_all.at[target, owner], f_sem))
                z_copies.append(
                    pltpu.make_async_copy(
                        source.at[pl.ds(f_rows, local_rows)],
                        z_all.at[
                            pl.ds(pl.multiple_of(owner * local_rows, local_rows), local_rows),
                            pl.ds(pl.multiple_of(target * span, span), span),
                        ],
                        z_sem,
                    )
                )
    for copy in f_copies + z_copies:
        copy.start()
    for copy in f_copies:
        copy.wait()
    per_side = span // 128
    for s in range(supers):
        for b in range(2 * per_side):
            lane = (b % per_side) * 128
            blk = f_all[b // per_side, :, s * part : (s + 1) * part, lane : lane + 128].reshape(width, 128)
            keep = jnp.where(occ_ref[s, b] > 0, blk, jnp.zeros_like(blk))
            pt[s, :, pl.ds(pl.multiple_of(block_ref[s, b] * 128, 128), 128)] = keep
    for copy in z_copies:
        copy.wait()
    c_rows = pl.ds(pl.multiple_of(col * half_w, half_w), half_w)

    def step(m, carry):
        at = pl.ds(pl.multiple_of(m * chunk, chunk), chunk)
        zm = z_all[at, :]
        cols0 = split2(-nt(zm, pt[0]))
        c0h[at, :], c0l[at, :] = cols0
        tmp[...] = nn2(cols0, link_ref[0])
        p1h[at, :], p1l[at, :] = split2(tmp[...])
        tmp[...] += nt(zm, pt[1])
        cols1 = split2(-tmp[...])
        c1h[at, :], c1l[at, :] = cols1
        cols2 = -(nt(zm, pt[2, c_rows, :]) + nn2(cols1, link_ref[1, :, c_rows]))
        c2h[at, :], c2l[at, :] = split2(cols2)
        return carry

    lax.fori_loop(0, rows // chunk, step, 0)

    own = pl.ds(pl.multiple_of(row * local_rows, local_rows), local_rows)
    tile = local_rows // 2
    o1 = (c1h[own, :], c1l[own, :])
    mine = [
        c0h[own, :].astype(f32) + c0l[own, :].astype(f32),
        o1[0].astype(f32) + o1[1].astype(f32),
        -(nt(z_all[own, :], pt[2]) + nn2(o1, link_ref[1])),
    ]
    for s in range(supers):
        col_out[s] = jnp.where(col == 0, mine[s][:tile], mine[s][tile:])

    scale = 1.0 / rows
    whole = lambda s: (
        jnp.where(col == 0, diag_ref[s], diag_other_ref[s]),
        jnp.where(col == 0, diag_other_ref[s], diag_ref[s]),
    )
    d0 = jnp.concatenate(whole(0), axis=1) - nn2r(pt[0], (c0h[...], c0l[...])) * scale
    u1 = nn2r(pt[1], (p1h[...], p1l[...]))
    i1 = nn2r(pt[1], (c1h[...], c1l[...])) - u1.T
    d1 = jnp.concatenate(whole(1), axis=1) - i1 * scale + nn2r(link_ref[0].T, split2(nn2(split2(d0), link_ref[0])))
    n2 = nn2r(pt[2, c_rows, :], (c1h[...], c1l[...]))
    i2 = nn2r(pt[2], (c2h[...], c2l[...])) - nn2(split2(n2), link_ref[1]).T
    d2 = diag_ref[2] - i2 * scale + nn2r(link_ref[1].T, split2(nn2(split2(d1), link_ref[1, :, c_rows])))
    diag_out[0] = jnp.where(col == 0, d0[:, :half_w], d0[:, half_w:])
    diag_out[1] = jnp.where(col == 0, d1[:, :half_w], d1[:, half_w:])
    diag_out[2] = d2


def replicated_plan(inverse_block, factor_cols, occupancy, row_block, coupling, diag_inverse):
    row_parts = lax.axis_size("row")
    supers, span, part = factor_cols.shape
    width = part * row_parts
    local_rows = inverse_block.shape[0]
    rows = local_rows * row_parts
    own = jnp.concatenate(
        [jnp.transpose(factor_cols, (0, 2, 1)).reshape(supers * part, span), inverse_block], axis=0
    )
    planes = [[r for r in range(row_parts) if r // 4 == z] for z in range(row_parts // 4)]
    over_plane = lambda value: lax.all_gather(value, "row", axis_index_groups=planes)
    across = lambda value: lax.ppermute(value, "col", [(0, 1), (1, 0)])
    line = [own] + [swap(own, "row", 4 * k, row_parts) for k in range(1, row_parts // 4)]
    mine = [over_plane(value) for value in line]
    other = [across(value) for value in mine]
    diag_other = across(diag_inverse)
    values = mine + other
    chunk = rows // 2
    any_spec = pl.BlockSpec(memory_space=pl.ANY)
    smem = pl.BlockSpec(memory_space=pltpu.SMEM)
    vmem = pl.BlockSpec(memory_space=pltpu.VMEM)
    wide = lambda cols: pltpu.VMEM((rows, cols), bf16)
    return pl.pallas_call(
        functools.partial(local_kernel, len(mine), (supers, width, rows, span, part, chunk)),
        out_shape=(
            jax.ShapeDtypeStruct((supers, local_rows // 2, width), f32),
            jax.ShapeDtypeStruct((supers, width, width // 2), f32),
        ),
        in_specs=[smem] * 2 + [any_spec] * len(values) + [vmem] * 3,
        out_specs=(vmem, vmem),
        scratch_shapes=[
            pltpu.VMEM((2, row_parts, supers * part, span), bf16),
            pltpu.VMEM((rows, 2 * span), bf16),
            pltpu.VMEM((supers, width, rows), bf16),
            wide(width), wide(width), wide(width), wide(width), wide(width), wide(width),
            wide(width // 2), wide(width // 2),
            pltpu.VMEM((chunk, width), f32),
            pltpu.SemaphoreType.DMA,
            pltpu.SemaphoreType.DMA,
        ],
        compiler_params=pltpu.CompilerParams(vmem_limit_bytes=40 * 2**20),
        name="selected_inverse",
    )(
        occupancy, row_block,
        *values,
        coupling, diag_inverse, diag_other,
    )


def solution(mesh):
    row_parts, col_parts = mesh.shape["row"], mesh.shape["col"]
    in_specs = (P("row", "col"), P(None, "col", "row"), P(), P(), P(), P(None, None, "col"))
    out_specs = (P(None, ("row", "col"), None), P(None, None, "col"))

    def per_device(inverse_block, factor_cols, *rest):
        held = (inverse_block.size + factor_cols.size) * 2 * row_parts * col_parts
        fits = held <= REPLICATE_BYTES and col_parts == 2 and row_parts in (8, 16)
        plan = replicated_plan if fits else grid_plan
        return plan(inverse_block, factor_cols, *rest)

    return jax.shard_map(
        per_device, mesh=mesh, in_specs=in_specs, out_specs=out_specs, check_vma=False
    )
```

```python
import functools

import jax
import jax.numpy as jnp
from jax import lax
from jax.experimental import pallas as pl
from jax.experimental.pallas import tpu as pltpu
from jax.sharding import PartitionSpec as P

highest = lax.Precision.HIGHEST
f32 = jnp.float32
bf16 = jnp.bfloat16

REPLICATE_BYTES = 12 * 2**20


def routed(gathered, occupancy, row_block, nblocks):
    count = gathered.shape[0]
    width_part = gathered.shape[1] // (nblocks * 128)
    blocks = gathered.reshape(count, nblocks, 128, width_part)
    levels = lax.broadcasted_iota(jnp.int32, (count, nblocks, nblocks), 1)
    picks = ((row_block[:, None, :] == levels) & (occupancy[:, None, :] > 0)).astype(jnp.bfloat16)
    placed = jnp.einsum("kqb,kbtx->kxqt", picks, blocks, preferred_element_type=jnp.float32)
    return placed.astype(jnp.bfloat16).reshape(count, width_part, nblocks * 128)


def split_rows(placed, column, row_parts, col_parts, tile):
    count, width_part, total = placed.shape
    span = total // col_parts
    column_part = lax.dynamic_slice_in_dim(placed, column * span, span, 2)
    grid = placed.reshape(count, width_part, row_parts, col_parts, tile)
    mine = lax.dynamic_index_in_dim(grid, column, 3, keepdims=False)
    return (column_part, jnp.transpose(mine, (0, 2, 1, 3)))


def make_term(inverse_block, column_full):
    return lax.dot_general(
        inverse_block, column_full, (((1,), (2,)), ((), ())), preferred_element_type=jnp.float32
    )


def local_step(summed, own_rows, previous, link, diag_part, column, row_first, rows_total):
    if link is None:
        coupled = jnp.zeros_like(summed)
    else:
        coupled = jnp.dot(previous, link.astype(jnp.float32), precision=highest)
    current = -(summed + coupled)
    own = own_rows.astype(jnp.float32)
    inner = jnp.dot(own, current, precision=highest) - jnp.dot(coupled.T, own.T, precision=highest)
    width = summed.shape[1]
    diag_cols = diag_part.shape[1]
    embedded = lax.dynamic_update_slice(
        jnp.zeros((width, width), jnp.float32), diag_part, (0, column * diag_cols)
    )
    return (current, row_first * embedded - inner / rows_total)


def chain_diag(total, chain_prev, link):
    if link is None:
        return total
    link_wide = link.astype(jnp.float32)
    return total + jnp.dot(
        link_wide.T, jnp.dot(chain_prev, link_wide, precision=highest), precision=highest
    )


def grid_plan(inverse_block, factor_cols, occupancy, row_block, coupling, diag_inverse):
    column = lax.axis_index("col")
    row_first = (lax.axis_index("row") == 0).astype(jnp.float32)
    row_parts = lax.axis_size("row")
    col_parts = lax.axis_size("col")
    local_rows = inverse_block.shape[0]
    rows_total = local_rows * row_parts
    supers, span, width_part = factor_cols.shape
    width = width_part * row_parts
    tile = local_rows // col_parts
    nblocks = occupancy.shape[1]
    diag_cols = diag_inverse.shape[2]
    flat = factor_cols.reshape(supers, span * width_part)
    column_list = []
    partial_list = []
    previous = None
    gathered = lax.all_gather(flat, "col", axis=1, tiled=True)
    placed = routed(gathered, occupancy, row_block, nblocks)
    column_part, outgoing = split_rows(placed, column, row_parts, col_parts, tile)
    column_full = lax.all_gather(column_part, "row", axis=1, tiled=True)
    arrived = lax.all_to_all(outgoing, "row", split_axis=1, concat_axis=1, tiled=True)
    own_all = arrived.reshape(supers, width, tile)
    summed = lax.psum_scatter(
        make_term(inverse_block, column_full), "col", scatter_dimension=0, tiled=True
    )
    for position in range(supers):
        link = None if position == 0 else coupling[position - 1]
        current, partial_value = local_step(
            summed[:, position, :],
            own_all[position],
            previous,
            link,
            diag_inverse[position],
            column,
            row_first,
            rows_total,
        )
        column_list.append(current)
        partial_list.append(partial_value)
        previous = current
    diag_list = []
    totals = lax.psum(jnp.stack(partial_list), ("row", "col"))
    chain_prev = None
    for position in range(supers):
        link = None if position == 0 else coupling[position - 1]
        diag_now = chain_diag(totals[position], chain_prev, link)
        diag_list.append(lax.dynamic_slice_in_dim(diag_now, column * diag_cols, diag_cols, 1))
        chain_prev = diag_now
    diagonals = jnp.stack(diag_list)
    return (jnp.stack(column_list), diagonals)


def swap(value, axis, bit, parts):
    return lax.ppermute(value, axis, [(i, i ^ bit) for i in range(parts)])


def over_line(own, row_parts):
    lines = [[r for r in range(row_parts) if r % 4 == place] for place in range(4)]
    return lax.all_gather(own, "row", axis_index_groups=lines)


def far_place(over_x, over_y, row_parts):
    half = over_x.shape[0] // 2
    return swap(over_y[:half], "row", 1, row_parts), swap(over_x[half:], "row", 2, row_parts)


def split2(value):
    high = value.astype(bf16)
    return high, (value - high.astype(f32)).astype(bf16)


def nn(a, b):
    return lax.dot_general(a, b, (((1,), (0,)), ((), ())), preferred_element_type=f32)


def nt(a, b):
    return lax.dot_general(a, b, (((1,), (1,)), ((), ())), preferred_element_type=f32)


def nn2(pair, b):
    return nn(pair[0], b) + nn(pair[1], b)


def nn2r(a, pair):
    return nn(a, pair[0]) + nn(a, pair[1])


def local_kernel(groups, dims, *refs):
    supers, width, rows, span, part, chunk = dims
    n = len(groups)
    occ_ref, block_ref = refs[:2]
    f_refs = refs[2 : 2 + 2 * n]
    z_refs = refs[2 + 2 * n : 2 + 4 * n]
    link_ref, diag_ref, diag_other_ref = refs[2 + 4 * n : 5 + 4 * n]
    col_out, diag_out = refs[5 + 4 * n : 7 + 4 * n]
    (f_all, z_all, pt, c0h, c0l, c1h, c1l, p1h, p1l, c2h, c2l, tmp, f_sem, z_sem) = refs[7 + 4 * n :]
    row = lax.axis_index("row")
    col = lax.axis_index("col")
    local_rows = z_refs[0].shape[1]
    half_w = width // 2
    f_copies, z_copies = [], []
    for side in range(2):
        target = col if side == 0 else 1 - col
        for g, (plane, first, count) in enumerate(groups):
            for k in range(count):
                owner = 4 * (first + k) + ((row % 4) ^ plane)
                f_copies.append(pltpu.make_async_copy(f_refs[side * n + g].at[k], f_all.at[target, owner], f_sem))
                z_copies.append(
                    pltpu.make_async_copy(
                        z_refs[side * n + g].at[k],
                        z_all.at[
                            pl.ds(pl.multiple_of(owner * local_rows, local_rows), local_rows),
                            pl.ds(pl.multiple_of(target * span, span), span),
                        ],
                        z_sem,
                    )
                )
    for copy in f_copies + z_copies:
        copy.start()
    for copy in f_copies:
        copy.wait()
    per_side = span // 128
    for s in range(supers):
        for b in range(2 * per_side):
            lane = (b % per_side) * 128
            blk = f_all[b // per_side, :, s * part : (s + 1) * part, lane : lane + 128].reshape(width, 128)
            keep = jnp.where(occ_ref[s, b] > 0, blk, jnp.zeros_like(blk))
            pt[s, :, pl.ds(pl.multiple_of(block_ref[s, b] * 128, 128), 128)] = keep
    for copy in z_copies:
        copy.wait()
    c_rows = pl.ds(pl.multiple_of(col * half_w, half_w), half_w)

    def step(m, carry):
        at = pl.ds(pl.multiple_of(m * chunk, chunk), chunk)
        zm = z_all[at, :]
        cols0 = split2(-nt(zm, pt[0]))
        c0h[at, :], c0l[at, :] = cols0
        tmp[...] = nn2(cols0, link_ref[0])
        p1h[at, :], p1l[at, :] = split2(tmp[...])
        tmp[...] += nt(zm, pt[1])
        cols1 = split2(-tmp[...])
        c1h[at, :], c1l[at, :] = cols1
        cols2 = -(nt(zm, pt[2, c_rows, :]) + nn2(cols1, link_ref[1, :, c_rows]))
        c2h[at, :], c2l[at, :] = split2(cols2)
        return carry

    lax.fori_loop(0, rows // chunk, step, 0)

    own = pl.ds(pl.multiple_of(row * local_rows, local_rows), local_rows)
    tile = local_rows // 2
    o1 = (c1h[own, :], c1l[own, :])
    mine = [
        c0h[own, :].astype(f32) + c0l[own, :].astype(f32),
        o1[0].astype(f32) + o1[1].astype(f32),
        -(nt(z_all[own, :], pt[2]) + nn2(o1, link_ref[1])),
    ]
    for s in range(supers):
        col_out[s] = jnp.where(col == 0, mine[s][:tile], mine[s][tile:])

    scale = 1.0 / rows
    whole = lambda s: (
        jnp.where(col == 0, diag_ref[s], diag_other_ref[s]),
        jnp.where(col == 0, diag_other_ref[s], diag_ref[s]),
    )
    d0 = jnp.concatenate(whole(0), axis=1) - nn2r(pt[0], (c0h[...], c0l[...])) * scale
    u1 = nn2r(pt[1], (p1h[...], p1l[...]))
    i1 = nn2r(pt[1], (c1h[...], c1l[...])) - u1.T
    d1 = jnp.concatenate(whole(1), axis=1) - i1 * scale + nn2r(link_ref[0].T, split2(nn2(split2(d0), link_ref[0])))
    n2 = nn2r(pt[2, c_rows, :], (c1h[...], c1l[...]))
    i2 = nn2r(pt[2], (c2h[...], c2l[...])) - nn2(split2(n2), link_ref[1]).T
    d2 = diag_ref[2] - i2 * scale + nn2r(link_ref[1].T, split2(nn2(split2(d1), link_ref[1, :, c_rows])))
    diag_out[0] = jnp.where(col == 0, d0[:, :half_w], d0[:, half_w:])
    diag_out[1] = jnp.where(col == 0, d1[:, :half_w], d1[:, half_w:])
    diag_out[2] = d2


def replicated_plan(inverse_block, factor_cols, occupancy, row_block, coupling, diag_inverse):
    row_parts = lax.axis_size("row")
    supers, span, part = factor_cols.shape
    width = part * row_parts
    local_rows = inverse_block.shape[0]
    rows = local_rows * row_parts
    f_own = jnp.transpose(factor_cols, (0, 2, 1)).reshape(supers * part, span)
    f_line = over_line(f_own, row_parts)
    f_line, z_own = lax.optimization_barrier((f_line, inverse_block))
    f_x, f_y = swap(f_line, "row", 1, row_parts), swap(f_line, "row", 2, row_parts)
    z_line = over_line(z_own, row_parts)
    f_far = far_place(f_x, f_y, row_parts)
    z_line, f_x, f_y = lax.optimization_barrier((z_line, f_x, f_y))
    z_x, z_y = swap(z_line, "row", 1, row_parts), swap(z_line, "row", 2, row_parts)
    z_far = far_place(z_x, z_y, row_parts)
    across = lambda value: lax.ppermute(value, "col", [(0, 1), (1, 0)])
    diag_other = across(diag_inverse)
    f_values = [f_line, f_x, f_y, *f_far]
    z_values = [z_line, z_x, z_y, *z_far]
    f_values = f_values + [across(value) for value in f_values]
    z_values = z_values + [across(value) for value in z_values]
    outer = row_parts // 4
    groups = ((0, 0, outer), (1, 0, outer), (2, 0, outer), (3, 0, outer // 2), (3, outer // 2, outer // 2))
    chunk = rows // 2
    any_spec = pl.BlockSpec(memory_space=pl.ANY)
    smem = pl.BlockSpec(memory_space=pltpu.SMEM)
    vmem = pl.BlockSpec(memory_space=pltpu.VMEM)
    wide = lambda cols: pltpu.VMEM((rows, cols), bf16)
    return pl.pallas_call(
        functools.partial(local_kernel, groups, (supers, width, rows, span, part, chunk)),
        out_shape=(
            jax.ShapeDtypeStruct((supers, local_rows // 2, width), f32),
            jax.ShapeDtypeStruct((supers, width, width // 2), f32),
        ),
        in_specs=[smem] * 2 + [any_spec] * (4 * len(groups)) + [vmem] * 3,
        out_specs=(vmem, vmem),
        scratch_shapes=[
            pltpu.VMEM((2, row_parts, supers * part, span), bf16),
            pltpu.VMEM((rows, 2 * span), bf16),
            pltpu.VMEM((supers, width, rows), bf16),
            wide(width), wide(width), wide(width), wide(width), wide(width), wide(width),
            wide(width // 2), wide(width // 2),
            pltpu.VMEM((chunk, width), f32),
            pltpu.SemaphoreType.DMA,
            pltpu.SemaphoreType.DMA,
        ],
        compiler_params=pltpu.CompilerParams(vmem_limit_bytes=40 * 2**20),
        name="selected_inverse",
    )(
        occupancy, row_block,
        *f_values, *z_values,
        coupling, diag_inverse, diag_other,
    )


def solution(mesh):
    row_parts, col_parts = mesh.shape["row"], mesh.shape["col"]
    in_specs = (P("row", "col"), P(None, "col", "row"), P(), P(), P(), P(None, None, "col"))
    out_specs = (P(None, ("row", "col"), None), P(None, None, "col"))

    def per_device(inverse_block, factor_cols, *rest):
        held = (inverse_block.size + factor_cols.size) * 2 * row_parts * col_parts
        fits = held <= REPLICATE_BYTES and col_parts == 2 and row_parts in (8, 16)
        plan = replicated_plan if fits else grid_plan
        return plan(inverse_block, factor_cols, *rest)

    return jax.shard_map(
        per_device, mesh=mesh, in_specs=in_specs, out_specs=out_specs, check_vma=False
    )
```

```python
import functools

import jax
import jax.numpy as jnp
from jax import lax
from jax.experimental import pallas as pl
from jax.experimental.pallas import tpu as pltpu
from jax.sharding import PartitionSpec as P

highest = lax.Precision.HIGHEST
f32 = jnp.float32
bf16 = jnp.bfloat16

REPLICATE_BYTES = 12 * 2**20


def routed(gathered, occupancy, row_block, nblocks):
    count = gathered.shape[0]
    width_part = gathered.shape[1] // (nblocks * 128)
    blocks = gathered.reshape(count, nblocks, 128, width_part)
    levels = lax.broadcasted_iota(jnp.int32, (count, nblocks, nblocks), 1)
    picks = ((row_block[:, None, :] == levels) & (occupancy[:, None, :] > 0)).astype(jnp.bfloat16)
    placed = jnp.einsum("kqb,kbtx->kxqt", picks, blocks, preferred_element_type=jnp.float32)
    return placed.astype(jnp.bfloat16).reshape(count, width_part, nblocks * 128)


def split_rows(placed, column, row_parts, col_parts, tile):
    count, width_part, total = placed.shape
    span = total // col_parts
    column_part = lax.dynamic_slice_in_dim(placed, column * span, span, 2)
    grid = placed.reshape(count, width_part, row_parts, col_parts, tile)
    mine = lax.dynamic_index_in_dim(grid, column, 3, keepdims=False)
    return (column_part, jnp.transpose(mine, (0, 2, 1, 3)))


def make_term(inverse_block, column_full):
    return lax.dot_general(
        inverse_block, column_full, (((1,), (2,)), ((), ())), preferred_element_type=jnp.float32
    )


def local_step(summed, own_rows, previous, link, diag_part, column, row_first, rows_total):
    if link is None:
        coupled = jnp.zeros_like(summed)
    else:
        coupled = jnp.dot(previous, link.astype(jnp.float32), precision=highest)
    current = -(summed + coupled)
    own = own_rows.astype(jnp.float32)
    inner = jnp.dot(own, current, precision=highest) - jnp.dot(coupled.T, own.T, precision=highest)
    width = summed.shape[1]
    diag_cols = diag_part.shape[1]
    embedded = lax.dynamic_update_slice(
        jnp.zeros((width, width), jnp.float32), diag_part, (0, column * diag_cols)
    )
    return (current, row_first * embedded - inner / rows_total)


def chain_diag(total, chain_prev, link):
    if link is None:
        return total
    link_wide = link.astype(jnp.float32)
    return total + jnp.dot(
        link_wide.T, jnp.dot(chain_prev, link_wide, precision=highest), precision=highest
    )


def grid_plan(inverse_block, factor_cols, occupancy, row_block, coupling, diag_inverse):
    column = lax.axis_index("col")
    row_first = (lax.axis_index("row") == 0).astype(jnp.float32)
    row_parts = lax.axis_size("row")
    col_parts = lax.axis_size("col")
    local_rows = inverse_block.shape[0]
    rows_total = local_rows * row_parts
    supers, span, width_part = factor_cols.shape
    width = width_part * row_parts
    tile = local_rows // col_parts
    nblocks = occupancy.shape[1]
    diag_cols = diag_inverse.shape[2]
    flat = factor_cols.reshape(supers, span * width_part)
    column_list = []
    partial_list = []
    previous = None
    gathered = lax.all_gather(flat, "col", axis=1, tiled=True)
    placed = routed(gathered, occupancy, row_block, nblocks)
    column_part, outgoing = split_rows(placed, column, row_parts, col_parts, tile)
    column_full = lax.all_gather(column_part, "row", axis=1, tiled=True)
    arrived = lax.all_to_all(outgoing, "row", split_axis=1, concat_axis=1, tiled=True)
    own_all = arrived.reshape(supers, width, tile)
    summed = lax.psum_scatter(
        make_term(inverse_block, column_full), "col", scatter_dimension=0, tiled=True
    )
    for position in range(supers):
        link = None if position == 0 else coupling[position - 1]
        current, partial_value = local_step(
            summed[:, position, :],
            own_all[position],
            previous,
            link,
            diag_inverse[position],
            column,
            row_first,
            rows_total,
        )
        column_list.append(current)
        partial_list.append(partial_value)
        previous = current
    diag_list = []
    totals = lax.psum(jnp.stack(partial_list), ("row", "col"))
    chain_prev = None
    for position in range(supers):
        link = None if position == 0 else coupling[position - 1]
        diag_now = chain_diag(totals[position], chain_prev, link)
        diag_list.append(lax.dynamic_slice_in_dim(diag_now, column * diag_cols, diag_cols, 1))
        chain_prev = diag_now
    diagonals = jnp.stack(diag_list)
    return (jnp.stack(column_list), diagonals)


def swap(value, axis, bit, parts):
    return lax.ppermute(value, axis, [(i, i ^ bit) for i in range(parts)])


def across(value):
    return lax.ppermute(value, "col", [(0, 1), (1, 0)])


def spread(own, row_parts):
    outer = row_parts // 4
    x, y = (lambda value: swap(value, "row", 1, row_parts)), (lambda value: swap(value, "row", 2, row_parts))
    line = [swap(own, "row", 4 * k, row_parts) for k in range(1, outer)]
    planes, others = [], []
    waves = [[own], [line[0]], line[1:]]
    after = ()
    for number, wave in enumerate(waves):
        if after:
            wave, after = lax.optimization_barrier((wave, after))
            planes[-1][1:3] = after
        both = jnp.stack(wave) if len(wave) > 1 else wave[0][None]
        over_x, over_y = x(both), y(both)
        after = [over_x, over_y]
        for i in range(len(wave)):
            far = x(over_y[i]) if (number + i) % 2 == 0 else y(over_x[i])
            planes.append([wave[i], over_x[i], over_y[i], far])
        if len(wave) == 1:
            planes[-1][1:3] = [over_x, over_y]
    for plane in planes:
        plane[1:3] = [v[0] if v.ndim > own.ndim else v for v in plane[1:3]]
        mine = jnp.stack(plane)
        others.append(across(mine))
        plane[:] = [mine]
    return [plane[0] for plane in planes], others


def split2(value):
    high = value.astype(bf16)
    return high, (value - high.astype(f32)).astype(bf16)


def nn(a, b):
    return lax.dot_general(a, b, (((1,), (0,)), ((), ())), preferred_element_type=f32)


def nt(a, b):
    return lax.dot_general(a, b, (((1,), (1,)), ((), ())), preferred_element_type=f32)


def nn2(pair, b):
    return nn(pair[0], b) + nn(pair[1], b)


def nn2r(a, pair):
    return nn(a, pair[0]) + nn(a, pair[1])


def local_kernel(outer, dims, *refs):
    supers, width, rows, span, part, chunk = dims
    n = 2 * outer
    occ_ref, block_ref = refs[:2]
    held = refs[2 : 2 + n]
    link_ref, diag_ref, diag_other_ref = refs[2 + n : 5 + n]
    col_out, diag_out = refs[5 + n : 7 + n]
    (f_all, z_all, pt, c0h, c0l, c1h, c1l, p1h, p1l, c2h, c2l, tmp, f_sem, z_sem) = refs[7 + n :]
    row = lax.axis_index("row")
    col = lax.axis_index("col")
    f_rows = supers * part
    local_rows = held[0].shape[1] - f_rows
    half_w = width // 2
    f_copies, z_copies = [], []
    for side in range(2):
        target = col if side == 0 else 1 - col
        for k in range(outer):
            plane = (row // 4) ^ k
            for j in range(4):
                source = held[side * outer + k].at[j]
                owner = plane * 4 + ((row % 4) ^ j)
                f_copies.append(pltpu.make_async_copy(source.at[pl.ds(0, f_rows)], f_all.at[target, owner], f_sem))
                z_copies.append(
                    pltpu.make_async_copy(
                        source.at[pl.ds(f_rows, local_rows)],
                        z_all.at[
                            pl.ds(pl.multiple_of(owner * local_rows, local_rows), local_rows),
                            pl.ds(pl.multiple_of(target * span, span), span),
                        ],
                        z_sem,
                    )
                )
    for copy in f_copies + z_copies:
        copy.start()
    for copy in f_copies:
        copy.wait()
    per_side = span // 128
    for s in range(supers):
        for b in range(2 * per_side):
            lane = (b % per_side) * 128
            blk = f_all[b // per_side, :, s * part : (s + 1) * part, lane : lane + 128].reshape(width, 128)
            keep = jnp.where(occ_ref[s, b] > 0, blk, jnp.zeros_like(blk))
            pt[s, :, pl.ds(pl.multiple_of(block_ref[s, b] * 128, 128), 128)] = keep
    for copy in z_copies:
        copy.wait()
    c_rows = pl.ds(pl.multiple_of(col * half_w, half_w), half_w)

    def step(m, carry):
        at = pl.ds(pl.multiple_of(m * chunk, chunk), chunk)
        zm = z_all[at, :]
        cols0 = split2(-nt(zm, pt[0]))
        c0h[at, :], c0l[at, :] = cols0
        tmp[...] = nn2(cols0, link_ref[0])
        p1h[at, :], p1l[at, :] = split2(tmp[...])
        tmp[...] += nt(zm, pt[1])
        cols1 = split2(-tmp[...])
        c1h[at, :], c1l[at, :] = cols1
        cols2 = -(nt(zm, pt[2, c_rows, :]) + nn2(cols1, link_ref[1, :, c_rows]))
        c2h[at, :], c2l[at, :] = split2(cols2)
        return carry

    lax.fori_loop(0, rows // chunk, step, 0)

    own = pl.ds(pl.multiple_of(row * local_rows, local_rows), local_rows)
    tile = local_rows // 2
    o1 = (c1h[own, :], c1l[own, :])
    mine = [
        c0h[own, :].astype(f32) + c0l[own, :].astype(f32),
        o1[0].astype(f32) + o1[1].astype(f32),
        -(nt(z_all[own, :], pt[2]) + nn2(o1, link_ref[1])),
    ]
    for s in range(supers):
        col_out[s] = jnp.where(col == 0, mine[s][:tile], mine[s][tile:])

    scale = 1.0 / rows
    whole = lambda s: (
        jnp.where(col == 0, diag_ref[s], diag_other_ref[s]),
        jnp.where(col == 0, diag_other_ref[s], diag_ref[s]),
    )
    d0 = jnp.concatenate(whole(0), axis=1) - nn2r(pt[0], (c0h[...], c0l[...])) * scale
    u1 = nn2r(pt[1], (p1h[...], p1l[...]))
    i1 = nn2r(pt[1], (c1h[...], c1l[...])) - u1.T
    d1 = jnp.concatenate(whole(1), axis=1) - i1 * scale + nn2r(link_ref[0].T, split2(nn2(split2(d0), link_ref[0])))
    n2 = nn2r(pt[2, c_rows, :], (c1h[...], c1l[...]))
    i2 = nn2r(pt[2], (c2h[...], c2l[...])) - nn2(split2(n2), link_ref[1]).T
    d2 = diag_ref[2] - i2 * scale + nn2r(link_ref[1].T, split2(nn2(split2(d1), link_ref[1, :, c_rows])))
    diag_out[0] = jnp.where(col == 0, d0[:, :half_w], d0[:, half_w:])
    diag_out[1] = jnp.where(col == 0, d1[:, :half_w], d1[:, half_w:])
    diag_out[2] = d2


def replicated_plan(inverse_block, factor_cols, occupancy, row_block, coupling, diag_inverse):
    row_parts = lax.axis_size("row")
    supers, span, part = factor_cols.shape
    width = part * row_parts
    local_rows = inverse_block.shape[0]
    rows = local_rows * row_parts
    own = jnp.concatenate(
        [jnp.transpose(factor_cols, (0, 2, 1)).reshape(supers * part, span), inverse_block], axis=0
    )
    mine, other = spread(own, row_parts)
    diag_other = across(diag_inverse)
    values = mine + other
    chunk = rows // 2
    any_spec = pl.BlockSpec(memory_space=pl.ANY)
    smem = pl.BlockSpec(memory_space=pltpu.SMEM)
    vmem = pl.BlockSpec(memory_space=pltpu.VMEM)
    wide = lambda cols: pltpu.VMEM((rows, cols), bf16)
    return pl.pallas_call(
        functools.partial(local_kernel, len(mine), (supers, width, rows, span, part, chunk)),
        out_shape=(
            jax.ShapeDtypeStruct((supers, local_rows // 2, width), f32),
            jax.ShapeDtypeStruct((supers, width, width // 2), f32),
        ),
        in_specs=[smem] * 2 + [any_spec] * len(values) + [vmem] * 3,
        out_specs=(vmem, vmem),
        scratch_shapes=[
            pltpu.VMEM((2, row_parts, supers * part, span), bf16),
            pltpu.VMEM((rows, 2 * span), bf16),
            pltpu.VMEM((supers, width, rows), bf16),
            wide(width), wide(width), wide(width), wide(width), wide(width), wide(width),
            wide(width // 2), wide(width // 2),
            pltpu.VMEM((chunk, width), f32),
            pltpu.SemaphoreType.DMA,
            pltpu.SemaphoreType.DMA,
        ],
        compiler_params=pltpu.CompilerParams(vmem_limit_bytes=40 * 2**20),
        name="selected_inverse",
    )(
        occupancy, row_block,
        *values,
        coupling, diag_inverse, diag_other,
    )


def solution(mesh):
    row_parts, col_parts = mesh.shape["row"], mesh.shape["col"]
    in_specs = (P("row", "col"), P(None, "col", "row"), P(), P(), P(), P(None, None, "col"))
    out_specs = (P(None, ("row", "col"), None), P(None, None, "col"))

    def per_device(inverse_block, factor_cols, *rest):
        held = (inverse_block.size + factor_cols.size) * 2 * row_parts * col_parts
        fits = held <= REPLICATE_BYTES and col_parts == 2 and row_parts in (8, 16)
        plan = replicated_plan if fits else grid_plan
        return plan(inverse_block, factor_cols, *rest)

    return jax.shard_map(
        per_device, mesh=mesh, in_specs=in_specs, out_specs=out_specs, check_vma=False
    )
```

```python
import functools

import jax
import jax.numpy as jnp
from jax import lax
from jax.experimental import pallas as pl
from jax.experimental.pallas import tpu as pltpu
from jax.sharding import PartitionSpec as P

highest = lax.Precision.HIGHEST
f32 = jnp.float32
bf16 = jnp.bfloat16

REPLICATE_BYTES = 12 * 2**20
VMEM_LIMIT = 40 * 2**20


def routed(gathered, occupancy, row_block, nblocks):
    count = gathered.shape[0]
    width_part = gathered.shape[1] // (nblocks * 128)
    blocks = gathered.reshape(count, nblocks, 128, width_part)
    levels = lax.broadcasted_iota(jnp.int32, (count, nblocks, nblocks), 1)
    picks = ((row_block[:, None, :] == levels) & (occupancy[:, None, :] > 0)).astype(jnp.bfloat16)
    placed = jnp.einsum("kqb,kbtx->kxqt", picks, blocks, preferred_element_type=jnp.float32)
    return placed.astype(jnp.bfloat16).reshape(count, width_part, nblocks * 128)


def split_rows(placed, column, row_parts, col_parts, tile):
    count, width_part, total = placed.shape
    span = total // col_parts
    column_part = lax.dynamic_slice_in_dim(placed, column * span, span, 2)
    grid = placed.reshape(count, width_part, row_parts, col_parts, tile)
    mine = lax.dynamic_index_in_dim(grid, column, 3, keepdims=False)
    return (column_part, jnp.transpose(mine, (0, 2, 1, 3)))


def make_term(inverse_block, column_full):
    return lax.dot_general(
        inverse_block, column_full, (((1,), (2,)), ((), ())), preferred_element_type=jnp.float32
    )


def local_step(summed, own_rows, previous, link, diag_part, column, row_first, rows_total):
    if link is None:
        coupled = jnp.zeros_like(summed)
    else:
        coupled = jnp.dot(previous, link.astype(jnp.float32), precision=highest)
    current = -(summed + coupled)
    own = own_rows.astype(jnp.float32)
    inner = jnp.dot(own, current, precision=highest) - jnp.dot(coupled.T, own.T, precision=highest)
    width = summed.shape[1]
    diag_cols = diag_part.shape[1]
    embedded = lax.dynamic_update_slice(
        jnp.zeros((width, width), jnp.float32), diag_part, (0, column * diag_cols)
    )
    return (current, row_first * embedded - inner / rows_total)


def chain_diag(total, chain_prev, link):
    if link is None:
        return total
    link_wide = link.astype(jnp.float32)
    return total + jnp.dot(
        link_wide.T, jnp.dot(chain_prev, link_wide, precision=highest), precision=highest
    )


def grid_plan(inverse_block, factor_cols, occupancy, row_block, coupling, diag_inverse):
    column = lax.axis_index("col")
    row_first = (lax.axis_index("row") == 0).astype(jnp.float32)
    row_parts = lax.axis_size("row")
    col_parts = lax.axis_size("col")
    local_rows = inverse_block.shape[0]
    rows_total = local_rows * row_parts
    supers, span, width_part = factor_cols.shape
    width = width_part * row_parts
    tile = local_rows // col_parts
    nblocks = occupancy.shape[1]
    diag_cols = diag_inverse.shape[2]
    flat = factor_cols.reshape(supers, span * width_part)
    column_list = []
    partial_list = []
    previous = None
    gathered = lax.all_gather(flat, "col", axis=1, tiled=True)
    placed = routed(gathered, occupancy, row_block, nblocks)
    column_part, outgoing = split_rows(placed, column, row_parts, col_parts, tile)
    column_full = lax.all_gather(column_part, "row", axis=1, tiled=True)
    arrived = lax.all_to_all(outgoing, "row", split_axis=1, concat_axis=1, tiled=True)
    own_all = arrived.reshape(supers, width, tile)
    summed = lax.psum_scatter(
        make_term(inverse_block, column_full), "col", scatter_dimension=0, tiled=True
    )
    for position in range(supers):
        link = None if position == 0 else coupling[position - 1]
        current, partial_value = local_step(
            summed[:, position, :],
            own_all[position],
            previous,
            link,
            diag_inverse[position],
            column,
            row_first,
            rows_total,
        )
        column_list.append(current)
        partial_list.append(partial_value)
        previous = current
    diag_list = []
    totals = lax.psum(jnp.stack(partial_list), ("row", "col"))
    chain_prev = None
    for position in range(supers):
        link = None if position == 0 else coupling[position - 1]
        diag_now = chain_diag(totals[position], chain_prev, link)
        diag_list.append(lax.dynamic_slice_in_dim(diag_now, column * diag_cols, diag_cols, 1))
        chain_prev = diag_now
    diagonals = jnp.stack(diag_list)
    return (jnp.stack(column_list), diagonals)


def swap(value, axis, bit, parts):
    return lax.ppermute(value, axis, [(i, i ^ bit) for i in range(parts)])


def across(value):
    return lax.ppermute(value, "col", [(0, 1), (1, 0)])


def along_line(own, row_parts):
    return [own] + [swap(own, "row", 4 * k, row_parts) for k in range(1, row_parts // 4)]


def over_plane(own, row_parts):
    return swap(own, "row", 1, row_parts), swap(own, "row", 2, row_parts)


def after(values, *events):
    return lax.optimization_barrier((values, events))[0]


def split2(value):
    high = value.astype(bf16)
    return high, (value - high.astype(f32)).astype(bf16)


def nn(a, b):
    return lax.dot_general(a, b, (((1,), (0,)), ((), ())), preferred_element_type=f32)


def nt(a, b):
    return lax.dot_general(a, b, (((1,), (1,)), ((), ())), preferred_element_type=f32)


def nn2(pair, b):
    return nn(pair[0], b) + nn(pair[1], b)


def nn2r(a, pair):
    return nn(a, pair[0]) + nn(a, pair[1])


def owner_of(row, wave, count, j, i):
    return 4 * ((row // 4) ^ (wave * count + i)) + ((row % 4) ^ j)


def place_kernel(dims, *refs):
    supers, width, rows, span, part = dims
    occ_ref, block_ref = refs[:2]
    f_refs, z_ref, z_other_ref, link_ref = refs[2:6], refs[6], refs[7], refs[8]
    pt, col_out, f_all, sem = refs[9:]
    row, col = lax.axis_index("row"), lax.axis_index("col")
    copies = []
    for side in range(2):
        for wave in range(2):
            source = f_refs[2 * side + wave]
            for j in range(4):
                for i in range(source.shape[1]):
                    owner = owner_of(row, wave, source.shape[1], j, i)
                    target = col if side == 0 else 1 - col
                    copies.append(pltpu.make_async_copy(source.at[j, i], f_all.at[target, owner], sem))
    for copy in copies:
        copy.start()
    for copy in copies:
        copy.wait()
    per_side = span // 128
    for s in range(supers):
        for b in range(2 * per_side):
            lane = (b % per_side) * 128
            blk = f_all[b // per_side, :, s * part : (s + 1) * part, lane : lane + 128].reshape(width, 128)
            keep = jnp.where(occ_ref[s, b] > 0, blk, jnp.zeros_like(blk))
            pt[s, :, pl.ds(pl.multiple_of(block_ref[s, b] * 128, 128), 128)] = keep
    local_rows = z_ref.shape[0]
    tile = local_rows // 2
    mine, theirs = z_ref[...], z_other_ref[...]
    z_own = jnp.concatenate([jnp.where(col == 0, mine, theirs), jnp.where(col == 0, theirs, mine)], axis=1)
    previous = None
    for s in range(supers):
        current = -nt(z_own, pt[s])
        if s > 0:
            current = current - nn2(split2(previous), link_ref[s - 1])
        col_out[s] = jnp.where(col == 0, current[:tile], current[tile:])
        previous = current


def add_rows(wave, dims, col, row, pt, z_refs, link_ref, sums, scratch):
    width, span = dims
    z_all, c0h, c0l, c1h, c1l, p1h, p1l, c2h, c2l, tmp, sem = scratch
    half_rows = z_all.shape[0]
    half_w = width // 2
    copies = []
    for side in range(2):
        target = col if side == 0 else 1 - col
        source = z_refs[side]
        local_rows = source.shape[2]
        for j in range(4):
            for i in range(source.shape[1]):
                place = owner_of(row, wave, source.shape[1], j, i) % (half_rows // local_rows)
                copies.append(
                    pltpu.make_async_copy(
                        source.at[j, i],
                        z_all.at[
                            pl.ds(pl.multiple_of(place * local_rows, local_rows), local_rows),
                            pl.ds(pl.multiple_of(target * span, span), span),
                        ],
                        sem,
                    )
                )
    for copy in copies:
        copy.start()
    for copy in copies:
        copy.wait()
    c_rows = pl.ds(pl.multiple_of(col * half_w, half_w), half_w)
    half = owner_of(row, wave, z_refs[0].shape[1], 0, 0) // (half_rows // local_rows)
    lanes = pl.ds(pl.multiple_of(half * half_rows, half_rows), half_rows)
    zm = z_all[...]
    cols0 = split2(-nt(zm, pt[0]))
    c0h[...], c0l[...] = cols0
    tmp[...] = nn2(cols0, link_ref[0])
    p1h[...], p1l[...] = split2(tmp[...])
    tmp[...] += nt(zm, pt[1])
    cols1 = split2(-tmp[...])
    c1h[...], c1l[...] = cols1
    cols2 = -(nt(zm, pt[2, c_rows, :]) + nn2(cols1, link_ref[1, :, c_rows]))
    c2h[...], c2l[...] = split2(cols2)
    left = pt[1, :, lanes]
    terms = [
        nn2r(pt[0, :, lanes], (c0h[...], c0l[...])),
        nn2r(left, (p1h[...], p1l[...])),
        nn2r(left, (c1h[...], c1l[...])),
        nn2r(pt[2, c_rows, lanes], (c1h[...], c1l[...])),
        nn2r(pt[2, :, lanes], (c2h[...], c2l[...])),
    ]
    for total, term in zip(sums, terms):
        total[...] = term if wave == 0 else total[...] + term


def first_kernel(dims, *refs):
    pt, z_refs, link_ref = refs[0], refs[1:3], refs[3]
    add_rows(0, dims, lax.axis_index("col"), lax.axis_index("row"), pt, z_refs, link_ref, refs[4:9], refs[9:])


def last_kernel(dims, rows, *refs):
    pt, z_refs, link_ref, diag_ref, diag_other_ref = refs[0], refs[1:3], refs[3], refs[4], refs[5]
    before, diag_out, sums, scratch = refs[6:11], refs[11], refs[12:17], refs[17:]
    col = lax.axis_index("col")
    width, _ = dims
    half_w = width // 2
    for total, value in zip(sums, before):
        total[...] = value[...]
    add_rows(1, dims, col, lax.axis_index("row"), pt, z_refs, link_ref, sums, scratch)
    s0, u1, s1, n2, s2 = sums
    scale = 1.0 / rows
    c_rows = pl.ds(pl.multiple_of(col * half_w, half_w), half_w)

    def whole(s):
        mine, theirs = diag_ref[s], diag_other_ref[s]
        return jnp.concatenate([jnp.where(col == 0, mine, theirs), jnp.where(col == 0, theirs, mine)], axis=1)

    d0 = whole(0) - s0[...] * scale
    i1 = s1[...] - u1[...].T
    d1 = whole(1) - i1 * scale + nn2r(link_ref[0].T, split2(nn2(split2(d0), link_ref[0])))
    i2 = s2[...] - nn2(split2(n2[...]), link_ref[1]).T
    d2 = diag_ref[2] - i2 * scale + nn2r(link_ref[1].T, split2(nn2(split2(d1), link_ref[1, :, c_rows])))
    diag_out[0] = jnp.where(col == 0, d0[:, :half_w], d0[:, half_w:])
    diag_out[1] = jnp.where(col == 0, d1[:, :half_w], d1[:, half_w:])
    diag_out[2] = d2


def replicated_plan(inverse_block, factor_cols, occupancy, row_block, coupling, diag_inverse):
    row_parts = lax.axis_size("row")
    supers, span, part = factor_cols.shape
    width = part * row_parts
    local_rows = inverse_block.shape[0]
    rows = local_rows * row_parts
    count = row_parts // 8
    any_spec = pl.BlockSpec(memory_space=pl.ANY)
    smem = pl.BlockSpec(memory_space=pltpu.SMEM)
    vmem = pl.BlockSpec(memory_space=pltpu.VMEM)
    shape = jax.ShapeDtypeStruct

    def call(body, name, flops, **kwargs):
        return pl.pallas_call(
            body,
            compiler_params=pltpu.CompilerParams(vmem_limit_bytes=VMEM_LIMIT),
            cost_estimate=pl.CostEstimate(flops=flops, bytes_accessed=8 * 2**20, transcendentals=0),
            name=name,
            **kwargs,
        )

    f_own = jnp.transpose(factor_cols, (0, 2, 1)).reshape(supers * part, span)
    f_parts = along_line(f_own, row_parts)
    f_a, f_b = jnp.stack(f_parts[:count]), jnp.stack(f_parts[count:])
    f_ax, f_ay = over_plane(f_a, row_parts)
    f_bx, f_by = over_plane(f_b, row_parts)
    z_cross = across(inverse_block)
    z_parts = along_line(after(inverse_block, f_b), row_parts)
    z_a, z_b = jnp.stack(z_parts[:count]), jnp.stack(z_parts[count:])
    f_ay, f_bx = after((f_ay, f_bx), z_b)
    f_far_a, f_far_b = swap(f_ay, "row", 1, row_parts), swap(f_bx, "row", 2, row_parts)
    z_a = after(z_a, f_ay, f_bx)
    z_ax, z_ay = over_plane(z_a, row_parts)
    f_mine = [jnp.stack([f_a, f_ax, f_ay, f_far_a]), jnp.stack([f_b, f_bx, f_by, f_far_b])]
    f_all = f_mine + [across(v) for v in f_mine]
    z_b = after(z_b, z_ax, z_ay)
    z_bx, z_by = over_plane(z_b, row_parts)
    z_far_a = swap(z_ay, "row", 1, row_parts)
    z_first = jnp.stack([z_a, z_ax, z_ay, z_far_a])
    z_first_other = across(z_first)
    diag_other = across(diag_inverse)

    pt, columns = call(
        functools.partial(place_kernel, (supers, width, rows, span, part)),
        "place", 4 * 10**9,
        out_shape=(shape((supers, width, rows), bf16), shape((supers, local_rows // 2, width), f32)),
        in_specs=[smem] * 2 + [any_spec] * 4 + [vmem] * 3,
        out_specs=(vmem, vmem),
        scratch_shapes=[pltpu.VMEM((2, row_parts, supers * part, span), bf16), pltpu.SemaphoreType.DMA],
    )(occupancy, row_block, *f_all, inverse_block, z_cross, coupling)

    z_bx, pt = after((z_bx, pt), pt)
    z_far_b = swap(z_bx, "row", 2, row_parts)
    dims = (width, span)
    half_rows, half_w = rows // 2, width // 2
    sum_shapes = [(width, width), (width, width), (width, width), (half_w, width), (width, half_w)]
    scratch = (
        [pltpu.VMEM((half_rows, 2 * span), bf16)]
        + [pltpu.VMEM((half_rows, width), bf16)] * 6
        + [pltpu.VMEM((half_rows, half_w), bf16)] * 2
        + [pltpu.VMEM((half_rows, width), f32), pltpu.SemaphoreType.DMA]
    )
    sums = call(
        functools.partial(first_kernel, dims),
        "own_half", 12 * 10**9,
        out_shape=tuple(shape(v, f32) for v in sum_shapes),
        in_specs=[vmem] + [any_spec] * 2 + [vmem],
        out_specs=(vmem,) * 5,
        scratch_shapes=scratch,
    )(pt, z_first, z_first_other, coupling)
    z_far_b, *sums = after((z_far_b, *sums), sums[0])
    z_last = jnp.stack([z_b, z_bx, z_by, z_far_b])
    z_last_other = across(z_last)
    diagonals = call(
        functools.partial(last_kernel, dims, rows),
        "other_half", 15 * 10**9,
        out_shape=shape((supers, width, half_w), f32),
        in_specs=[vmem] + [any_spec] * 2 + [vmem] * 8,
        out_specs=vmem,
        scratch_shapes=[pltpu.VMEM(v, f32) for v in sum_shapes] + scratch,
    )(pt, z_last, z_last_other, coupling, diag_inverse, diag_other, *sums)
    return columns, diagonals


def solution(mesh):
    row_parts, col_parts = mesh.shape["row"], mesh.shape["col"]
    in_specs = (P("row", "col"), P(None, "col", "row"), P(), P(), P(), P(None, None, "col"))
    out_specs = (P(None, ("row", "col"), None), P(None, None, "col"))

    def per_device(inverse_block, factor_cols, *rest):
        held = (inverse_block.size + factor_cols.size) * 2 * row_parts * col_parts
        fits = held <= REPLICATE_BYTES and col_parts == 2 and row_parts in (8, 16)
        plan = replicated_plan if fits else grid_plan
        return plan(inverse_block, factor_cols, *rest)

    return jax.shard_map(
        per_device, mesh=mesh, in_specs=in_specs, out_specs=out_specs, check_vma=False
    )
```

```python
import functools

import jax
import jax.numpy as jnp
from jax import lax
from jax.experimental import pallas as pl
from jax.experimental.pallas import tpu as pltpu
from jax.sharding import PartitionSpec as P

highest = lax.Precision.HIGHEST
f32 = jnp.float32
bf16 = jnp.bfloat16

REPLICATE_BYTES = 12 * 2**20
VMEM_LIMIT = 40 * 2**20


def routed(gathered, occupancy, row_block, nblocks):
    count = gathered.shape[0]
    width_part = gathered.shape[1] // (nblocks * 128)
    blocks = gathered.reshape(count, nblocks, 128, width_part)
    levels = lax.broadcasted_iota(jnp.int32, (count, nblocks, nblocks), 1)
    picks = ((row_block[:, None, :] == levels) & (occupancy[:, None, :] > 0)).astype(jnp.bfloat16)
    placed = jnp.einsum("kqb,kbtx->kxqt", picks, blocks, preferred_element_type=jnp.float32)
    return placed.astype(jnp.bfloat16).reshape(count, width_part, nblocks * 128)


def split_rows(placed, column, row_parts, col_parts, tile):
    count, width_part, total = placed.shape
    span = total // col_parts
    column_part = lax.dynamic_slice_in_dim(placed, column * span, span, 2)
    grid = placed.reshape(count, width_part, row_parts, col_parts, tile)
    mine = lax.dynamic_index_in_dim(grid, column, 3, keepdims=False)
    return (column_part, jnp.transpose(mine, (0, 2, 1, 3)))


def make_term(inverse_block, column_full):
    return lax.dot_general(
        inverse_block, column_full, (((1,), (2,)), ((), ())), preferred_element_type=jnp.float32
    )


def local_step(summed, own_rows, previous, link, diag_part, column, row_first, rows_total):
    if link is None:
        coupled = jnp.zeros_like(summed)
    else:
        coupled = jnp.dot(previous, link.astype(jnp.float32), precision=highest)
    current = -(summed + coupled)
    own = own_rows.astype(jnp.float32)
    inner = jnp.dot(own, current, precision=highest) - jnp.dot(coupled.T, own.T, precision=highest)
    width = summed.shape[1]
    diag_cols = diag_part.shape[1]
    embedded = lax.dynamic_update_slice(
        jnp.zeros((width, width), jnp.float32), diag_part, (0, column * diag_cols)
    )
    return (current, row_first * embedded - inner / rows_total)


def chain_diag(total, chain_prev, link):
    if link is None:
        return total
    link_wide = link.astype(jnp.float32)
    return total + jnp.dot(
        link_wide.T, jnp.dot(chain_prev, link_wide, precision=highest), precision=highest
    )


def grid_plan(inverse_block, factor_cols, occupancy, row_block, coupling, diag_inverse):
    column = lax.axis_index("col")
    row_first = (lax.axis_index("row") == 0).astype(jnp.float32)
    row_parts = lax.axis_size("row")
    col_parts = lax.axis_size("col")
    local_rows = inverse_block.shape[0]
    rows_total = local_rows * row_parts
    supers, span, width_part = factor_cols.shape
    width = width_part * row_parts
    tile = local_rows // col_parts
    nblocks = occupancy.shape[1]
    diag_cols = diag_inverse.shape[2]
    flat = factor_cols.reshape(supers, span * width_part)
    column_list = []
    partial_list = []
    previous = None
    gathered = lax.all_gather(flat, "col", axis=1, tiled=True)
    placed = routed(gathered, occupancy, row_block, nblocks)
    column_part, outgoing = split_rows(placed, column, row_parts, col_parts, tile)
    column_full = lax.all_gather(column_part, "row", axis=1, tiled=True)
    arrived = lax.all_to_all(outgoing, "row", split_axis=1, concat_axis=1, tiled=True)
    own_all = arrived.reshape(supers, width, tile)
    summed = lax.psum_scatter(
        make_term(inverse_block, column_full), "col", scatter_dimension=0, tiled=True
    )
    for position in range(supers):
        link = None if position == 0 else coupling[position - 1]
        current, partial_value = local_step(
            summed[:, position, :],
            own_all[position],
            previous,
            link,
            diag_inverse[position],
            column,
            row_first,
            rows_total,
        )
        column_list.append(current)
        partial_list.append(partial_value)
        previous = current
    diag_list = []
    totals = lax.psum(jnp.stack(partial_list), ("row", "col"))
    chain_prev = None
    for position in range(supers):
        link = None if position == 0 else coupling[position - 1]
        diag_now = chain_diag(totals[position], chain_prev, link)
        diag_list.append(lax.dynamic_slice_in_dim(diag_now, column * diag_cols, diag_cols, 1))
        chain_prev = diag_now
    diagonals = jnp.stack(diag_list)
    return (jnp.stack(column_list), diagonals)


def swap(value, axis, bit, parts):
    return lax.ppermute(value, axis, [(i, i ^ bit) for i in range(parts)])


def across(value):
    return lax.ppermute(value, "col", [(0, 1), (1, 0)])


def after(values, *events):
    return lax.optimization_barrier((values, events))[0]


def split2(value):
    high = value.astype(bf16)
    return high, (value - high.astype(f32)).astype(bf16)


def nn(a, b):
    return lax.dot_general(a, b, (((1,), (0,)), ((), ())), preferred_element_type=f32)


def nt(a, b):
    return lax.dot_general(a, b, (((1,), (1,)), ((), ())), preferred_element_type=f32)


def nn2(pair, b):
    return nn(pair[0], b) + nn(pair[1], b)


def nn2r(a, pair):
    return nn(a, pair[0]) + nn(a, pair[1])


def owner_of(row, wave, count, j, i):
    return 4 * ((row // 4) ^ (wave * count + i)) + ((row % 4) ^ j)


def place_kernel(dims, *refs):
    supers, width, rows, span, part = dims
    occ_ref, block_ref = refs[:2]
    f_refs, pt = refs[2:6], refs[6]
    row, col = lax.axis_index("row"), lax.axis_index("col")
    per_side = span // 128
    for side in range(2):
        target = col if side == 0 else 1 - col
        for s in range(supers):
            for b in range(per_side):
                lanes = pl.ds(pl.multiple_of(block_ref[s, target * per_side + b] * 128, 128), 128)
                for wave in range(2):
                    source = f_refs[2 * side + wave]
                    for j in range(4):
                        for i in range(source.shape[1]):
                            first = owner_of(row, wave, source.shape[1], j, i) * part
                            pt[s, pl.ds(pl.multiple_of(first, part), part), lanes] = source[
                                j, i, s * part : (s + 1) * part, b * 128 : (b + 1) * 128
                            ]
    for s in range(supers):
        for b in range(2 * per_side):

            @pl.when(occ_ref[s, b] == 0)
            def _():
                lanes = pl.ds(pl.multiple_of(block_ref[s, b] * 128, 128), 128)
                pt[s, :, lanes] = jnp.zeros((width, 128), bf16)


def add_rows(wave, skip, dims, col, row, pt, z_refs, link_ref, sums, scratch):
    width, span = dims
    z_all, c0h, c0l, c1h, c1l, p1h, p1l, c2h, c2l, tmp, sem = scratch
    half_rows = z_all.shape[0]
    half_w = width // 2
    copies = []
    for side in range(2):
        target = col if side == 0 else 1 - col
        source = z_refs[side]
        local_rows = source.shape[2] - skip
        for j in range(4):
            for i in range(source.shape[1]):
                place = owner_of(row, wave, source.shape[1], j, i) % (half_rows // local_rows)
                copies.append(
                    pltpu.make_async_copy(
                        source.at[j, i, pl.ds(skip, local_rows)],
                        z_all.at[
                            pl.ds(pl.multiple_of(place * local_rows, local_rows), local_rows),
                            pl.ds(pl.multiple_of(target * span, span), span),
                        ],
                        sem,
                    )
                )
    for copy in copies:
        copy.start()
    for copy in copies:
        copy.wait()
    c_rows = pl.ds(pl.multiple_of(col * half_w, half_w), half_w)
    half = owner_of(row, wave, z_refs[0].shape[1], 0, 0) // (half_rows // local_rows)
    lanes = pl.ds(pl.multiple_of(half * half_rows, half_rows), half_rows)
    zm = z_all[...]
    cols0 = split2(-nt(zm, pt[0]))
    c0h[...], c0l[...] = cols0
    tmp[...] = nn2(cols0, link_ref[0])
    p1h[...], p1l[...] = split2(tmp[...])
    tmp[...] += nt(zm, pt[1])
    cols1 = split2(-tmp[...])
    c1h[...], c1l[...] = cols1
    cols2 = -(nt(zm, pt[2, c_rows, :]) + nn2(cols1, link_ref[1, :, c_rows]))
    c2h[...], c2l[...] = split2(cols2)
    left = pt[1, :, lanes]
    terms = [
        nn2r(pt[0, :, lanes], (c0h[...], c0l[...])),
        nn2r(left, (p1h[...], p1l[...])),
        nn2r(left, (c1h[...], c1l[...])),
        nn2r(pt[2, c_rows, lanes], (c1h[...], c1l[...])),
        nn2r(pt[2, :, lanes], (c2h[...], c2l[...])),
    ]
    for total, term in zip(sums, terms):
        total[...] = term if wave == 0 else total[...] + term


def first_kernel(dims, skip, *refs):
    pt, z_refs, link_ref = refs[0], refs[1:3], refs[3]
    sums, col_out, scratch = refs[4:9], refs[9], refs[10:]
    col, row = lax.axis_index("col"), lax.axis_index("row")
    add_rows(0, skip, dims, col, row, pt, z_refs, link_ref, sums, scratch)
    z_all, c0h, c0l, c1h, c1l = scratch[:5]
    tile = col_out.shape[1]
    place = row % (z_all.shape[0] // (2 * tile))
    own = pl.ds(pl.multiple_of(place * 2 * tile, 2 * tile), 2 * tile)
    cols1 = (c1h[own, :], c1l[own, :])
    mine = [
        c0h[own, :].astype(f32) + c0l[own, :].astype(f32),
        cols1[0].astype(f32) + cols1[1].astype(f32),
        -(nt(z_all[own, :], pt[2]) + nn2(cols1, link_ref[1])),
    ]
    for s, value in enumerate(mine):
        col_out[s] = jnp.where(col == 0, value[:tile], value[tile:])


def last_kernel(dims, rows, *refs):
    pt, z_refs, link_ref, diag_ref, diag_other_ref = refs[0], refs[1:3], refs[3], refs[4], refs[5]
    before, diag_out, sums, scratch = refs[6:11], refs[11], refs[12:17], refs[17:]
    col = lax.axis_index("col")
    width, _ = dims
    half_w = width // 2
    for total, value in zip(sums, before):
        total[...] = value[...]
    add_rows(1, 0, dims, col, lax.axis_index("row"), pt, z_refs, link_ref, sums, scratch)
    s0, u1, s1, n2, s2 = sums
    scale = 1.0 / rows
    c_rows = pl.ds(pl.multiple_of(col * half_w, half_w), half_w)

    def whole(s):
        mine, theirs = diag_ref[s], diag_other_ref[s]
        return jnp.concatenate([jnp.where(col == 0, mine, theirs), jnp.where(col == 0, theirs, mine)], axis=1)

    d0 = whole(0) - s0[...] * scale
    i1 = s1[...] - u1[...].T
    d1 = whole(1) - i1 * scale + nn2r(link_ref[0].T, split2(nn2(split2(d0), link_ref[0])))
    i2 = s2[...] - nn2(split2(n2[...]), link_ref[1]).T
    d2 = diag_ref[2] - i2 * scale + nn2r(link_ref[1].T, split2(nn2(split2(d1), link_ref[1, :, c_rows])))
    diag_out[0] = jnp.where(col == 0, d0[:, :half_w], d0[:, half_w:])
    diag_out[1] = jnp.where(col == 0, d1[:, :half_w], d1[:, half_w:])
    diag_out[2] = d2


def replicated_plan(inverse_block, factor_cols, occupancy, row_block, coupling, diag_inverse):
    row_parts = lax.axis_size("row")
    supers, span, part = factor_cols.shape
    width = part * row_parts
    local_rows = inverse_block.shape[0]
    rows = local_rows * row_parts
    count = row_parts // 8
    any_spec = pl.BlockSpec(memory_space=pl.ANY)
    smem = pl.BlockSpec(memory_space=pltpu.SMEM)
    vmem = pl.BlockSpec(memory_space=pltpu.VMEM)
    shape = jax.ShapeDtypeStruct

    def call(body, name, flops, **kwargs):
        return pl.pallas_call(
            body,
            compiler_params=pltpu.CompilerParams(vmem_limit_bytes=VMEM_LIMIT),
            cost_estimate=pl.CostEstimate(flops=flops, bytes_accessed=8 * 2**20, transcendentals=0),
            name=name,
            **kwargs,
        )

    outer = row_parts // 4
    x = lambda value: swap(value, "row", 1, row_parts)
    y = lambda value: swap(value, "row", 2, row_parts)
    line = lambda value, k: swap(value, "row", 4 * k, row_parts)

    def far(over_x, over_y, i):
        return x(over_y) if i % 2 == 0 else y(over_x)

    def late_wave(parts, *events):
        own = after(jnp.stack(parts), *events)
        return own, x(own), y(own)

    f_own = jnp.transpose(factor_cols, (0, 2, 1)).reshape(supers * part, span)
    f_late = [line(f_own, k) for k in range(count, outer)]
    own = jnp.concatenate([f_own, inverse_block], axis=0)
    early = []
    for k in range(count):
        value = own if k == 0 else line(own, k)
        value = after(value, *early[-1][1:3]) if k else value
        over_x, over_y = x(value), y(value)
        early.append([value, over_x, over_y, far(over_x, over_y, k)])
    first = jnp.stack([jnp.stack([p[j] for p in early]) for j in range(4)])
    first_other = across(first)
    block = after(inverse_block, *f_late, *early[-1][1:3])
    z_late = [line(block, k) for k in range(count, outer)]
    f_b, f_bx, f_by = late_wave(f_late, *early[-1][1:3], early[0][3])
    f_bx, f_by = after((f_bx, f_by), *z_late)
    f_far = jnp.stack([far(f_bx[i], f_by[i], i) for i in range(count)])
    f_last = jnp.stack([f_b, f_bx, f_by, f_far])
    f_last_other = across(f_last)
    z_b, z_bx, z_by = late_wave(z_late, f_bx, f_by)
    diag_other = across(diag_inverse)

    pt = call(
        functools.partial(place_kernel, (supers, width, rows, span, part)),
        "place", 2 * 10**9,
        out_shape=shape((supers, width, rows), bf16),
        in_specs=[smem] * 2 + [vmem] * 4,
        out_specs=vmem,
    )(occupancy, row_block, first, f_last, first_other, f_last_other)

    z_bx, z_by, pt = after((z_bx, z_by, pt), pt)
    z_far = jnp.stack([far(z_bx[i], z_by[i], i) for i in range(count)])
    dims = (width, span)
    half_rows, half_w = rows // 2, width // 2
    sum_shapes = [(width, width), (width, width), (width, width), (half_w, width), (width, half_w)]
    scratch = (
        [pltpu.VMEM((half_rows, 2 * span), bf16)]
        + [pltpu.VMEM((half_rows, width), bf16)] * 6
        + [pltpu.VMEM((half_rows, half_w), bf16)] * 2
        + [pltpu.VMEM((half_rows, width), f32), pltpu.SemaphoreType.DMA]
    )
    *sums, columns = call(
        functools.partial(first_kernel, dims, supers * part),
        "own_half", 8 * 10**9,
        out_shape=tuple(shape(v, f32) for v in sum_shapes) + (shape((supers, local_rows // 2, width), f32),),
        in_specs=[vmem] + [any_spec] * 2 + [vmem],
        out_specs=(vmem,) * 6,
        scratch_shapes=scratch,
    )(pt, first, first_other, coupling)
    z_far, *sums = after((z_far, *sums), sums[0])
    z_last = jnp.stack([z_b, z_bx, z_by, z_far])
    z_last_other = across(z_last)
    diagonals = call(
        functools.partial(last_kernel, dims, rows),
        "other_half", 12 * 10**9,
        out_shape=shape((supers, width, half_w), f32),
        in_specs=[vmem] + [any_spec] * 2 + [vmem] * 8,
        out_specs=vmem,
        scratch_shapes=[pltpu.VMEM(v, f32) for v in sum_shapes] + scratch,
    )(pt, z_last, z_last_other, coupling, diag_inverse, diag_other, *sums)
    return columns, diagonals


def solution(mesh):
    row_parts, col_parts = mesh.shape["row"], mesh.shape["col"]
    in_specs = (P("row", "col"), P(None, "col", "row"), P(), P(), P(), P(None, None, "col"))
    out_specs = (P(None, ("row", "col"), None), P(None, None, "col"))

    def per_device(inverse_block, factor_cols, *rest):
        held = (inverse_block.size + factor_cols.size) * 2 * row_parts * col_parts
        fits = held <= REPLICATE_BYTES and col_parts == 2 and row_parts in (8, 16)
        plan = replicated_plan if fits else grid_plan
        return plan(inverse_block, factor_cols, *rest)

    return jax.shard_map(
        per_device, mesh=mesh, in_specs=in_specs, out_specs=out_specs, check_vma=False
    )
```

```python
import functools

import jax
import jax.numpy as jnp
from jax import lax
from jax.experimental import pallas as pl
from jax.experimental.pallas import tpu as pltpu
from jax.sharding import PartitionSpec as P

highest = lax.Precision.HIGHEST
f32 = jnp.float32
bf16 = jnp.bfloat16

REPLICATE_BYTES = 12 * 2**20
VMEM_LIMIT = 40 * 2**20


def routed(gathered, occupancy, row_block, nblocks):
    count = gathered.shape[0]
    width_part = gathered.shape[1] // (nblocks * 128)
    blocks = gathered.reshape(count, nblocks, 128, width_part)
    levels = lax.broadcasted_iota(jnp.int32, (count, nblocks, nblocks), 1)
    picks = ((row_block[:, None, :] == levels) & (occupancy[:, None, :] > 0)).astype(jnp.bfloat16)
    placed = jnp.einsum("kqb,kbtx->kxqt", picks, blocks, preferred_element_type=jnp.float32)
    return placed.astype(jnp.bfloat16).reshape(count, width_part, nblocks * 128)


def split_rows(placed, column, row_parts, col_parts, tile):
    count, width_part, total = placed.shape
    span = total // col_parts
    column_part = lax.dynamic_slice_in_dim(placed, column * span, span, 2)
    grid = placed.reshape(count, width_part, row_parts, col_parts, tile)
    mine = lax.dynamic_index_in_dim(grid, column, 3, keepdims=False)
    return (column_part, jnp.transpose(mine, (0, 2, 1, 3)))


def make_term(inverse_block, column_full):
    return lax.dot_general(
        inverse_block, column_full, (((1,), (2,)), ((), ())), preferred_element_type=jnp.float32
    )


def local_step(summed, own_rows, previous, link, diag_part, column, row_first, rows_total):
    if link is None:
        coupled = jnp.zeros_like(summed)
    else:
        coupled = jnp.dot(previous, link.astype(jnp.float32), precision=highest)
    current = -(summed + coupled)
    own = own_rows.astype(jnp.float32)
    inner = jnp.dot(own, current, precision=highest) - jnp.dot(coupled.T, own.T, precision=highest)
    width = summed.shape[1]
    diag_cols = diag_part.shape[1]
    embedded = lax.dynamic_update_slice(
        jnp.zeros((width, width), jnp.float32), diag_part, (0, column * diag_cols)
    )
    return (current, row_first * embedded - inner / rows_total)


def chain_diag(total, chain_prev, link):
    if link is None:
        return total
    link_wide = link.astype(jnp.float32)
    return total + jnp.dot(
        link_wide.T, jnp.dot(chain_prev, link_wide, precision=highest), precision=highest
    )


def grid_plan(inverse_block, factor_cols, occupancy, row_block, coupling, diag_inverse):
    column = lax.axis_index("col")
    row_first = (lax.axis_index("row") == 0).astype(jnp.float32)
    row_parts = lax.axis_size("row")
    col_parts = lax.axis_size("col")
    local_rows = inverse_block.shape[0]
    rows_total = local_rows * row_parts
    supers, span, width_part = factor_cols.shape
    width = width_part * row_parts
    tile = local_rows // col_parts
    nblocks = occupancy.shape[1]
    diag_cols = diag_inverse.shape[2]
    flat = factor_cols.reshape(supers, span * width_part)
    column_list = []
    partial_list = []
    previous = None
    gathered = lax.all_gather(flat, "col", axis=1, tiled=True)
    placed = routed(gathered, occupancy, row_block, nblocks)
    column_part, outgoing = split_rows(placed, column, row_parts, col_parts, tile)
    column_full = lax.all_gather(column_part, "row", axis=1, tiled=True)
    arrived = lax.all_to_all(outgoing, "row", split_axis=1, concat_axis=1, tiled=True)
    own_all = arrived.reshape(supers, width, tile)
    summed = lax.psum_scatter(
        make_term(inverse_block, column_full), "col", scatter_dimension=0, tiled=True
    )
    for position in range(supers):
        link = None if position == 0 else coupling[position - 1]
        current, partial_value = local_step(
            summed[:, position, :],
            own_all[position],
            previous,
            link,
            diag_inverse[position],
            column,
            row_first,
            rows_total,
        )
        column_list.append(current)
        partial_list.append(partial_value)
        previous = current
    diag_list = []
    totals = lax.psum(jnp.stack(partial_list), ("row", "col"))
    chain_prev = None
    for position in range(supers):
        link = None if position == 0 else coupling[position - 1]
        diag_now = chain_diag(totals[position], chain_prev, link)
        diag_list.append(lax.dynamic_slice_in_dim(diag_now, column * diag_cols, diag_cols, 1))
        chain_prev = diag_now
    diagonals = jnp.stack(diag_list)
    return (jnp.stack(column_list), diagonals)


def swap(value, axis, bit, parts):
    return lax.ppermute(value, axis, [(i, i ^ bit) for i in range(parts)])


def across(value):
    return lax.ppermute(value, "col", [(0, 1), (1, 0)])


def after(values, *events):
    return lax.optimization_barrier((values, events))[0]


def split2(value):
    high = value.astype(bf16)
    return high, (value - high.astype(f32)).astype(bf16)


def nn(a, b):
    return lax.dot_general(a, b, (((1,), (0,)), ((), ())), preferred_element_type=f32)


def nt(a, b):
    return lax.dot_general(a, b, (((1,), (1,)), ((), ())), preferred_element_type=f32)


def nn2(pair, b):
    return nn(pair[0], b) + nn(pair[1], b)


def nn2r(a, pair):
    return nn(a, pair[0]) + nn(a, pair[1])


def owner_of(row, wave, count, j, i):
    return 4 * ((row // 4) ^ (wave * count + i)) + ((row % 4) ^ j)


def place_kernel(dims, *refs):
    supers, width, rows, span, part = dims
    occ_ref, block_ref = refs[:2]
    f_refs, pt = refs[2:6], refs[6]
    row, col = lax.axis_index("row"), lax.axis_index("col")
    per_side = span // 128
    for side in range(2):
        target = col if side == 0 else 1 - col
        for s in range(supers):
            for b in range(per_side):
                lanes = pl.ds(pl.multiple_of(block_ref[s, target * per_side + b] * 128, 128), 128)
                for wave in range(2):
                    source = f_refs[2 * side + wave]
                    for j in range(4):
                        for i in range(source.shape[1]):
                            first = owner_of(row, wave, source.shape[1], j, i) * part
                            pt[s, pl.ds(pl.multiple_of(first, part), part), lanes] = source[
                                j, i, s * part : (s + 1) * part, b * 128 : (b + 1) * 128
                            ]
    for s in range(supers):
        for b in range(2 * per_side):

            @pl.when(occ_ref[s, b] == 0)
            def _():
                lanes = pl.ds(pl.multiple_of(block_ref[s, b] * 128, 128), 128)
                pt[s, :, lanes] = jnp.zeros((width, 128), bf16)


def add_rows(wave, skip, dims, col, row, pt, z_refs, link_ref, sums, scratch):
    width, span = dims
    z_all, c0h, c0l, c1h, c1l, p1h, p1l, c2h, c2l, tmp, sem = scratch
    half_rows = z_all.shape[0]
    half_w = width // 2
    copies = []
    for side in range(2):
        target = col if side == 0 else 1 - col
        source = z_refs[side]
        local_rows = source.shape[2] - skip
        for j in range(4):
            for i in range(source.shape[1]):
                place = owner_of(row, wave, source.shape[1], j, i) % (half_rows // local_rows)
                copies.append(
                    pltpu.make_async_copy(
                        source.at[j, i, pl.ds(skip, local_rows)],
                        z_all.at[
                            pl.ds(pl.multiple_of(place * local_rows, local_rows), local_rows),
                            pl.ds(pl.multiple_of(target * span, span), span),
                        ],
                        sem,
                    )
                )
    for copy in copies:
        copy.start()
    for copy in copies:
        copy.wait()
    c_rows = pl.ds(pl.multiple_of(col * half_w, half_w), half_w)
    half = owner_of(row, wave, z_refs[0].shape[1], 0, 0) // (half_rows // local_rows)
    lanes = pl.ds(pl.multiple_of(half * half_rows, half_rows), half_rows)
    zm = z_all[...]
    cols0 = split2(-nt(zm, pt[0]))
    c0h[...], c0l[...] = cols0
    tmp[...] = nn2(cols0, link_ref[0])
    p1h[...], p1l[...] = split2(tmp[...])
    tmp[...] += nt(zm, pt[1])
    cols1 = split2(-tmp[...])
    c1h[...], c1l[...] = cols1
    cols2 = -(nt(zm, pt[2, c_rows, :]) + nn2(cols1, link_ref[1, :, c_rows]))
    c2h[...], c2l[...] = split2(cols2)
    left = pt[1, :, lanes]
    terms = [
        nn2r(pt[0, :, lanes], (c0h[...], c0l[...])),
        nn2r(left, (p1h[...], p1l[...])),
        nn2r(left, (c1h[...], c1l[...])),
        nn2r(pt[2, c_rows, lanes], (c1h[...], c1l[...])),
        nn2r(pt[2, :, lanes], (c2h[...], c2l[...])),
    ]
    for total, term in zip(sums, terms):
        total[...] = term if wave == 0 else total[...] + term


def first_kernel(dims, skip, *refs):
    pt, z_refs, link_ref = refs[0], refs[1:3], refs[3]
    sums, col_out, scratch = refs[4:9], refs[9], refs[10:]
    col, row = lax.axis_index("col"), lax.axis_index("row")
    add_rows(0, skip, dims, col, row, pt, z_refs, link_ref, sums, scratch)
    z_all, c0h, c0l, c1h, c1l = scratch[:5]
    tile = col_out.shape[1]
    place = row % (z_all.shape[0] // (2 * tile))
    own = pl.ds(pl.multiple_of(place * 2 * tile, 2 * tile), 2 * tile)
    cols1 = (c1h[own, :], c1l[own, :])
    mine = [
        c0h[own, :].astype(f32) + c0l[own, :].astype(f32),
        cols1[0].astype(f32) + cols1[1].astype(f32),
        -(nt(z_all[own, :], pt[2]) + nn2(cols1, link_ref[1])),
    ]
    for s, value in enumerate(mine):
        col_out[s] = jnp.where(col == 0, value[:tile], value[tile:])


def last_kernel(dims, rows, *refs):
    pt, z_refs, link_ref, diag_ref, diag_other_ref = refs[0], refs[1:3], refs[3], refs[4], refs[5]
    before, diag_out, sums, scratch = refs[6:11], refs[11], refs[12:17], refs[17:]
    col = lax.axis_index("col")
    width, _ = dims
    half_w = width // 2
    for total, value in zip(sums, before):
        total[...] = value[...]
    add_rows(1, 0, dims, col, lax.axis_index("row"), pt, z_refs, link_ref, sums, scratch)
    s0, u1, s1, n2, s2 = sums
    scale = 1.0 / rows
    c_rows = pl.ds(pl.multiple_of(col * half_w, half_w), half_w)

    def whole(s):
        mine, theirs = diag_ref[s], diag_other_ref[s]
        return jnp.concatenate([jnp.where(col == 0, mine, theirs), jnp.where(col == 0, theirs, mine)], axis=1)

    d0 = whole(0) - s0[...] * scale
    i1 = s1[...] - u1[...].T
    d1 = whole(1) - i1 * scale + nn2r(link_ref[0].T, split2(nn2(split2(d0), link_ref[0])))
    i2 = s2[...] - nn2(split2(n2[...]), link_ref[1]).T
    d2 = diag_ref[2] - i2 * scale + nn2r(link_ref[1].T, split2(nn2(split2(d1), link_ref[1, :, c_rows])))
    diag_out[0] = jnp.where(col == 0, d0[:, :half_w], d0[:, half_w:])
    diag_out[1] = jnp.where(col == 0, d1[:, :half_w], d1[:, half_w:])
    diag_out[2] = d2


def replicated_plan(inverse_block, factor_cols, occupancy, row_block, coupling, diag_inverse):
    row_parts = lax.axis_size("row")
    supers, span, part = factor_cols.shape
    width = part * row_parts
    local_rows = inverse_block.shape[0]
    rows = local_rows * row_parts
    count = row_parts // 8
    any_spec = pl.BlockSpec(memory_space=pl.ANY)
    smem = pl.BlockSpec(memory_space=pltpu.SMEM)
    vmem = pl.BlockSpec(memory_space=pltpu.VMEM)
    shape = jax.ShapeDtypeStruct

    def call(body, name, flops, **kwargs):
        return pl.pallas_call(
            body,
            compiler_params=pltpu.CompilerParams(vmem_limit_bytes=VMEM_LIMIT),
            cost_estimate=pl.CostEstimate(flops=flops, bytes_accessed=8 * 2**20, transcendentals=0),
            name=name,
            **kwargs,
        )

    outer = row_parts // 4
    x = lambda value: swap(value, "row", 1, row_parts)
    y = lambda value: swap(value, "row", 2, row_parts)
    line = lambda value, k: swap(value, "row", 4 * k, row_parts)

    def far(over_x, over_y, i):
        return x(over_y) if i % 2 == 0 else y(over_x)

    def late_wave(parts, *events):
        own = after(jnp.stack(parts), *events)
        return own, x(own), y(own)

    f_own = jnp.transpose(factor_cols, (0, 2, 1)).reshape(supers * part, span)
    f_late = [line(f_own, k) for k in range(count, outer)]
    own = jnp.concatenate([f_own, inverse_block], axis=0)
    early = []
    for k in range(count):
        value = own if k == 0 else line(own, k)
        value = after(value, *early[-1][1:3]) if k else value
        over_x, over_y = x(value), y(value)
        early.append([value, over_x, over_y, far(over_x, over_y, k)])
    block = after(inverse_block, *f_late, *early[-1][1:3])
    z_late = [line(block, k) for k in range(count, outer)]
    f_b, f_bx, f_by = late_wave(f_late, *early[-1][1:3], early[0][3])
    first = jnp.stack([jnp.stack([p[j] for p in early]) for j in range(4)])
    first_other = across(first)
    z_b = jnp.stack(z_late)
    f_rows = supers * part
    z_flat = z_b.reshape(count * local_rows, span)
    by_x = [f_by[i] for i in range(0, count, 2)] + [z_flat]
    by_y = [f_bx[i] for i in range(1, count, 2)] + [z_flat]
    by_x, by_y = x(jnp.concatenate(by_x, axis=0)), y(jnp.concatenate(by_y, axis=0))
    f_far = [(by_x, by_y)[i % 2][i // 2 * f_rows : (i // 2 + 1) * f_rows] for i in range(count)]
    z_bx = by_x[-count * local_rows :].reshape(z_b.shape)
    z_by = by_y[-count * local_rows :].reshape(z_b.shape)
    f_last = jnp.stack([f_b, f_bx, f_by, jnp.stack(f_far)])
    f_last_other = across(f_last)
    z_far = jnp.stack([far(z_bx[i], z_by[i], i) for i in range(count)])
    diag_other = across(diag_inverse)

    pt = call(
        functools.partial(place_kernel, (supers, width, rows, span, part)),
        "place", 2 * 10**9,
        out_shape=shape((supers, width, rows), bf16),
        in_specs=[smem] * 2 + [vmem] * 4,
        out_specs=vmem,
    )(occupancy, row_block, first, f_last, first_other, f_last_other)

    z_far, pt = after((z_far, pt), pt)
    z_last = jnp.stack([z_b, z_bx, z_by, z_far])
    z_last_other = across(z_last)
    dims = (width, span)
    half_rows, half_w = rows // 2, width // 2
    sum_shapes = [(width, width), (width, width), (width, width), (half_w, width), (width, half_w)]
    scratch = (
        [pltpu.VMEM((half_rows, 2 * span), bf16)]
        + [pltpu.VMEM((half_rows, width), bf16)] * 6
        + [pltpu.VMEM((half_rows, half_w), bf16)] * 2
        + [pltpu.VMEM((half_rows, width), f32), pltpu.SemaphoreType.DMA]
    )
    *sums, columns = call(
        functools.partial(first_kernel, dims, supers * part),
        "own_half", 8 * 10**9,
        out_shape=tuple(shape(v, f32) for v in sum_shapes) + (shape((supers, local_rows // 2, width), f32),),
        in_specs=[vmem] + [any_spec] * 2 + [vmem],
        out_specs=(vmem,) * 6,
        scratch_shapes=scratch,
    )(pt, first, first_other, coupling)
    diagonals = call(
        functools.partial(last_kernel, dims, rows),
        "other_half", 12 * 10**9,
        out_shape=shape((supers, width, half_w), f32),
        in_specs=[vmem] + [any_spec] * 2 + [vmem] * 8,
        out_specs=vmem,
        scratch_shapes=[pltpu.VMEM(v, f32) for v in sum_shapes] + scratch,
    )(pt, z_last, z_last_other, coupling, diag_inverse, diag_other, *sums)
    return columns, diagonals


def solution(mesh):
    row_parts, col_parts = mesh.shape["row"], mesh.shape["col"]
    in_specs = (P("row", "col"), P(None, "col", "row"), P(), P(), P(), P(None, None, "col"))
    out_specs = (P(None, ("row", "col"), None), P(None, None, "col"))

    def per_device(inverse_block, factor_cols, *rest):
        held = (inverse_block.size + factor_cols.size) * 2 * row_parts * col_parts
        fits = held <= REPLICATE_BYTES and col_parts == 2 and row_parts in (8, 16)
        plan = replicated_plan if fits else grid_plan
        return plan(inverse_block, factor_cols, *rest)

    return jax.shard_map(
        per_device, mesh=mesh, in_specs=in_specs, out_specs=out_specs, check_vma=False
    )
```

```python
import functools

import jax
import jax.numpy as jnp
from jax import lax
from jax.experimental import pallas as pl
from jax.experimental.pallas import tpu as pltpu
from jax.sharding import PartitionSpec as P

highest = lax.Precision.HIGHEST
f32 = jnp.float32
bf16 = jnp.bfloat16

REPLICATE_BYTES = 12 * 2**20
VMEM_LIMIT = 40 * 2**20


def routed(gathered, occupancy, row_block, nblocks):
    count = gathered.shape[0]
    width_part = gathered.shape[1] // (nblocks * 128)
    blocks = gathered.reshape(count, nblocks, 128, width_part)
    levels = lax.broadcasted_iota(jnp.int32, (count, nblocks, nblocks), 1)
    picks = ((row_block[:, None, :] == levels) & (occupancy[:, None, :] > 0)).astype(jnp.bfloat16)
    placed = jnp.einsum("kqb,kbtx->kxqt", picks, blocks, preferred_element_type=jnp.float32)
    return placed.astype(jnp.bfloat16).reshape(count, width_part, nblocks * 128)


def split_rows(placed, column, row_parts, col_parts, tile):
    count, width_part, total = placed.shape
    span = total // col_parts
    column_part = lax.dynamic_slice_in_dim(placed, column * span, span, 2)
    grid = placed.reshape(count, width_part, row_parts, col_parts, tile)
    mine = lax.dynamic_index_in_dim(grid, column, 3, keepdims=False)
    return (column_part, jnp.transpose(mine, (0, 2, 1, 3)))


def make_term(inverse_block, column_full):
    return lax.dot_general(
        inverse_block, column_full, (((1,), (2,)), ((), ())), preferred_element_type=jnp.float32
    )


def local_step(summed, own_rows, previous, link, diag_part, column, row_first, rows_total):
    if link is None:
        coupled = jnp.zeros_like(summed)
    else:
        coupled = jnp.dot(previous, link.astype(jnp.float32), precision=highest)
    current = -(summed + coupled)
    own = own_rows.astype(jnp.float32)
    inner = jnp.dot(own, current, precision=highest) - jnp.dot(coupled.T, own.T, precision=highest)
    width = summed.shape[1]
    diag_cols = diag_part.shape[1]
    embedded = lax.dynamic_update_slice(
        jnp.zeros((width, width), jnp.float32), diag_part, (0, column * diag_cols)
    )
    return (current, row_first * embedded - inner / rows_total)


def chain_diag(total, chain_prev, link):
    if link is None:
        return total
    link_wide = link.astype(jnp.float32)
    return total + jnp.dot(
        link_wide.T, jnp.dot(chain_prev, link_wide, precision=highest), precision=highest
    )


def grid_plan(inverse_block, factor_cols, occupancy, row_block, coupling, diag_inverse):
    column = lax.axis_index("col")
    row_first = (lax.axis_index("row") == 0).astype(jnp.float32)
    row_parts = lax.axis_size("row")
    col_parts = lax.axis_size("col")
    local_rows = inverse_block.shape[0]
    rows_total = local_rows * row_parts
    supers, span, width_part = factor_cols.shape
    width = width_part * row_parts
    tile = local_rows // col_parts
    nblocks = occupancy.shape[1]
    diag_cols = diag_inverse.shape[2]
    flat = factor_cols.reshape(supers, span * width_part)
    column_list = []
    partial_list = []
    previous = None
    gathered = lax.all_gather(flat, "col", axis=1, tiled=True)
    placed = routed(gathered, occupancy, row_block, nblocks)
    column_part, outgoing = split_rows(placed, column, row_parts, col_parts, tile)
    column_full = lax.all_gather(column_part, "row", axis=1, tiled=True)
    arrived = lax.all_to_all(outgoing, "row", split_axis=1, concat_axis=1, tiled=True)
    own_all = arrived.reshape(supers, width, tile)
    summed = lax.psum_scatter(
        make_term(inverse_block, column_full), "col", scatter_dimension=0, tiled=True
    )
    for position in range(supers):
        link = None if position == 0 else coupling[position - 1]
        current, partial_value = local_step(
            summed[:, position, :],
            own_all[position],
            previous,
            link,
            diag_inverse[position],
            column,
            row_first,
            rows_total,
        )
        column_list.append(current)
        partial_list.append(partial_value)
        previous = current
    diag_list = []
    totals = lax.psum(jnp.stack(partial_list), ("row", "col"))
    chain_prev = None
    for position in range(supers):
        link = None if position == 0 else coupling[position - 1]
        diag_now = chain_diag(totals[position], chain_prev, link)
        diag_list.append(lax.dynamic_slice_in_dim(diag_now, column * diag_cols, diag_cols, 1))
        chain_prev = diag_now
    diagonals = jnp.stack(diag_list)
    return (jnp.stack(column_list), diagonals)


def swap(value, axis, bit, parts):
    return lax.ppermute(value, axis, [(i, i ^ bit) for i in range(parts)])


def across(value):
    return lax.ppermute(value, "col", [(0, 1), (1, 0)])


def after(values, *events):
    return lax.optimization_barrier((values, events))[0]


def split2(value):
    high = value.astype(bf16)
    return high, (value - high.astype(f32)).astype(bf16)


def nn(a, b):
    return lax.dot_general(a, b, (((1,), (0,)), ((), ())), preferred_element_type=f32)


def nt(a, b):
    return lax.dot_general(a, b, (((1,), (1,)), ((), ())), preferred_element_type=f32)


def nn2(pair, b):
    return nn(pair[0], b) + nn(pair[1], b)


def nn2r(a, pair):
    return nn(a, pair[0]) + nn(a, pair[1])


def owner_of(row, wave, count, j, i):
    return 4 * ((row // 4) ^ (wave * count + i)) + ((row % 4) ^ j)


def place_kernel(dims, *refs):
    supers, width, rows, span, part = dims
    occ_ref, block_ref = refs[:2]
    f_refs, pt = refs[2:6], refs[6]
    row, col = lax.axis_index("row"), lax.axis_index("col")
    per_side = span // 128
    for side in range(2):
        target = col if side == 0 else 1 - col
        for s in range(supers):
            for b in range(per_side):
                lanes = pl.ds(pl.multiple_of(block_ref[s, target * per_side + b] * 128, 128), 128)
                for wave in range(2):
                    source = f_refs[2 * side + wave]
                    for j in range(4):
                        for i in range(source.shape[1]):
                            first = owner_of(row, wave, source.shape[1], j, i) * part
                            pt[s, pl.ds(pl.multiple_of(first, part), part), lanes] = source[
                                j, i, s * part : (s + 1) * part, b * 128 : (b + 1) * 128
                            ]
    for s in range(supers):
        for b in range(2 * per_side):

            @pl.when(occ_ref[s, b] == 0)
            def _():
                lanes = pl.ds(pl.multiple_of(block_ref[s, b] * 128, 128), 128)
                pt[s, :, lanes] = jnp.zeros((width, 128), bf16)


def add_rows(wave, skip, dims, col, row, pt, z_refs, link_ref, before, sums, scratch):
    width, span = dims
    z_all, c0h, c0l, c1h, c1l, p1h, p1l, c2h, c2l, tmp, sem = scratch
    half_rows = z_all.shape[0]
    half_w = width // 2
    copies = []
    for side in range(2):
        target = col if side == 0 else 1 - col
        source = z_refs[side]
        local_rows = source.shape[2] - skip
        for j in range(4):
            for i in range(source.shape[1]):
                place = owner_of(row, wave, source.shape[1], j, i) % (half_rows // local_rows)
                copies.append(
                    pltpu.make_async_copy(
                        source.at[j, i, pl.ds(skip, local_rows)],
                        z_all.at[
                            pl.ds(pl.multiple_of(place * local_rows, local_rows), local_rows),
                            pl.ds(pl.multiple_of(target * span, span), span),
                        ],
                        sem,
                    )
                )
    for copy in copies:
        copy.start()
    for copy in copies:
        copy.wait()
    c_rows = pl.ds(pl.multiple_of(col * half_w, half_w), half_w)
    half = owner_of(row, wave, z_refs[0].shape[1], 0, 0) // (half_rows // local_rows)
    lanes = pl.ds(pl.multiple_of(half * half_rows, half_rows), half_rows)
    zm = z_all[...]
    cols0 = split2(-nt(zm, pt[0]))
    c0h[...], c0l[...] = cols0
    tmp[...] = nn2(cols0, link_ref[0])
    p1h[...], p1l[...] = split2(tmp[...])
    tmp[...] += nt(zm, pt[1])
    cols1 = split2(-tmp[...])
    c1h[...], c1l[...] = cols1
    cols2 = -(nt(zm, pt[2, c_rows, :]) + nn2(cols1, link_ref[1, :, c_rows]))
    c2h[...], c2l[...] = split2(cols2)
    left = pt[1, :, lanes]
    terms = [
        nn2r(pt[0, :, lanes], (c0h[...], c0l[...])),
        nn2r(left, (p1h[...], p1l[...])),
        nn2r(left, (c1h[...], c1l[...])),
        nn2r(pt[2, c_rows, lanes], (c1h[...], c1l[...])),
        nn2r(pt[2, :, lanes], (c2h[...], c2l[...])),
    ]
    for i, term in enumerate(terms):
        sums[i][...] = before[i][...] + term if before else term


def first_kernel(dims, skip, *refs):
    pt, z_refs, link_ref = refs[0], refs[1:3], refs[3]
    sums, col_out, scratch = refs[4:9], refs[9], refs[10:]
    col, row = lax.axis_index("col"), lax.axis_index("row")
    add_rows(0, skip, dims, col, row, pt, z_refs, link_ref, (), sums, scratch)
    z_all, c0h, c0l, c1h, c1l = scratch[:5]
    tile = col_out.shape[1]
    place = row % (z_all.shape[0] // (2 * tile))
    own = pl.ds(pl.multiple_of(place * 2 * tile, 2 * tile), 2 * tile)
    cols1 = (c1h[own, :], c1l[own, :])
    mine = [
        c0h[own, :].astype(f32) + c0l[own, :].astype(f32),
        cols1[0].astype(f32) + cols1[1].astype(f32),
        -(nt(z_all[own, :], pt[2]) + nn2(cols1, link_ref[1])),
    ]
    for s, value in enumerate(mine):
        col_out[s] = jnp.where(col == 0, value[:tile], value[tile:])


def last_kernel(dims, rows, *refs):
    pt, z_refs, link_ref, diag_ref, diag_other_ref = refs[0], refs[1:3], refs[3], refs[4], refs[5]
    before, diag_out, sums, scratch = refs[6:11], refs[11], refs[12:17], refs[17:]
    col = lax.axis_index("col")
    width, _ = dims
    half_w = width // 2
    add_rows(1, 0, dims, col, lax.axis_index("row"), pt, z_refs, link_ref, before, sums, scratch)
    s0, u1, s1, n2, s2 = sums
    scale = 1.0 / rows
    c_rows = pl.ds(pl.multiple_of(col * half_w, half_w), half_w)

    def whole(s):
        mine, theirs = diag_ref[s], diag_other_ref[s]
        return jnp.concatenate([jnp.where(col == 0, mine, theirs), jnp.where(col == 0, theirs, mine)], axis=1)

    d0 = whole(0) - s0[...] * scale
    i1 = s1[...] - u1[...].T
    d1 = whole(1) - i1 * scale + nn2r(link_ref[0].T, split2(nn2(split2(d0), link_ref[0])))
    i2 = s2[...] - nn2(split2(n2[...]), link_ref[1]).T
    d2 = diag_ref[2] - i2 * scale + nn2r(link_ref[1].T, split2(nn2(split2(d1), link_ref[1, :, c_rows])))
    diag_out[0] = jnp.where(col == 0, d0[:, :half_w], d0[:, half_w:])
    diag_out[1] = jnp.where(col == 0, d1[:, :half_w], d1[:, half_w:])
    diag_out[2] = d2


def replicated_plan(inverse_block, factor_cols, occupancy, row_block, coupling, diag_inverse):
    row_parts = lax.axis_size("row")
    supers, span, part = factor_cols.shape
    width = part * row_parts
    local_rows = inverse_block.shape[0]
    rows = local_rows * row_parts
    count = row_parts // 8
    any_spec = pl.BlockSpec(memory_space=pl.ANY)
    smem = pl.BlockSpec(memory_space=pltpu.SMEM)
    vmem = pl.BlockSpec(memory_space=pltpu.VMEM)
    shape = jax.ShapeDtypeStruct

    def call(body, name, flops, **kwargs):
        return pl.pallas_call(
            body,
            compiler_params=pltpu.CompilerParams(vmem_limit_bytes=VMEM_LIMIT),
            cost_estimate=pl.CostEstimate(flops=flops, bytes_accessed=8 * 2**20, transcendentals=0),
            name=name,
            **kwargs,
        )

    outer = row_parts // 4
    x = lambda value: swap(value, "row", 1, row_parts)
    y = lambda value: swap(value, "row", 2, row_parts)
    line = lambda value, k: swap(value, "row", 4 * k, row_parts)

    def far(over_x, over_y, i):
        return x(over_y) if i % 2 == 0 else y(over_x)

    def late_wave(parts, *events):
        own = after(jnp.stack(parts), *events)
        return own, x(own), y(own)

    f_own = jnp.transpose(factor_cols, (0, 2, 1)).reshape(supers * part, span)
    f_late = [line(f_own, k) for k in range(count, outer)]
    own = jnp.concatenate([f_own, inverse_block], axis=0)
    early = []
    for k in range(count):
        value = own if k == 0 else line(own, k)
        value = after(value, *early[-1][1:3]) if k else value
        over_x, over_y = x(value), y(value)
        early.append([value, over_x, over_y, far(over_x, over_y, k)])
    first = jnp.stack([jnp.stack([p[j] for p in early]) for j in range(4)])
    first_other = across(first)
    block = after(inverse_block, *f_late, *early[-1][1:3])
    z_late = [line(block, k) for k in range(count, outer)]
    f_b, f_bx, f_by = late_wave(f_late, *early[-1][1:3], early[0][3])
    f_bx, f_by = after((f_bx, f_by), *z_late)
    f_far = jnp.stack([far(f_bx[i], f_by[i], i) for i in range(count)])
    f_last = jnp.stack([f_b, f_bx, f_by, f_far])
    z_b, z_bx, z_by = late_wave(z_late, f_bx, f_by)
    f_last_other = across(after(f_last, z_bx, z_by))
    diag_other = across(diag_inverse)

    pt = call(
        functools.partial(place_kernel, (supers, width, rows, span, part)),
        "place", 2 * 10**9,
        out_shape=shape((supers, width, rows), bf16),
        in_specs=[smem] * 2 + [vmem] * 4,
        out_specs=vmem,
    )(occupancy, row_block, first, f_last, first_other, f_last_other)

    z_far = jnp.stack([far(z_bx[i], z_by[i], i) for i in range(count)])
    z_far, pt = after((z_far, pt), pt)
    z_last = jnp.stack([z_b, z_bx, z_by, z_far])
    z_last_other = across(z_last)
    dims = (width, span)
    half_rows, half_w = rows // 2, width // 2
    sum_shapes = [(width, width), (width, width), (width, width), (half_w, width), (width, half_w)]
    scratch = (
        [pltpu.VMEM((half_rows, 2 * span), bf16)]
        + [pltpu.VMEM((half_rows, width), bf16)] * 6
        + [pltpu.VMEM((half_rows, half_w), bf16)] * 2
        + [pltpu.VMEM((half_rows, width), f32), pltpu.SemaphoreType.DMA]
    )
    *sums, columns = call(
        functools.partial(first_kernel, dims, supers * part),
        "own_half", 8 * 10**9,
        out_shape=tuple(shape(v, f32) for v in sum_shapes) + (shape((supers, local_rows // 2, width), f32),),
        in_specs=[vmem] + [any_spec] * 2 + [vmem],
        out_specs=(vmem,) * 6,
        scratch_shapes=scratch,
    )(pt, first, first_other, coupling)
    diagonals = call(
        functools.partial(last_kernel, dims, rows),
        "other_half", 12 * 10**9,
        out_shape=shape((supers, width, half_w), f32),
        in_specs=[vmem] + [any_spec] * 2 + [vmem] * 8,
        out_specs=vmem,
        scratch_shapes=[pltpu.VMEM(v, f32) for v in sum_shapes] + scratch,
    )(pt, z_last, z_last_other, coupling, diag_inverse, diag_other, *sums)
    return columns, diagonals


def solution(mesh):
    row_parts, col_parts = mesh.shape["row"], mesh.shape["col"]
    in_specs = (P("row", "col"), P(None, "col", "row"), P(), P(), P(), P(None, None, "col"))
    out_specs = (P(None, ("row", "col"), None), P(None, None, "col"))

    def per_device(inverse_block, factor_cols, *rest):
        held = (inverse_block.size + factor_cols.size) * 2 * row_parts * col_parts
        fits = held <= REPLICATE_BYTES and col_parts == 2 and row_parts in (8, 16)
        plan = replicated_plan if fits else grid_plan
        return plan(inverse_block, factor_cols, *rest)

    return jax.shard_map(
        per_device, mesh=mesh, in_specs=in_specs, out_specs=out_specs, check_vma=False
    )
```

```python
import functools

import jax
import jax.numpy as jnp
from jax import lax
from jax.experimental import pallas as pl
from jax.experimental.pallas import tpu as pltpu
from jax.sharding import PartitionSpec as P

highest = lax.Precision.HIGHEST
f32 = jnp.float32
bf16 = jnp.bfloat16

REPLICATE_BYTES = 12 * 2**20
VMEM_LIMIT = 36 * 2**20


def routed(gathered, occupancy, row_block, nblocks):
    count = gathered.shape[0]
    width_part = gathered.shape[1] // (nblocks * 128)
    blocks = gathered.reshape(count, nblocks, 128, width_part)
    levels = lax.broadcasted_iota(jnp.int32, (count, nblocks, nblocks), 1)
    picks = ((row_block[:, None, :] == levels) & (occupancy[:, None, :] > 0)).astype(jnp.bfloat16)
    placed = jnp.einsum("kqb,kbtx->kxqt", picks, blocks, preferred_element_type=jnp.float32)
    return placed.astype(jnp.bfloat16).reshape(count, width_part, nblocks * 128)


def split_rows(placed, column, row_parts, col_parts, tile):
    count, width_part, total = placed.shape
    span = total // col_parts
    column_part = lax.dynamic_slice_in_dim(placed, column * span, span, 2)
    grid = placed.reshape(count, width_part, row_parts, col_parts, tile)
    mine = lax.dynamic_index_in_dim(grid, column, 3, keepdims=False)
    return (column_part, jnp.transpose(mine, (0, 2, 1, 3)))


def make_term(inverse_block, column_full):
    return lax.dot_general(
        inverse_block, column_full, (((1,), (2,)), ((), ())), preferred_element_type=jnp.float32
    )


def local_step(summed, own_rows, previous, link, diag_part, column, row_first, rows_total):
    if link is None:
        coupled = jnp.zeros_like(summed)
    else:
        coupled = jnp.dot(previous, link.astype(jnp.float32), precision=highest)
    current = -(summed + coupled)
    own = own_rows.astype(jnp.float32)
    inner = jnp.dot(own, current, precision=highest) - jnp.dot(coupled.T, own.T, precision=highest)
    width = summed.shape[1]
    diag_cols = diag_part.shape[1]
    embedded = lax.dynamic_update_slice(
        jnp.zeros((width, width), jnp.float32), diag_part, (0, column * diag_cols)
    )
    return (current, row_first * embedded - inner / rows_total)


def chain_diag(total, chain_prev, link):
    if link is None:
        return total
    link_wide = link.astype(jnp.float32)
    return total + jnp.dot(
        link_wide.T, jnp.dot(chain_prev, link_wide, precision=highest), precision=highest
    )


def grid_plan(inverse_block, factor_cols, occupancy, row_block, coupling, diag_inverse):
    column = lax.axis_index("col")
    row_first = (lax.axis_index("row") == 0).astype(jnp.float32)
    row_parts = lax.axis_size("row")
    col_parts = lax.axis_size("col")
    local_rows = inverse_block.shape[0]
    rows_total = local_rows * row_parts
    supers, span, width_part = factor_cols.shape
    width = width_part * row_parts
    tile = local_rows // col_parts
    nblocks = occupancy.shape[1]
    diag_cols = diag_inverse.shape[2]
    flat = factor_cols.reshape(supers, span * width_part)
    column_list = []
    partial_list = []
    previous = None
    gathered = lax.all_gather(flat, "col", axis=1, tiled=True)
    placed = routed(gathered, occupancy, row_block, nblocks)
    column_part, outgoing = split_rows(placed, column, row_parts, col_parts, tile)
    column_full = lax.all_gather(column_part, "row", axis=1, tiled=True)
    arrived = lax.all_to_all(outgoing, "row", split_axis=1, concat_axis=1, tiled=True)
    own_all = arrived.reshape(supers, width, tile)
    summed = lax.psum_scatter(
        make_term(inverse_block, column_full), "col", scatter_dimension=0, tiled=True
    )
    for position in range(supers):
        link = None if position == 0 else coupling[position - 1]
        current, partial_value = local_step(
            summed[:, position, :],
            own_all[position],
            previous,
            link,
            diag_inverse[position],
            column,
            row_first,
            rows_total,
        )
        column_list.append(current)
        partial_list.append(partial_value)
        previous = current
    diag_list = []
    totals = lax.psum(jnp.stack(partial_list), ("row", "col"))
    chain_prev = None
    for position in range(supers):
        link = None if position == 0 else coupling[position - 1]
        diag_now = chain_diag(totals[position], chain_prev, link)
        diag_list.append(lax.dynamic_slice_in_dim(diag_now, column * diag_cols, diag_cols, 1))
        chain_prev = diag_now
    diagonals = jnp.stack(diag_list)
    return (jnp.stack(column_list), diagonals)


def swap(value, axis, bit, parts):
    return lax.ppermute(value, axis, [(i, i ^ bit) for i in range(parts)])


def across(value):
    return lax.ppermute(value, "col", [(0, 1), (1, 0)])


def after(values, *events):
    return lax.optimization_barrier((values, events))[0]


def split2(value):
    high = value.astype(bf16)
    return high, (value - high.astype(f32)).astype(bf16)


def nn(a, b):
    return lax.dot_general(a, b, (((1,), (0,)), ((), ())), preferred_element_type=f32)


def nt(a, b):
    return lax.dot_general(a, b, (((1,), (1,)), ((), ())), preferred_element_type=f32)


def nn2(pair, b):
    return nn(pair[0], b) + nn(pair[1], b)


def nn2r(a, pair):
    return nn(a, pair[0]) + nn(a, pair[1])


def owner_of(row, wave, count, j, i):
    return 4 * ((row // 4) ^ (wave * count + i)) + ((row % 4) ^ j)


def place_kernel(dims, *refs):
    supers, width, rows, span, part = dims
    occ_ref, block_ref = refs[:2]
    f_refs, pt = refs[2:6], refs[6]
    row, col = lax.axis_index("row"), lax.axis_index("col")
    per_side = span // 128
    for side in range(2):
        target = col if side == 0 else 1 - col
        for s in range(supers):
            for b in range(per_side):
                lanes = pl.ds(pl.multiple_of(block_ref[s, target * per_side + b] * 128, 128), 128)
                for wave in range(2):
                    source = f_refs[2 * side + wave]
                    for j in range(4):
                        for i in range(source.shape[1]):
                            first = owner_of(row, wave, source.shape[1], j, i) * part
                            pt[s, pl.ds(pl.multiple_of(first, part), part), lanes] = source[
                                j, i, s * part : (s + 1) * part, b * 128 : (b + 1) * 128
                            ]
    for s in range(supers):
        for b in range(2 * per_side):

            @pl.when(occ_ref[s, b] == 0)
            def _():
                lanes = pl.ds(pl.multiple_of(block_ref[s, b] * 128, 128), 128)
                pt[s, :, lanes] = jnp.zeros((width, 128), bf16)


def load_rows(wave, skip, span, col, row, z_refs, z_all, sem):
    half_rows = z_all.shape[0]
    copies = []
    for side in range(2):
        target = col if side == 0 else 1 - col
        source = z_refs[side]
        local_rows = source.shape[2] - skip
        for j in range(4):
            for i in range(source.shape[1]):
                place = owner_of(row, wave, source.shape[1], j, i) % (half_rows // local_rows)
                copies.append(
                    pltpu.make_async_copy(
                        source.at[j, i, pl.ds(skip, local_rows)],
                        z_all.at[
                            pl.ds(pl.multiple_of(place * local_rows, local_rows), local_rows),
                            pl.ds(pl.multiple_of(target * span, span), span),
                        ],
                        sem,
                    )
                )
    for copy in copies:
        copy.start()
    for copy in copies:
        copy.wait()


def halves(col, half_w):
    return pl.ds(pl.multiple_of(col * half_w, half_w), half_w)


def lanes_of(row, wave, local_rows, half_rows, count):
    half = owner_of(row, wave, count, 0, 0) // (half_rows // local_rows)
    return pl.ds(pl.multiple_of(half * half_rows, half_rows), half_rows)


def row_products(pt, link_ref, zm, c_rows, held, tmp):
    c0h, c0l, p1h, p1l, c1h, c1l, c2h, c2l = held
    cols0 = split2(-nt(zm, pt[0]))
    c0h[...], c0l[...] = cols0
    tmp[...] = nn2(cols0, link_ref[0])
    p1h[...], p1l[...] = split2(tmp[...])
    tmp[...] += nt(zm, pt[1])
    cols1 = split2(-tmp[...])
    c1h[...], c1l[...] = cols1
    cols2 = -(nt(zm, pt[2, c_rows, :]) + nn2(cols1, link_ref[1, :, c_rows]))
    c2h[...], c2l[...] = split2(cols2)


def rows_kernel(dims, skip, *refs):
    width, span = dims
    pt, z_refs, link_ref = refs[0], refs[1:3], refs[3]
    held, z_own, z_all, tmp, sem = refs[4:12], refs[12], refs[13], refs[14], refs[15]
    col, row = lax.axis_index("col"), lax.axis_index("row")
    load_rows(0, skip, span, col, row, z_refs, z_all, sem)
    row_products(pt, link_ref, z_all[...], halves(col, width // 2), held, tmp)
    local_rows = z_own.shape[0]
    place = row % (z_all.shape[0] // local_rows)
    z_own[...] = z_all[pl.ds(pl.multiple_of(place * local_rows, local_rows), local_rows), :]


def early_sums_kernel(count, *refs):
    pt, c0h, c0l, p1h, p1l, c1h, c1l, z_own, link_ref = refs[:9]
    s0, u1, col_out = refs[9:]
    col, row = lax.axis_index("col"), lax.axis_index("row")
    local_rows, half_rows = z_own.shape[0], c0h.shape[0]
    lanes = lanes_of(row, 0, local_rows, half_rows, count)
    s0[...] = nn2r(pt[0, :, lanes], (c0h[...], c0l[...]))
    u1[...] = nn2r(pt[1, :, lanes], (p1h[...], p1l[...]))
    tile = col_out.shape[1]
    place = row % (half_rows // local_rows)
    own = pl.ds(pl.multiple_of(place * local_rows, local_rows), local_rows)
    cols1 = (c1h[own, :], c1l[own, :])
    mine = [
        c0h[own, :].astype(f32) + c0l[own, :].astype(f32),
        cols1[0].astype(f32) + cols1[1].astype(f32),
        -(nt(z_own[...], pt[2]) + nn2(cols1, link_ref[1])),
    ]
    for s, value in enumerate(mine):
        col_out[s] = jnp.where(col == 0, value[:tile], value[tile:])


def late_sums_kernel(count, local_rows, *refs):
    pt, c1h, c1l, c2h, c2l = refs[:5]
    s1, n2, s2 = refs[5:]
    col, row = lax.axis_index("col"), lax.axis_index("row")
    half_rows, half_w = c2h.shape
    lanes = lanes_of(row, 0, local_rows, half_rows, count)
    s1[...] = nn2r(pt[1, :, lanes], (c1h[...], c1l[...]))
    n2[...] = nn2r(pt[2, halves(col, half_w), lanes], (c1h[...], c1l[...]))
    s2[...] = nn2r(pt[2, :, lanes], (c2h[...], c2l[...]))


def last_kernel(dims, rows, *refs):
    width, span = dims
    pt, z_refs, link_ref, diag_ref, diag_other_ref = refs[0], refs[1:3], refs[3], refs[4], refs[5]
    before, diag_out, held, z_all, tmp, sem = refs[6:11], refs[11], refs[12:20], refs[20], refs[21], refs[22]
    col, row = lax.axis_index("col"), lax.axis_index("row")
    half_w = width // 2
    half_rows = z_all.shape[0]
    c_rows = halves(col, half_w)
    load_rows(1, 0, span, col, row, z_refs, z_all, sem)
    row_products(pt, link_ref, z_all[...], c_rows, held, tmp)
    c0h, c0l, p1h, p1l, c1h, c1l, c2h, c2l = held
    lanes = lanes_of(row, 1, z_refs[0].shape[2], half_rows, z_refs[0].shape[1])
    left = pt[1, :, lanes]
    s0 = before[0][...] + nn2r(pt[0, :, lanes], (c0h[...], c0l[...]))
    u1 = before[1][...] + nn2r(left, (p1h[...], p1l[...]))
    s1 = before[2][...] + nn2r(left, (c1h[...], c1l[...]))
    n2 = before[3][...] + nn2r(pt[2, c_rows, lanes], (c1h[...], c1l[...]))
    s2 = before[4][...] + nn2r(pt[2, :, lanes], (c2h[...], c2l[...]))
    scale = 1.0 / rows

    def whole(s):
        mine, theirs = diag_ref[s], diag_other_ref[s]
        return jnp.concatenate([jnp.where(col == 0, mine, theirs), jnp.where(col == 0, theirs, mine)], axis=1)

    d0 = whole(0) - s0 * scale
    i1 = s1 - u1.T
    d1 = whole(1) - i1 * scale + nn2r(link_ref[0].T, split2(nn2(split2(d0), link_ref[0])))
    i2 = s2 - nn2(split2(n2), link_ref[1]).T
    d2 = diag_ref[2] - i2 * scale + nn2r(link_ref[1].T, split2(nn2(split2(d1), link_ref[1, :, c_rows])))
    diag_out[0] = jnp.where(col == 0, d0[:, :half_w], d0[:, half_w:])
    diag_out[1] = jnp.where(col == 0, d1[:, :half_w], d1[:, half_w:])
    diag_out[2] = d2


def replicated_plan(inverse_block, factor_cols, occupancy, row_block, coupling, diag_inverse):
    row_parts = lax.axis_size("row")
    supers, span, part = factor_cols.shape
    width = part * row_parts
    local_rows = inverse_block.shape[0]
    rows = local_rows * row_parts
    count = row_parts // 8
    any_spec = pl.BlockSpec(memory_space=pl.ANY)
    smem = pl.BlockSpec(memory_space=pltpu.SMEM)
    vmem = pl.BlockSpec(memory_space=pltpu.VMEM)
    shape = jax.ShapeDtypeStruct

    def call(body, name, flops, **kwargs):
        return pl.pallas_call(
            body,
            compiler_params=pltpu.CompilerParams(vmem_limit_bytes=VMEM_LIMIT),
            cost_estimate=pl.CostEstimate(flops=flops, bytes_accessed=8 * 2**20, transcendentals=0),
            name=name,
            **kwargs,
        )

    outer = row_parts // 4
    x = lambda value: swap(value, "row", 1, row_parts)
    y = lambda value: swap(value, "row", 2, row_parts)
    line = lambda value, k: swap(value, "row", 4 * k, row_parts)

    def far(over_x, over_y, i):
        return x(over_y) if i % 2 == 0 else y(over_x)

    def late_wave(parts, *events):
        own = after(jnp.stack(parts), *events)
        return own, x(own), y(own)

    f_own = jnp.transpose(factor_cols, (0, 2, 1)).reshape(supers * part, span)
    f_late = [line(f_own, k) for k in range(count, outer)]
    own = jnp.concatenate([f_own, inverse_block], axis=0)
    early = []
    for k in range(count):
        value = own if k == 0 else line(own, k)
        value = after(value, *early[-1][1:3]) if k else value
        over_x, over_y = x(value), y(value)
        early.append([value, over_x, over_y, far(over_x, over_y, k)])
    first = jnp.stack([jnp.stack([p[j] for p in early]) for j in range(4)])
    first_other = across(first)
    block = after(inverse_block, *f_late, *early[-1][1:3])
    z_late = [line(block, k) for k in range(count, outer)]
    f_b, f_bx, f_by = late_wave(f_late, *early[-1][1:3], early[0][3])
    f_bx, f_by = after((f_bx, f_by), *z_late)
    f_far = jnp.stack([far(f_bx[i], f_by[i], i) for i in range(count)])
    f_last = jnp.stack([f_b, f_bx, f_by, f_far])
    f_last_other = across(f_last)
    z_b, z_bx, z_by = late_wave(z_late, f_bx, f_by)
    diag_other = across(diag_inverse)

    pt = call(
        functools.partial(place_kernel, (supers, width, rows, span, part)),
        "place", 2 * 10**9,
        out_shape=shape((supers, width, rows), bf16),
        in_specs=[smem] * 2 + [vmem] * 4,
        out_specs=vmem,
    )(occupancy, row_block, first, f_last, first_other, f_last_other)

    dims = (width, span)
    half_rows, half_w = rows // 2, width // 2
    held_shapes = [(half_rows, width)] * 6 + [(half_rows, half_w)] * 2
    work = [pltpu.VMEM((half_rows, 2 * span), bf16), pltpu.VMEM((half_rows, width), f32), pltpu.SemaphoreType.DMA]
    *held, z_own = call(
        functools.partial(rows_kernel, dims, supers * part),
        "own_half_rows", 4 * 10**9,
        out_shape=tuple(shape(v, bf16) for v in held_shapes) + (shape((local_rows, 2 * span), bf16),),
        in_specs=[vmem] + [any_spec] * 2 + [vmem],
        out_specs=(vmem,) * 9,
        scratch_shapes=work,
    )(pt, first, first_other, coupling)
    z_bx, z_by, *held = after((z_bx, z_by, *held), held[0])
    z_far = jnp.stack([far(z_bx[i], z_by[i], i) for i in range(count)])
    c0h, c0l, p1h, p1l, c1h, c1l, c2h, c2l = held
    s0, u1, columns = call(
        functools.partial(early_sums_kernel, count),
        "early_sums", 3 * 10**9,
        out_shape=(shape((width, width), f32),) * 2 + (shape((supers, local_rows // 2, width), f32),),
        in_specs=[vmem] * 9,
        out_specs=(vmem,) * 3,
    )(pt, c0h, c0l, p1h, p1l, c1h, c1l, z_own, coupling)
    z_far, c1h = after((z_far, c1h), s0)
    z_last = jnp.stack([z_b, z_bx, z_by, z_far])
    z_last_other = across(z_last)
    s1, n2, s2 = call(
        functools.partial(late_sums_kernel, count, local_rows),
        "late_sums", 2 * 10**9,
        out_shape=(shape((width, width), f32), shape((half_w, width), f32), shape((width, half_w), f32)),
        in_specs=[vmem] * 5,
        out_specs=(vmem,) * 3,
    )(pt, c1h, c1l, c2h, c2l)
    sums = [s0, u1, s1, n2, s2]
    diagonals = call(
        functools.partial(last_kernel, dims, rows),
        "other_half", 12 * 10**9,
        out_shape=shape((supers, width, half_w), f32),
        in_specs=[vmem] + [any_spec] * 2 + [vmem] * 8,
        out_specs=vmem,
        scratch_shapes=[pltpu.VMEM(v, bf16) for v in held_shapes] + work,
    )(pt, z_last, z_last_other, coupling, diag_inverse, diag_other, *sums)
    return columns, diagonals


def solution(mesh):
    row_parts, col_parts = mesh.shape["row"], mesh.shape["col"]
    in_specs = (P("row", "col"), P(None, "col", "row"), P(), P(), P(), P(None, None, "col"))
    out_specs = (P(None, ("row", "col"), None), P(None, None, "col"))

    def per_device(inverse_block, factor_cols, *rest):
        held = (inverse_block.size + factor_cols.size) * 2 * row_parts * col_parts
        fits = held <= REPLICATE_BYTES and col_parts == 2 and row_parts in (8, 16)
        plan = replicated_plan if fits else grid_plan
        return plan(inverse_block, factor_cols, *rest)

    return jax.shard_map(
        per_device, mesh=mesh, in_specs=in_specs, out_specs=out_specs, check_vma=False
    )
```

```python
import functools

import jax
import jax.numpy as jnp
from jax import lax
from jax.experimental import pallas as pl
from jax.experimental.pallas import tpu as pltpu
from jax.sharding import PartitionSpec as P

highest = lax.Precision.HIGHEST
f32 = jnp.float32
bf16 = jnp.bfloat16

REPLICATE_BYTES = 12 * 2**20
VMEM_LIMIT = 36 * 2**20


def routed(gathered, occupancy, row_block, nblocks):
    count = gathered.shape[0]
    width_part = gathered.shape[1] // (nblocks * 128)
    blocks = gathered.reshape(count, nblocks, 128, width_part)
    levels = lax.broadcasted_iota(jnp.int32, (count, nblocks, nblocks), 1)
    picks = ((row_block[:, None, :] == levels) & (occupancy[:, None, :] > 0)).astype(jnp.bfloat16)
    placed = jnp.einsum("kqb,kbtx->kxqt", picks, blocks, preferred_element_type=jnp.float32)
    return placed.astype(jnp.bfloat16).reshape(count, width_part, nblocks * 128)


def split_rows(placed, column, row_parts, col_parts, tile):
    count, width_part, total = placed.shape
    span = total // col_parts
    column_part = lax.dynamic_slice_in_dim(placed, column * span, span, 2)
    grid = placed.reshape(count, width_part, row_parts, col_parts, tile)
    mine = lax.dynamic_index_in_dim(grid, column, 3, keepdims=False)
    return (column_part, jnp.transpose(mine, (0, 2, 1, 3)))


def make_term(inverse_block, column_full):
    return lax.dot_general(
        inverse_block, column_full, (((1,), (2,)), ((), ())), preferred_element_type=jnp.float32
    )


def local_step(summed, own_rows, previous, link, diag_part, column, row_first, rows_total):
    if link is None:
        coupled = jnp.zeros_like(summed)
    else:
        coupled = jnp.dot(previous, link.astype(jnp.float32), precision=highest)
    current = -(summed + coupled)
    own = own_rows.astype(jnp.float32)
    inner = jnp.dot(own, current, precision=highest) - jnp.dot(coupled.T, own.T, precision=highest)
    width = summed.shape[1]
    diag_cols = diag_part.shape[1]
    embedded = lax.dynamic_update_slice(
        jnp.zeros((width, width), jnp.float32), diag_part, (0, column * diag_cols)
    )
    return (current, row_first * embedded - inner / rows_total)


def chain_diag(total, chain_prev, link):
    if link is None:
        return total
    link_wide = link.astype(jnp.float32)
    return total + jnp.dot(
        link_wide.T, jnp.dot(chain_prev, link_wide, precision=highest), precision=highest
    )


def grid_plan(inverse_block, factor_cols, occupancy, row_block, coupling, diag_inverse):
    column = lax.axis_index("col")
    row_first = (lax.axis_index("row") == 0).astype(jnp.float32)
    row_parts = lax.axis_size("row")
    col_parts = lax.axis_size("col")
    local_rows = inverse_block.shape[0]
    rows_total = local_rows * row_parts
    supers, span, width_part = factor_cols.shape
    width = width_part * row_parts
    tile = local_rows // col_parts
    nblocks = occupancy.shape[1]
    diag_cols = diag_inverse.shape[2]
    flat = factor_cols.reshape(supers, span * width_part)
    column_list = []
    partial_list = []
    previous = None
    gathered = lax.all_gather(flat, "col", axis=1, tiled=True)
    placed = routed(gathered, occupancy, row_block, nblocks)
    column_part, outgoing = split_rows(placed, column, row_parts, col_parts, tile)
    column_full = lax.all_gather(column_part, "row", axis=1, tiled=True)
    arrived = lax.all_to_all(outgoing, "row", split_axis=1, concat_axis=1, tiled=True)
    own_all = arrived.reshape(supers, width, tile)
    summed = lax.psum_scatter(
        make_term(inverse_block, column_full), "col", scatter_dimension=0, tiled=True
    )
    for position in range(supers):
        link = None if position == 0 else coupling[position - 1]
        current, partial_value = local_step(
            summed[:, position, :],
            own_all[position],
            previous,
            link,
            diag_inverse[position],
            column,
            row_first,
            rows_total,
        )
        column_list.append(current)
        partial_list.append(partial_value)
        previous = current
    diag_list = []
    totals = lax.psum(jnp.stack(partial_list), ("row", "col"))
    chain_prev = None
    for position in range(supers):
        link = None if position == 0 else coupling[position - 1]
        diag_now = chain_diag(totals[position], chain_prev, link)
        diag_list.append(lax.dynamic_slice_in_dim(diag_now, column * diag_cols, diag_cols, 1))
        chain_prev = diag_now
    diagonals = jnp.stack(diag_list)
    return (jnp.stack(column_list), diagonals)


def swap(value, axis, bit, parts):
    return lax.ppermute(value, axis, [(i, i ^ bit) for i in range(parts)])


def across(value):
    return lax.ppermute(value, "col", [(0, 1), (1, 0)])


def after(values, *events):
    return lax.optimization_barrier((values, events))[0]


def split2(value):
    high = value.astype(bf16)
    return high, (value - high.astype(f32)).astype(bf16)


def nn(a, b):
    return lax.dot_general(a, b, (((1,), (0,)), ((), ())), preferred_element_type=f32)


def nt(a, b):
    return lax.dot_general(a, b, (((1,), (1,)), ((), ())), preferred_element_type=f32)


def nn2(pair, b):
    return nn(pair[0], b) + nn(pair[1], b)


def nn2r(a, pair):
    return nn(a, pair[0]) + nn(a, pair[1])


def owner_of(row, wave, count, j, i):
    return 4 * ((row // 4) ^ (wave * count + i)) + ((row % 4) ^ j)


def place_kernel(dims, *refs):
    supers, width, rows, span, part = dims
    occ_ref, block_ref = refs[:2]
    f_refs, pt = refs[2:6], refs[6]
    row, col = lax.axis_index("row"), lax.axis_index("col")
    per_side = span // 128
    for side in range(2):
        target = col if side == 0 else 1 - col
        for s in range(supers):
            for b in range(per_side):
                lanes = pl.ds(pl.multiple_of(block_ref[s, target * per_side + b] * 128, 128), 128)
                for wave in range(2):
                    source = f_refs[2 * side + wave]
                    for j in range(4):
                        for i in range(source.shape[1]):
                            first = owner_of(row, wave, source.shape[1], j, i) * part
                            pt[s, pl.ds(pl.multiple_of(first, part), part), lanes] = source[
                                j, i, s * part : (s + 1) * part, b * 128 : (b + 1) * 128
                            ]
    for s in range(supers):
        for b in range(2 * per_side):

            @pl.when(occ_ref[s, b] == 0)
            def _():
                lanes = pl.ds(pl.multiple_of(block_ref[s, b] * 128, 128), 128)
                pt[s, :, lanes] = jnp.zeros((width, 128), bf16)


def load_rows(wave, skip, span, col, row, z_refs, z_all, sem):
    half_rows = z_all.shape[0]
    copies = []
    for side in range(2):
        target = col if side == 0 else 1 - col
        source = z_refs[side]
        local_rows = source.shape[2] - skip
        for j in range(4):
            for i in range(source.shape[1]):
                place = owner_of(row, wave, source.shape[1], j, i) % (half_rows // local_rows)
                copies.append(
                    pltpu.make_async_copy(
                        source.at[j, i, pl.ds(skip, local_rows)],
                        z_all.at[
                            pl.ds(pl.multiple_of(place * local_rows, local_rows), local_rows),
                            pl.ds(pl.multiple_of(target * span, span), span),
                        ],
                        sem,
                    )
                )
    for copy in copies:
        copy.start()
    for copy in copies:
        copy.wait()


def halves(col, half_w):
    return pl.ds(pl.multiple_of(col * half_w, half_w), half_w)


def lanes_of(row, wave, local_rows, half_rows, count):
    half = owner_of(row, wave, count, 0, 0) // (half_rows // local_rows)
    return pl.ds(pl.multiple_of(half * half_rows, half_rows), half_rows)


def row_products(pt, link_ref, zm, c_rows, held, tmp):
    c0h, c0l, p1h, p1l, c1h, c1l, c2h, c2l = held
    cols0 = split2(-nt(zm, pt[0]))
    c0h[...], c0l[...] = cols0
    tmp[...] = nn2(cols0, link_ref[0])
    p1h[...], p1l[...] = split2(tmp[...])
    tmp[...] += nt(zm, pt[1])
    cols1 = split2(-tmp[...])
    c1h[...], c1l[...] = cols1
    cols2 = -(nt(zm, pt[2, c_rows, :]) + nn2(cols1, link_ref[1, :, c_rows]))
    c2h[...], c2l[...] = split2(cols2)


def rows_kernel(dims, skip, *refs):
    width, span = dims
    pt, z_refs, link_ref = refs[0], refs[1:3], refs[3]
    held, z_own, z_all, tmp, sem = refs[4:12], refs[12], refs[13], refs[14], refs[15]
    col, row = lax.axis_index("col"), lax.axis_index("row")
    load_rows(0, skip, span, col, row, z_refs, z_all, sem)
    row_products(pt, link_ref, z_all[...], halves(col, width // 2), held, tmp)
    local_rows = z_own.shape[0]
    place = row % (z_all.shape[0] // local_rows)
    z_own[...] = z_all[pl.ds(pl.multiple_of(place * local_rows, local_rows), local_rows), :]


def early_sums_kernel(count, *refs):
    pt, c0h, c0l, p1h, p1l, c1h, c1l, z_own, link_ref = refs[:9]
    s0, u1, col_out = refs[9:]
    col, row = lax.axis_index("col"), lax.axis_index("row")
    local_rows, half_rows = z_own.shape[0], c0h.shape[0]
    lanes = lanes_of(row, 0, local_rows, half_rows, count)
    s0[...] = nn2r(pt[0, :, lanes], (c0h[...], c0l[...]))
    u1[...] = nn2r(pt[1, :, lanes], (p1h[...], p1l[...]))
    tile = col_out.shape[1]
    place = row % (half_rows // local_rows)
    own = pl.ds(pl.multiple_of(place * local_rows, local_rows), local_rows)
    cols1 = (c1h[own, :], c1l[own, :])
    mine = [
        c0h[own, :].astype(f32) + c0l[own, :].astype(f32),
        cols1[0].astype(f32) + cols1[1].astype(f32),
        -(nt(z_own[...], pt[2]) + nn2(cols1, link_ref[1])),
    ]
    for s, value in enumerate(mine):
        col_out[s] = jnp.where(col == 0, value[:tile], value[tile:])


def late_sums_kernel(count, local_rows, *refs):
    pt, c1h, c1l, c2h, c2l = refs[:5]
    s1, n2, s2 = refs[5:]
    col, row = lax.axis_index("col"), lax.axis_index("row")
    half_rows, half_w = c2h.shape
    lanes = lanes_of(row, 0, local_rows, half_rows, count)
    s1[...] = nn2r(pt[1, :, lanes], (c1h[...], c1l[...]))
    n2[...] = nn2r(pt[2, halves(col, half_w), lanes], (c1h[...], c1l[...]))
    s2[...] = nn2r(pt[2, :, lanes], (c2h[...], c2l[...]))


def last_kernel(dims, rows, *refs):
    width, span = dims
    pt, z_refs, link_ref, diag_ref, diag_other_ref = refs[0], refs[1:3], refs[3], refs[4], refs[5]
    before, diag_out, held, z_all, tmp, sem = refs[6:11], refs[11], refs[12:20], refs[20], refs[21], refs[22]
    col, row = lax.axis_index("col"), lax.axis_index("row")
    half_w = width // 2
    half_rows = z_all.shape[0]
    c_rows = halves(col, half_w)
    load_rows(1, 0, span, col, row, z_refs, z_all, sem)
    row_products(pt, link_ref, z_all[...], c_rows, held, tmp)
    c0h, c0l, p1h, p1l, c1h, c1l, c2h, c2l = held
    lanes = lanes_of(row, 1, z_refs[0].shape[2], half_rows, z_refs[0].shape[1])
    left = pt[1, :, lanes]
    s0 = before[0][...] + nn2r(pt[0, :, lanes], (c0h[...], c0l[...]))
    u1 = before[1][...] + nn2r(left, (p1h[...], p1l[...]))
    s1 = before[2][...] + nn2r(left, (c1h[...], c1l[...]))
    n2 = before[3][...] + nn2r(pt[2, c_rows, lanes], (c1h[...], c1l[...]))
    s2 = before[4][...] + nn2r(pt[2, :, lanes], (c2h[...], c2l[...]))
    scale = 1.0 / rows

    def whole(s):
        mine, theirs = diag_ref[s], diag_other_ref[s]
        return jnp.concatenate([jnp.where(col == 0, mine, theirs), jnp.where(col == 0, theirs, mine)], axis=1)

    d0 = whole(0) - s0 * scale
    i1 = s1 - u1.T
    d1 = whole(1) - i1 * scale + nn2r(link_ref[0].T, split2(nn2(split2(d0), link_ref[0])))
    i2 = s2 - nn2(split2(n2), link_ref[1]).T
    d2 = diag_ref[2] - i2 * scale + nn2r(link_ref[1].T, split2(nn2(split2(d1), link_ref[1, :, c_rows])))
    diag_out[0] = jnp.where(col == 0, d0[:, :half_w], d0[:, half_w:])
    diag_out[1] = jnp.where(col == 0, d1[:, :half_w], d1[:, half_w:])
    diag_out[2] = d2


def replicated_plan(inverse_block, factor_cols, occupancy, row_block, coupling, diag_inverse):
    row_parts = lax.axis_size("row")
    supers, span, part = factor_cols.shape
    width = part * row_parts
    local_rows = inverse_block.shape[0]
    rows = local_rows * row_parts
    count = row_parts // 8
    any_spec = pl.BlockSpec(memory_space=pl.ANY)
    smem = pl.BlockSpec(memory_space=pltpu.SMEM)
    vmem = pl.BlockSpec(memory_space=pltpu.VMEM)
    shape = jax.ShapeDtypeStruct

    def call(body, name, flops, **kwargs):
        return pl.pallas_call(
            body,
            compiler_params=pltpu.CompilerParams(vmem_limit_bytes=VMEM_LIMIT),
            cost_estimate=pl.CostEstimate(flops=flops, bytes_accessed=8 * 2**20, transcendentals=0),
            name=name,
            **kwargs,
        )

    x = lambda value: swap(value, "row", 1, row_parts)
    y = lambda value: swap(value, "row", 2, row_parts)
    line = lambda value, k: swap(value, "row", 4 * k, row_parts)

    def far(over_x, over_y, i):
        return x(over_y) if i % 2 == 0 else y(over_x)

    f_rows = supers * part
    own = jnp.concatenate(
        [jnp.transpose(factor_cols, (0, 2, 1)).reshape(f_rows, span), inverse_block], axis=0
    )
    early = []
    for k in range(count):
        value = own if k == 0 else line(own, k)
        value = after(value, *early[-1][1:3]) if k else value
        over_x, over_y = x(value), y(value)
        early.append([value, over_x, over_y, far(over_x, over_y, k)])
    first = jnp.stack([jnp.stack([p[j] for p in early]) for j in range(4)])
    first_other = across(first)
    f_late = line(jnp.stack([p[0][:f_rows] for p in early]), count)
    z_near = after(jnp.stack([p[0][f_rows:] for p in early]), f_late, *early[-1][1:3])
    z_late = line(z_near, count)
    f_b = after(f_late, *early[-1][1:3], early[0][3])
    f_bx, f_by = x(f_b), y(f_b)
    f_bx, f_by = after((f_bx, f_by), z_late)
    f_far = jnp.stack([far(f_bx[i], f_by[i], i) for i in range(count)])
    f_last = jnp.stack([f_b, f_bx, f_by, f_far])
    f_last_other = across(f_last)
    z_b = after(z_late, f_bx, f_by)
    z_bx, z_by = x(z_b), y(z_b)
    diag_other = across(diag_inverse)

    pt = call(
        functools.partial(place_kernel, (supers, width, rows, span, part)),
        "place", 2 * 10**9,
        out_shape=shape((supers, width, rows), bf16),
        in_specs=[smem] * 2 + [vmem] * 4,
        out_specs=vmem,
    )(occupancy, row_block, first, f_last, first_other, f_last_other)

    dims = (width, span)
    half_rows, half_w = rows // 2, width // 2
    held_shapes = [(half_rows, width)] * 6 + [(half_rows, half_w)] * 2
    work = [pltpu.VMEM((half_rows, 2 * span), bf16), pltpu.VMEM((half_rows, width), f32), pltpu.SemaphoreType.DMA]
    *held, z_own = call(
        functools.partial(rows_kernel, dims, supers * part),
        "own_half_rows", 4 * 10**9,
        out_shape=tuple(shape(v, bf16) for v in held_shapes) + (shape((local_rows, 2 * span), bf16),),
        in_specs=[vmem] + [any_spec] * 2 + [vmem],
        out_specs=(vmem,) * 9,
        scratch_shapes=work,
    )(pt, first, first_other, coupling)
    z_bx, z_by, *held = after((z_bx, z_by, *held), held[0])
    z_far = jnp.stack([far(z_bx[i], z_by[i], i) for i in range(count)])
    c0h, c0l, p1h, p1l, c1h, c1l, c2h, c2l = held
    s0, u1, columns = call(
        functools.partial(early_sums_kernel, count),
        "early_sums", 3 * 10**9,
        out_shape=(shape((width, width), f32),) * 2 + (shape((supers, local_rows // 2, width), f32),),
        in_specs=[vmem] * 9,
        out_specs=(vmem,) * 3,
    )(pt, c0h, c0l, p1h, p1l, c1h, c1l, z_own, coupling)
    z_far, c1h = after((z_far, c1h), s0)
    z_last = jnp.stack([z_b, z_bx, z_by, z_far])
    z_last_other = across(z_last)
    s1, n2, s2 = call(
        functools.partial(late_sums_kernel, count, local_rows),
        "late_sums", 2 * 10**9,
        out_shape=(shape((width, width), f32), shape((half_w, width), f32), shape((width, half_w), f32)),
        in_specs=[vmem] * 5,
        out_specs=(vmem,) * 3,
    )(pt, c1h, c1l, c2h, c2l)
    sums = [s0, u1, s1, n2, s2]
    diagonals = call(
        functools.partial(last_kernel, dims, rows),
        "other_half", 12 * 10**9,
        out_shape=shape((supers, width, half_w), f32),
        in_specs=[vmem] + [any_spec] * 2 + [vmem] * 8,
        out_specs=vmem,
        scratch_shapes=[pltpu.VMEM(v, bf16) for v in held_shapes] + work,
    )(pt, z_last, z_last_other, coupling, diag_inverse, diag_other, *sums)
    return columns, diagonals


def solution(mesh):
    row_parts, col_parts = mesh.shape["row"], mesh.shape["col"]
    in_specs = (P("row", "col"), P(None, "col", "row"), P(), P(), P(), P(None, None, "col"))
    out_specs = (P(None, ("row", "col"), None), P(None, None, "col"))

    def per_device(inverse_block, factor_cols, *rest):
        held = (inverse_block.size + factor_cols.size) * 2 * row_parts * col_parts
        fits = held <= REPLICATE_BYTES and col_parts == 2 and row_parts in (8, 16)
        plan = replicated_plan if fits else grid_plan
        return plan(inverse_block, factor_cols, *rest)

    return jax.shard_map(
        per_device, mesh=mesh, in_specs=in_specs, out_specs=out_specs, check_vma=False
    )
```

```python
import functools

import jax
import jax.numpy as jnp
from jax import lax
from jax.experimental import pallas as pl
from jax.experimental.pallas import tpu as pltpu
from jax.sharding import PartitionSpec as P

highest = lax.Precision.HIGHEST
f32 = jnp.float32
bf16 = jnp.bfloat16

REPLICATE_BYTES = 12 * 2**20
VMEM_LIMIT = 36 * 2**20


def routed(gathered, occupancy, row_block, nblocks):
    count = gathered.shape[0]
    width_part = gathered.shape[1] // (nblocks * 128)
    blocks = gathered.reshape(count, nblocks, 128, width_part)
    levels = lax.broadcasted_iota(jnp.int32, (count, nblocks, nblocks), 1)
    picks = ((row_block[:, None, :] == levels) & (occupancy[:, None, :] > 0)).astype(jnp.bfloat16)
    placed = jnp.einsum("kqb,kbtx->kxqt", picks, blocks, preferred_element_type=jnp.float32)
    return placed.astype(jnp.bfloat16).reshape(count, width_part, nblocks * 128)


def split_rows(placed, column, row_parts, col_parts, tile):
    count, width_part, total = placed.shape
    span = total // col_parts
    column_part = lax.dynamic_slice_in_dim(placed, column * span, span, 2)
    grid = placed.reshape(count, width_part, row_parts, col_parts, tile)
    mine = lax.dynamic_index_in_dim(grid, column, 3, keepdims=False)
    return (column_part, jnp.transpose(mine, (0, 2, 1, 3)))


def make_term(inverse_block, column_full):
    return lax.dot_general(
        inverse_block, column_full, (((1,), (2,)), ((), ())), preferred_element_type=jnp.float32
    )


def local_step(summed, own_rows, previous, link, diag_part, column, row_first, rows_total):
    if link is None:
        coupled = jnp.zeros_like(summed)
    else:
        coupled = jnp.dot(previous, link.astype(jnp.float32), precision=highest)
    current = -(summed + coupled)
    own = own_rows.astype(jnp.float32)
    inner = jnp.dot(own, current, precision=highest) - jnp.dot(coupled.T, own.T, precision=highest)
    width = summed.shape[1]
    diag_cols = diag_part.shape[1]
    embedded = lax.dynamic_update_slice(
        jnp.zeros((width, width), jnp.float32), diag_part, (0, column * diag_cols)
    )
    return (current, row_first * embedded - inner / rows_total)


def chain_diag(total, chain_prev, link):
    if link is None:
        return total
    link_wide = link.astype(jnp.float32)
    return total + jnp.dot(
        link_wide.T, jnp.dot(chain_prev, link_wide, precision=highest), precision=highest
    )


def grid_plan(inverse_block, factor_cols, occupancy, row_block, coupling, diag_inverse):
    column = lax.axis_index("col")
    row_first = (lax.axis_index("row") == 0).astype(jnp.float32)
    row_parts = lax.axis_size("row")
    col_parts = lax.axis_size("col")
    local_rows = inverse_block.shape[0]
    rows_total = local_rows * row_parts
    supers, span, width_part = factor_cols.shape
    width = width_part * row_parts
    tile = local_rows // col_parts
    nblocks = occupancy.shape[1]
    diag_cols = diag_inverse.shape[2]
    flat = factor_cols.reshape(supers, span * width_part)
    column_list = []
    partial_list = []
    previous = None
    gathered = lax.all_gather(flat, "col", axis=1, tiled=True)
    placed = routed(gathered, occupancy, row_block, nblocks)
    column_part, outgoing = split_rows(placed, column, row_parts, col_parts, tile)
    column_full = lax.all_gather(column_part, "row", axis=1, tiled=True)
    arrived = lax.all_to_all(outgoing, "row", split_axis=1, concat_axis=1, tiled=True)
    own_all = arrived.reshape(supers, width, tile)
    summed = lax.psum_scatter(
        make_term(inverse_block, column_full), "col", scatter_dimension=0, tiled=True
    )
    for position in range(supers):
        link = None if position == 0 else coupling[position - 1]
        current, partial_value = local_step(
            summed[:, position, :],
            own_all[position],
            previous,
            link,
            diag_inverse[position],
            column,
            row_first,
            rows_total,
        )
        column_list.append(current)
        partial_list.append(partial_value)
        previous = current
    diag_list = []
    totals = lax.psum(jnp.stack(partial_list), ("row", "col"))
    chain_prev = None
    for position in range(supers):
        link = None if position == 0 else coupling[position - 1]
        diag_now = chain_diag(totals[position], chain_prev, link)
        diag_list.append(lax.dynamic_slice_in_dim(diag_now, column * diag_cols, diag_cols, 1))
        chain_prev = diag_now
    diagonals = jnp.stack(diag_list)
    return (jnp.stack(column_list), diagonals)


def swap(value, axis, bit, parts):
    return lax.ppermute(value, axis, [(i, i ^ bit) for i in range(parts)])


def across(value):
    return lax.ppermute(value, "col", [(0, 1), (1, 0)])


def after(values, *events):
    return lax.optimization_barrier((values, events))[0]


def split2(value):
    high = value.astype(bf16)
    return high, (value - high.astype(f32)).astype(bf16)


def nn(a, b):
    return lax.dot_general(a, b, (((1,), (0,)), ((), ())), preferred_element_type=f32)


def nt(a, b):
    return lax.dot_general(a, b, (((1,), (1,)), ((), ())), preferred_element_type=f32)


def nn2(pair, b):
    return nn(pair[0], b) + nn(pair[1], b)


def nn2r(a, pair):
    return nn(a, pair[0]) + nn(a, pair[1])


def owner_of(row, wave, count, j, i):
    return 4 * ((row // 4) ^ (wave * count + i)) + ((row % 4) ^ j)


def place_kernel(dims, *refs):
    supers, width, rows, span, part = dims
    occ_ref, block_ref = refs[:2]
    f_refs, pt = refs[2:6], refs[6]
    row, col = lax.axis_index("row"), lax.axis_index("col")
    per_side = span // 128
    for side in range(2):
        target = col if side == 0 else 1 - col
        for s in range(supers):
            for b in range(per_side):
                lanes = pl.ds(pl.multiple_of(block_ref[s, target * per_side + b] * 128, 128), 128)
                for wave in range(2):
                    source = f_refs[2 * side + wave]
                    for j in range(4):
                        for i in range(source.shape[1]):
                            first = owner_of(row, wave, source.shape[1], j, i) * part
                            pt[s, pl.ds(pl.multiple_of(first, part), part), lanes] = source[
                                j, i, s * part : (s + 1) * part, b * 128 : (b + 1) * 128
                            ]
    for s in range(supers):
        for b in range(2 * per_side):

            @pl.when(occ_ref[s, b] == 0)
            def _():
                lanes = pl.ds(pl.multiple_of(block_ref[s, b] * 128, 128), 128)
                pt[s, :, lanes] = jnp.zeros((width, 128), bf16)


def load_rows(wave, skip, span, col, row, z_refs, z_all, sem):
    half_rows = z_all.shape[0]
    copies = []
    for side in range(2):
        target = col if side == 0 else 1 - col
        source = z_refs[side]
        local_rows = source.shape[2] - skip
        for j in range(4):
            for i in range(source.shape[1]):
                place = owner_of(row, wave, source.shape[1], j, i) % (half_rows // local_rows)
                copies.append(
                    pltpu.make_async_copy(
                        source.at[j, i, pl.ds(skip, local_rows)],
                        z_all.at[
                            pl.ds(pl.multiple_of(place * local_rows, local_rows), local_rows),
                            pl.ds(pl.multiple_of(target * span, span), span),
                        ],
                        sem,
                    )
                )
    for copy in copies:
        copy.start()
    for copy in copies:
        copy.wait()


def halves(col, half_w):
    return pl.ds(pl.multiple_of(col * half_w, half_w), half_w)


def lanes_of(row, wave, local_rows, half_rows, count):
    half = owner_of(row, wave, count, 0, 0) // (half_rows // local_rows)
    return pl.ds(pl.multiple_of(half * half_rows, half_rows), half_rows)


def row_products(pt, link_ref, zm, c_rows, held, tmp):
    c0h, c0l, p1h, p1l, c1h, c1l, c2h, c2l = held
    cols0 = split2(-nt(zm, pt[0]))
    c0h[...], c0l[...] = cols0
    tmp[...] = nn2(cols0, link_ref[0])
    p1h[...], p1l[...] = split2(tmp[...])
    tmp[...] += nt(zm, pt[1])
    cols1 = split2(-tmp[...])
    c1h[...], c1l[...] = cols1
    cols2 = -(nt(zm, pt[2, c_rows, :]) + nn2(cols1, link_ref[1, :, c_rows]))
    c2h[...], c2l[...] = split2(cols2)


def rows_kernel(dims, skip, *refs):
    width, span = dims
    pt, z_refs, link_ref = refs[0], refs[1:3], refs[3]
    held, z_own, z_all, tmp, sem = refs[4:12], refs[12], refs[13], refs[14], refs[15]
    col, row = lax.axis_index("col"), lax.axis_index("row")
    load_rows(0, skip, span, col, row, z_refs, z_all, sem)
    row_products(pt, link_ref, z_all[...], halves(col, width // 2), held, tmp)
    local_rows = z_own.shape[0]
    place = row % (z_all.shape[0] // local_rows)
    z_own[...] = z_all[pl.ds(pl.multiple_of(place * local_rows, local_rows), local_rows), :]


def early_sums_kernel(count, *refs):
    pt, c0h, c0l, p1h, p1l, c1h, c1l, z_own, link_ref = refs[:9]
    s0, u1, col_out = refs[9:]
    col, row = lax.axis_index("col"), lax.axis_index("row")
    local_rows, half_rows = z_own.shape[0], c0h.shape[0]
    lanes = lanes_of(row, 0, local_rows, half_rows, count)
    s0[...] = nn2r(pt[0, :, lanes], (c0h[...], c0l[...]))
    u1[...] = nn2r(pt[1, :, lanes], (p1h[...], p1l[...]))
    tile = col_out.shape[1]
    place = row % (half_rows // local_rows)
    own = pl.ds(pl.multiple_of(place * local_rows, local_rows), local_rows)
    cols1 = (c1h[own, :], c1l[own, :])
    mine = [
        c0h[own, :].astype(f32) + c0l[own, :].astype(f32),
        cols1[0].astype(f32) + cols1[1].astype(f32),
        -(nt(z_own[...], pt[2]) + nn2(cols1, link_ref[1])),
    ]
    for s, value in enumerate(mine):
        col_out[s] = jnp.where(col == 0, value[:tile], value[tile:])


def late_sums_kernel(count, local_rows, *refs):
    pt, c1h, c1l, c2h, c2l = refs[:5]
    s1, n2, s2 = refs[5:]
    col, row = lax.axis_index("col"), lax.axis_index("row")
    half_rows, half_w = c2h.shape
    lanes = lanes_of(row, 0, local_rows, half_rows, count)
    s1[...] = nn2r(pt[1, :, lanes], (c1h[...], c1l[...]))
    n2[...] = nn2r(pt[2, halves(col, half_w), lanes], (c1h[...], c1l[...]))
    s2[...] = nn2r(pt[2, :, lanes], (c2h[...], c2l[...]))


def last_kernel(dims, rows, *refs):
    width, span = dims
    pt, z_refs, link_ref, diag_ref, diag_other_ref = refs[0], refs[1:3], refs[3], refs[4], refs[5]
    before, diag_out, held, z_all, tmp, sem = refs[6:11], refs[11], refs[12:20], refs[20], refs[21], refs[22]
    col, row = lax.axis_index("col"), lax.axis_index("row")
    half_w = width // 2
    half_rows = z_all.shape[0]
    c_rows = halves(col, half_w)
    load_rows(1, 0, span, col, row, z_refs, z_all, sem)
    row_products(pt, link_ref, z_all[...], c_rows, held, tmp)
    c0h, c0l, p1h, p1l, c1h, c1l, c2h, c2l = held
    lanes = lanes_of(row, 1, z_refs[0].shape[2], half_rows, z_refs[0].shape[1])
    left = pt[1, :, lanes]
    s0 = before[0][...] + nn2r(pt[0, :, lanes], (c0h[...], c0l[...]))
    u1 = before[1][...] + nn2r(left, (p1h[...], p1l[...]))
    s1 = before[2][...] + nn2r(left, (c1h[...], c1l[...]))
    n2 = before[3][...] + nn2r(pt[2, c_rows, lanes], (c1h[...], c1l[...]))
    s2 = before[4][...] + nn2r(pt[2, :, lanes], (c2h[...], c2l[...]))
    scale = 1.0 / rows

    def whole(s):
        mine, theirs = diag_ref[s], diag_other_ref[s]
        return jnp.concatenate([jnp.where(col == 0, mine, theirs), jnp.where(col == 0, theirs, mine)], axis=1)

    d0 = whole(0) - s0 * scale
    i1 = s1 - u1.T
    d1 = whole(1) - i1 * scale + nn2r(link_ref[0].T, split2(nn2(split2(d0), link_ref[0])))
    i2 = s2 - nn2(split2(n2), link_ref[1]).T
    d2 = diag_ref[2] - i2 * scale + nn2r(link_ref[1].T, split2(nn2(split2(d1), link_ref[1, :, c_rows])))
    diag_out[0] = jnp.where(col == 0, d0[:, :half_w], d0[:, half_w:])
    diag_out[1] = jnp.where(col == 0, d1[:, :half_w], d1[:, half_w:])
    diag_out[2] = d2


def replicated_plan(inverse_block, factor_cols, occupancy, row_block, coupling, diag_inverse):
    row_parts = lax.axis_size("row")
    supers, span, part = factor_cols.shape
    width = part * row_parts
    local_rows = inverse_block.shape[0]
    rows = local_rows * row_parts
    count = row_parts // 8
    any_spec = pl.BlockSpec(memory_space=pl.ANY)
    smem = pl.BlockSpec(memory_space=pltpu.SMEM)
    vmem = pl.BlockSpec(memory_space=pltpu.VMEM)
    shape = jax.ShapeDtypeStruct

    def call(body, name, flops, **kwargs):
        return pl.pallas_call(
            body,
            compiler_params=pltpu.CompilerParams(vmem_limit_bytes=VMEM_LIMIT),
            cost_estimate=pl.CostEstimate(flops=flops, bytes_accessed=8 * 2**20, transcendentals=0),
            name=name,
            **kwargs,
        )

    x = lambda value: swap(value, "row", 1, row_parts)
    y = lambda value: swap(value, "row", 2, row_parts)
    line = lambda value, k: swap(value, "row", 4 * k, row_parts)

    def far(over_x, over_y, i):
        return x(over_y) if i % 2 == 0 else y(over_x)

    f_rows = supers * part
    f_own = jnp.transpose(factor_cols, (0, 2, 1)).reshape(f_rows, span)
    f_late = [line(f_own, k) for k in range(count, row_parts // 4)]
    own = jnp.concatenate([f_own, inverse_block], axis=0)
    early = []
    for k in range(count):
        value = own if k == 0 else line(own, k)
        value = after(value, *early[-1][1:3]) if k else value
        early.append([value, x(value), y(value)])
    z_near = jnp.stack([p[0][f_rows:] for p in early])
    z_late = line(z_near, count)
    for k, part_k in enumerate(early):
        over = after(part_k[1:3], z_late) if k else part_k[1:3]
        part_k.append(far(*over, k))
    first = jnp.stack([jnp.stack([p[j] for p in early]) for j in range(4)])
    first_other = across(first)
    f_b = after(jnp.stack(f_late), *early[-1][1:3], early[0][3])
    f_bx, f_by = x(f_b), y(f_b)
    f_bx, f_by = after((f_bx, f_by), z_late)
    f_far = jnp.stack([far(f_bx[i], f_by[i], i) for i in range(count)])
    f_last = jnp.stack([f_b, f_bx, f_by, f_far])
    f_last_other = across(f_last)
    z_b = after(z_late, f_bx, f_by)
    z_bx, z_by = x(z_b), y(z_b)
    diag_other = across(diag_inverse)

    pt = call(
        functools.partial(place_kernel, (supers, width, rows, span, part)),
        "place", 2 * 10**9,
        out_shape=shape((supers, width, rows), bf16),
        in_specs=[smem] * 2 + [vmem] * 4,
        out_specs=vmem,
    )(occupancy, row_block, first, f_last, first_other, f_last_other)

    dims = (width, span)
    half_rows, half_w = rows // 2, width // 2
    held_shapes = [(half_rows, width)] * 6 + [(half_rows, half_w)] * 2
    work = [pltpu.VMEM((half_rows, 2 * span), bf16), pltpu.VMEM((half_rows, width), f32), pltpu.SemaphoreType.DMA]
    *held, z_own = call(
        functools.partial(rows_kernel, dims, supers * part),
        "own_half_rows", 4 * 10**9,
        out_shape=tuple(shape(v, bf16) for v in held_shapes) + (shape((local_rows, 2 * span), bf16),),
        in_specs=[vmem] + [any_spec] * 2 + [vmem],
        out_specs=(vmem,) * 9,
        scratch_shapes=work,
    )(pt, first, first_other, coupling)
    z_bx, z_by, *held = after((z_bx, z_by, *held), held[0])
    z_far = jnp.stack([far(z_bx[i], z_by[i], i) for i in range(count)])
    c0h, c0l, p1h, p1l, c1h, c1l, c2h, c2l = held
    s0, u1, columns = call(
        functools.partial(early_sums_kernel, count),
        "early_sums", 3 * 10**9,
        out_shape=(shape((width, width), f32),) * 2 + (shape((supers, local_rows // 2, width), f32),),
        in_specs=[vmem] * 9,
        out_specs=(vmem,) * 3,
    )(pt, c0h, c0l, p1h, p1l, c1h, c1l, z_own, coupling)
    z_far, c1h = after((z_far, c1h), s0)
    z_last = jnp.stack([z_b, z_bx, z_by, z_far])
    z_last_other = across(z_last)
    s1, n2, s2 = call(
        functools.partial(late_sums_kernel, count, local_rows),
        "late_sums", 2 * 10**9,
        out_shape=(shape((width, width), f32), shape((half_w, width), f32), shape((width, half_w), f32)),
        in_specs=[vmem] * 5,
        out_specs=(vmem,) * 3,
    )(pt, c1h, c1l, c2h, c2l)
    sums = [s0, u1, s1, n2, s2]
    diagonals = call(
        functools.partial(last_kernel, dims, rows),
        "other_half", 12 * 10**9,
        out_shape=shape((supers, width, half_w), f32),
        in_specs=[vmem] + [any_spec] * 2 + [vmem] * 8,
        out_specs=vmem,
        scratch_shapes=[pltpu.VMEM(v, bf16) for v in held_shapes] + work,
    )(pt, z_last, z_last_other, coupling, diag_inverse, diag_other, *sums)
    return columns, diagonals


def solution(mesh):
    row_parts, col_parts = mesh.shape["row"], mesh.shape["col"]
    in_specs = (P("row", "col"), P(None, "col", "row"), P(), P(), P(), P(None, None, "col"))
    out_specs = (P(None, ("row", "col"), None), P(None, None, "col"))

    def per_device(inverse_block, factor_cols, *rest):
        held = (inverse_block.size + factor_cols.size) * 2 * row_parts * col_parts
        fits = held <= REPLICATE_BYTES and col_parts == 2 and row_parts in (8, 16)
        plan = replicated_plan if fits else grid_plan
        return plan(inverse_block, factor_cols, *rest)

    return jax.shard_map(
        per_device, mesh=mesh, in_specs=in_specs, out_specs=out_specs, check_vma=False
    )
```

```python
import functools

import jax
import jax.numpy as jnp
from jax import lax
from jax.experimental import pallas as pl
from jax.experimental.pallas import tpu as pltpu
from jax.sharding import PartitionSpec as P

highest = lax.Precision.HIGHEST
f32 = jnp.float32
bf16 = jnp.bfloat16

REPLICATE_BYTES = 12 * 2**20
VMEM_LIMIT = 40 * 2**20


def routed(gathered, occupancy, row_block, nblocks):
    count = gathered.shape[0]
    width_part = gathered.shape[1] // (nblocks * 128)
    blocks = gathered.reshape(count, nblocks, 128, width_part)
    levels = lax.broadcasted_iota(jnp.int32, (count, nblocks, nblocks), 1)
    picks = ((row_block[:, None, :] == levels) & (occupancy[:, None, :] > 0)).astype(jnp.bfloat16)
    placed = jnp.einsum("kqb,kbtx->kxqt", picks, blocks, preferred_element_type=jnp.float32)
    return placed.astype(jnp.bfloat16).reshape(count, width_part, nblocks * 128)


def split_rows(placed, column, row_parts, col_parts, tile):
    count, width_part, total = placed.shape
    span = total // col_parts
    column_part = lax.dynamic_slice_in_dim(placed, column * span, span, 2)
    grid = placed.reshape(count, width_part, row_parts, col_parts, tile)
    mine = lax.dynamic_index_in_dim(grid, column, 3, keepdims=False)
    return (column_part, jnp.transpose(mine, (0, 2, 1, 3)))


def make_term(inverse_block, column_full):
    return lax.dot_general(
        inverse_block, column_full, (((1,), (2,)), ((), ())), preferred_element_type=jnp.float32
    )


def local_step(summed, own_rows, previous, link, diag_part, column, row_first, rows_total):
    if link is None:
        coupled = jnp.zeros_like(summed)
    else:
        coupled = jnp.dot(previous, link.astype(jnp.float32), precision=highest)
    current = -(summed + coupled)
    own = own_rows.astype(jnp.float32)
    inner = jnp.dot(own, current, precision=highest) - jnp.dot(coupled.T, own.T, precision=highest)
    width = summed.shape[1]
    diag_cols = diag_part.shape[1]
    embedded = lax.dynamic_update_slice(
        jnp.zeros((width, width), jnp.float32), diag_part, (0, column * diag_cols)
    )
    return (current, row_first * embedded - inner / rows_total)


def chain_diag(total, chain_prev, link):
    if link is None:
        return total
    link_wide = link.astype(jnp.float32)
    return total + jnp.dot(
        link_wide.T, jnp.dot(chain_prev, link_wide, precision=highest), precision=highest
    )


def grid_plan(inverse_block, factor_cols, occupancy, row_block, coupling, diag_inverse):
    column = lax.axis_index("col")
    row_first = (lax.axis_index("row") == 0).astype(jnp.float32)
    row_parts = lax.axis_size("row")
    col_parts = lax.axis_size("col")
    local_rows = inverse_block.shape[0]
    rows_total = local_rows * row_parts
    supers, span, width_part = factor_cols.shape
    width = width_part * row_parts
    tile = local_rows // col_parts
    nblocks = occupancy.shape[1]
    diag_cols = diag_inverse.shape[2]
    flat = factor_cols.reshape(supers, span * width_part)
    column_list = []
    partial_list = []
    previous = None
    gathered = lax.all_gather(flat, "col", axis=1, tiled=True)
    placed = routed(gathered, occupancy, row_block, nblocks)
    column_part, outgoing = split_rows(placed, column, row_parts, col_parts, tile)
    column_full = lax.all_gather(column_part, "row", axis=1, tiled=True)
    arrived = lax.all_to_all(outgoing, "row", split_axis=1, concat_axis=1, tiled=True)
    own_all = arrived.reshape(supers, width, tile)
    summed = lax.psum_scatter(
        make_term(inverse_block, column_full), "col", scatter_dimension=0, tiled=True
    )
    for position in range(supers):
        link = None if position == 0 else coupling[position - 1]
        current, partial_value = local_step(
            summed[:, position, :],
            own_all[position],
            previous,
            link,
            diag_inverse[position],
            column,
            row_first,
            rows_total,
        )
        column_list.append(current)
        partial_list.append(partial_value)
        previous = current
    diag_list = []
    totals = lax.psum(jnp.stack(partial_list), ("row", "col"))
    chain_prev = None
    for position in range(supers):
        link = None if position == 0 else coupling[position - 1]
        diag_now = chain_diag(totals[position], chain_prev, link)
        diag_list.append(lax.dynamic_slice_in_dim(diag_now, column * diag_cols, diag_cols, 1))
        chain_prev = diag_now
    diagonals = jnp.stack(diag_list)
    return (jnp.stack(column_list), diagonals)


def swap(value, axis, bit, parts):
    return lax.ppermute(value, axis, [(i, i ^ bit) for i in range(parts)])


def across(value):
    return lax.ppermute(value, "col", [(0, 1), (1, 0)])


def after(values, *events):
    return lax.optimization_barrier((values, events))[0]


def split2(value):
    high = value.astype(bf16)
    return high, (value - high.astype(f32)).astype(bf16)


def nn(a, b):
    return lax.dot_general(a, b, (((1,), (0,)), ((), ())), preferred_element_type=f32)


def nt(a, b):
    return lax.dot_general(a, b, (((1,), (1,)), ((), ())), preferred_element_type=f32)


def nn2(pair, b):
    return nn(pair[0], b) + nn(pair[1], b)


def nn2r(a, pair):
    return nn(a, pair[0]) + nn(a, pair[1])


def owner_of(row, wave, count, j, i):
    return 4 * ((row // 4) ^ (wave * count + i)) + ((row % 4) ^ j)


def place_kernel(dims, *refs):
    supers, width, rows, span, part = dims
    occ_ref, block_ref = refs[:2]
    f_refs, pt = refs[2:6], refs[6]
    row, col = lax.axis_index("row"), lax.axis_index("col")
    per_side = span // 128
    for side in range(2):
        target = col if side == 0 else 1 - col
        for s in range(supers):
            for b in range(per_side):
                lanes = pl.ds(pl.multiple_of(block_ref[s, target * per_side + b] * 128, 128), 128)
                for wave in range(2):
                    source = f_refs[2 * side + wave]
                    for j in range(4):
                        for i in range(source.shape[1]):
                            first = owner_of(row, wave, source.shape[1], j, i) * part
                            pt[s, pl.ds(pl.multiple_of(first, part), part), lanes] = source[
                                j, i, s * part : (s + 1) * part, b * 128 : (b + 1) * 128
                            ]
    for s in range(supers):
        for b in range(2 * per_side):

            @pl.when(occ_ref[s, b] == 0)
            def _():
                lanes = pl.ds(pl.multiple_of(block_ref[s, b] * 128, 128), 128)
                pt[s, :, lanes] = jnp.zeros((width, 128), bf16)


def add_rows(wave, skip, dims, col, row, pt, z_refs, link_ref, before, sums, scratch, meanwhile=None):
    width, span = dims
    z_all, c0h, c0l, c1h, c1l, p1h, p1l, c2h, c2l, tmp, sem = scratch
    half_rows = z_all.shape[0]
    half_w = width // 2
    copies = []
    for side in range(2):
        target = col if side == 0 else 1 - col
        source = z_refs[side]
        local_rows = source.shape[2] - skip
        for j in range(4):
            for i in range(source.shape[1]):
                place = owner_of(row, wave, source.shape[1], j, i) % (half_rows // local_rows)
                copies.append(
                    pltpu.make_async_copy(
                        source.at[j, i, pl.ds(skip, local_rows)],
                        z_all.at[
                            pl.ds(pl.multiple_of(place * local_rows, local_rows), local_rows),
                            pl.ds(pl.multiple_of(target * span, span), span),
                        ],
                        sem,
                    )
                )
    for copy in copies:
        copy.start()
    if meanwhile is not None:
        meanwhile()
    for copy in copies:
        copy.wait()
    c_rows = pl.ds(pl.multiple_of(col * half_w, half_w), half_w)
    half = owner_of(row, wave, z_refs[0].shape[1], 0, 0) // (half_rows // local_rows)
    lanes = pl.ds(pl.multiple_of(half * half_rows, half_rows), half_rows)
    zm = z_all[...]
    cols0 = split2(-nt(zm, pt[0]))
    c0h[...], c0l[...] = cols0
    tmp[...] = nn2(cols0, link_ref[0])
    p1h[...], p1l[...] = split2(tmp[...])
    tmp[...] += nt(zm, pt[1])
    cols1 = split2(-tmp[...])
    c1h[...], c1l[...] = cols1
    cols2 = -(nt(zm, pt[2, c_rows, :]) + nn2(cols1, link_ref[1, :, c_rows]))
    c2h[...], c2l[...] = split2(cols2)
    left = pt[1, :, lanes]
    terms = [
        nn2r(pt[0, :, lanes], (c0h[...], c0l[...])),
        nn2r(left, (p1h[...], p1l[...])),
        nn2r(left, (c1h[...], c1l[...])),
        nn2r(pt[2, c_rows, lanes], (c1h[...], c1l[...])),
        nn2r(pt[2, :, lanes], (c2h[...], c2l[...])),
    ]
    for i, term in enumerate(terms):
        sums[i][...] = before[i][...] + term if before else term


def first_kernel(dims, skip, *refs):
    pt, z_refs, link_ref = refs[0], refs[1:3], refs[3]
    sums, col_out, scratch = refs[4:9], refs[9], refs[10:]
    col, row = lax.axis_index("col"), lax.axis_index("row")
    add_rows(0, skip, dims, col, row, pt, z_refs, link_ref, (), sums, scratch)
    z_all, c0h, c0l, c1h, c1l = scratch[:5]
    tile = col_out.shape[1]
    place = row % (z_all.shape[0] // (2 * tile))
    own = pl.ds(pl.multiple_of(place * 2 * tile, 2 * tile), 2 * tile)
    cols1 = (c1h[own, :], c1l[own, :])
    mine = [
        c0h[own, :].astype(f32) + c0l[own, :].astype(f32),
        cols1[0].astype(f32) + cols1[1].astype(f32),
        -(nt(z_all[own, :], pt[2]) + nn2(cols1, link_ref[1])),
    ]
    for s, value in enumerate(mine):
        col_out[s] = jnp.where(col == 0, value[:tile], value[tile:])


def last_kernel(dims, rows, *refs):
    pt, z_refs, link_ref, diag_ref, diag_other_ref = refs[0], refs[1:3], refs[3], refs[4], refs[5]
    before, diag_out, sums, (link_t, whole), scratch = refs[6:11], refs[11], refs[12:17], refs[17:19], refs[19:]
    col = lax.axis_index("col")
    width, _ = dims
    half_w = width // 2

    def meanwhile():
        for s in range(2):
            link_t[s] = link_ref[s].T
            mine, theirs = diag_ref[s], diag_other_ref[s]
            whole[s, :, :half_w] = jnp.where(col == 0, mine, theirs)
            whole[s, :, half_w:] = jnp.where(col == 0, theirs, mine)

    add_rows(1, 0, dims, col, lax.axis_index("row"), pt, z_refs, link_ref, before, sums, scratch, meanwhile)
    s0, u1, s1, n2, s2 = sums
    scale = 1.0 / rows
    c_rows = pl.ds(pl.multiple_of(col * half_w, half_w), half_w)

    d0 = whole[0] - s0[...] * scale
    i1 = s1[...] - u1[...].T
    d1 = whole[1] - i1 * scale + nn2r(link_t[0], split2(nn2(split2(d0), link_ref[0])))
    i2 = s2[...] - nn2(split2(n2[...]), link_ref[1]).T
    d2 = diag_ref[2] - i2 * scale + nn2r(link_t[1], split2(nn2(split2(d1), link_ref[1, :, c_rows])))
    diag_out[0] = jnp.where(col == 0, d0[:, :half_w], d0[:, half_w:])
    diag_out[1] = jnp.where(col == 0, d1[:, :half_w], d1[:, half_w:])
    diag_out[2] = d2


def replicated_plan(inverse_block, factor_cols, occupancy, row_block, coupling, diag_inverse):
    row_parts = lax.axis_size("row")
    supers, span, part = factor_cols.shape
    width = part * row_parts
    local_rows = inverse_block.shape[0]
    rows = local_rows * row_parts
    count = row_parts // 8
    any_spec = pl.BlockSpec(memory_space=pl.ANY)
    smem = pl.BlockSpec(memory_space=pltpu.SMEM)
    vmem = pl.BlockSpec(memory_space=pltpu.VMEM)
    shape = jax.ShapeDtypeStruct

    def call(body, name, flops, **kwargs):
        return pl.pallas_call(
            body,
            compiler_params=pltpu.CompilerParams(vmem_limit_bytes=VMEM_LIMIT),
            cost_estimate=pl.CostEstimate(flops=flops, bytes_accessed=8 * 2**20, transcendentals=0),
            name=name,
            **kwargs,
        )

    outer = row_parts // 4
    x = lambda value: swap(value, "row", 1, row_parts)
    y = lambda value: swap(value, "row", 2, row_parts)
    line = lambda value, k: swap(value, "row", 4 * k, row_parts)

    def far(over_x, over_y, i):
        return x(over_y) if i % 2 == 0 else y(over_x)

    def late_wave(parts, *events):
        own = after(jnp.stack(parts), *events)
        return own, x(own), y(own)

    f_own = jnp.transpose(factor_cols, (0, 2, 1)).reshape(supers * part, span)
    f_late = [line(f_own, k) for k in range(count, outer)]
    own = jnp.concatenate([f_own, inverse_block], axis=0)
    early = []
    for k in range(count):
        value = own if k == 0 else line(own, k)
        value = after(value, *early[-1][1:3]) if k else value
        over_x, over_y = x(value), y(value)
        early.append([value, over_x, over_y, far(over_x, over_y, k)])
    first = jnp.stack([jnp.stack([p[j] for p in early]) for j in range(4)])
    first_other = across(first)
    block = after(inverse_block, *f_late, *early[-1][1:3])
    z_late = [line(block, k) for k in range(count, outer)]
    f_b, f_bx, f_by = late_wave(f_late, *early[-1][1:3], early[0][3])
    f_bx, f_by = after((f_bx, f_by), *z_late)
    f_far = jnp.stack([far(f_bx[i], f_by[i], i) for i in range(count)])
    f_last = jnp.stack([f_b, f_bx, f_by, f_far])
    z_b, z_bx, z_by = late_wave(z_late, f_bx, f_by)
    f_last_other = across(after(f_last, z_bx, z_by))
    diag_other = across(diag_inverse)

    pt = call(
        functools.partial(place_kernel, (supers, width, rows, span, part)),
        "place", 2 * 10**9,
        out_shape=shape((supers, width, rows), bf16),
        in_specs=[smem] * 2 + [vmem] * 4,
        out_specs=vmem,
    )(occupancy, row_block, first, f_last, first_other, f_last_other)

    z_far = jnp.stack([far(z_bx[i], z_by[i], i) for i in range(count)])
    z_far, pt = after((z_far, pt), pt)
    z_last = jnp.stack([z_b, z_bx, z_by, z_far])
    z_last_other = across(z_last)
    dims = (width, span)
    half_rows, half_w = rows // 2, width // 2
    sum_shapes = [(width, width), (width, width), (width, width), (half_w, width), (width, half_w)]
    scratch = (
        [pltpu.VMEM((half_rows, 2 * span), bf16)]
        + [pltpu.VMEM((half_rows, width), bf16)] * 6
        + [pltpu.VMEM((half_rows, half_w), bf16)] * 2
        + [pltpu.VMEM((half_rows, width), f32), pltpu.SemaphoreType.DMA]
    )
    *sums, columns = call(
        functools.partial(first_kernel, dims, supers * part),
        "own_half", 8 * 10**9,
        out_shape=tuple(shape(v, f32) for v in sum_shapes) + (shape((supers, local_rows // 2, width), f32),),
        in_specs=[vmem] + [any_spec] * 2 + [vmem],
        out_specs=(vmem,) * 6,
        scratch_shapes=scratch,
    )(pt, first, first_other, coupling)
    diagonals = call(
        functools.partial(last_kernel, dims, rows),
        "other_half", 12 * 10**9,
        out_shape=shape((supers, width, half_w), f32),
        in_specs=[vmem] + [any_spec] * 2 + [vmem] * 8,
        out_specs=vmem,
        scratch_shapes=[pltpu.VMEM(v, f32) for v in sum_shapes]
        + [pltpu.VMEM((2, width, width), bf16), pltpu.VMEM((2, width, width), f32)]
        + scratch,
    )(pt, z_last, z_last_other, coupling, diag_inverse, diag_other, *sums)
    return columns, diagonals


def solution(mesh):
    row_parts, col_parts = mesh.shape["row"], mesh.shape["col"]
    in_specs = (P("row", "col"), P(None, "col", "row"), P(), P(), P(), P(None, None, "col"))
    out_specs = (P(None, ("row", "col"), None), P(None, None, "col"))

    def per_device(inverse_block, factor_cols, *rest):
        held = (inverse_block.size + factor_cols.size) * 2 * row_parts * col_parts
        fits = held <= REPLICATE_BYTES and col_parts == 2 and row_parts in (8, 16)
        plan = replicated_plan if fits else grid_plan
        return plan(inverse_block, factor_cols, *rest)

    return jax.shard_map(
        per_device, mesh=mesh, in_specs=in_specs, out_specs=out_specs, check_vma=False
    )
```

```python
import functools

import jax
import jax.numpy as jnp
from jax import lax
from jax.experimental import pallas as pl
from jax.experimental.pallas import tpu as pltpu
from jax.sharding import PartitionSpec as P

highest = lax.Precision.HIGHEST
f32 = jnp.float32
bf16 = jnp.bfloat16

REPLICATE_BYTES = 12 * 2**20
VMEM_LIMIT = 36 * 2**20


def routed(gathered, occupancy, row_block, nblocks):
    count = gathered.shape[0]
    width_part = gathered.shape[1] // (nblocks * 128)
    blocks = gathered.reshape(count, nblocks, 128, width_part)
    levels = lax.broadcasted_iota(jnp.int32, (count, nblocks, nblocks), 1)
    picks = ((row_block[:, None, :] == levels) & (occupancy[:, None, :] > 0)).astype(jnp.bfloat16)
    placed = jnp.einsum("kqb,kbtx->kxqt", picks, blocks, preferred_element_type=jnp.float32)
    return placed.astype(jnp.bfloat16).reshape(count, width_part, nblocks * 128)


def split_rows(placed, column, row_parts, col_parts, tile):
    count, width_part, total = placed.shape
    span = total // col_parts
    column_part = lax.dynamic_slice_in_dim(placed, column * span, span, 2)
    grid = placed.reshape(count, width_part, row_parts, col_parts, tile)
    mine = lax.dynamic_index_in_dim(grid, column, 3, keepdims=False)
    return (column_part, jnp.transpose(mine, (0, 2, 1, 3)))


def make_term(inverse_block, column_full):
    return lax.dot_general(
        inverse_block, column_full, (((1,), (2,)), ((), ())), preferred_element_type=jnp.float32
    )


def local_step(summed, own_rows, previous, link, diag_part, column, row_first, rows_total):
    if link is None:
        coupled = jnp.zeros_like(summed)
    else:
        coupled = jnp.dot(previous, link.astype(jnp.float32), precision=highest)
    current = -(summed + coupled)
    own = own_rows.astype(jnp.float32)
    inner = jnp.dot(own, current, precision=highest) - jnp.dot(coupled.T, own.T, precision=highest)
    width = summed.shape[1]
    diag_cols = diag_part.shape[1]
    embedded = lax.dynamic_update_slice(
        jnp.zeros((width, width), jnp.float32), diag_part, (0, column * diag_cols)
    )
    return (current, row_first * embedded - inner / rows_total)


def chain_diag(total, chain_prev, link):
    if link is None:
        return total
    link_wide = link.astype(jnp.float32)
    return total + jnp.dot(
        link_wide.T, jnp.dot(chain_prev, link_wide, precision=highest), precision=highest
    )


def grid_plan(inverse_block, factor_cols, occupancy, row_block, coupling, diag_inverse):
    column = lax.axis_index("col")
    row_first = (lax.axis_index("row") == 0).astype(jnp.float32)
    row_parts = lax.axis_size("row")
    col_parts = lax.axis_size("col")
    local_rows = inverse_block.shape[0]
    rows_total = local_rows * row_parts
    supers, span, width_part = factor_cols.shape
    width = width_part * row_parts
    tile = local_rows // col_parts
    nblocks = occupancy.shape[1]
    diag_cols = diag_inverse.shape[2]
    flat = factor_cols.reshape(supers, span * width_part)
    column_list = []
    partial_list = []
    previous = None
    gathered = lax.all_gather(flat, "col", axis=1, tiled=True)
    placed = routed(gathered, occupancy, row_block, nblocks)
    column_part, outgoing = split_rows(placed, column, row_parts, col_parts, tile)
    column_full = lax.all_gather(column_part, "row", axis=1, tiled=True)
    arrived = lax.all_to_all(outgoing, "row", split_axis=1, concat_axis=1, tiled=True)
    own_all = arrived.reshape(supers, width, tile)
    summed = lax.psum_scatter(
        make_term(inverse_block, column_full), "col", scatter_dimension=0, tiled=True
    )
    for position in range(supers):
        link = None if position == 0 else coupling[position - 1]
        current, partial_value = local_step(
            summed[:, position, :],
            own_all[position],
            previous,
            link,
            diag_inverse[position],
            column,
            row_first,
            rows_total,
        )
        column_list.append(current)
        partial_list.append(partial_value)
        previous = current
    diag_list = []
    totals = lax.psum(jnp.stack(partial_list), ("row", "col"))
    chain_prev = None
    for position in range(supers):
        link = None if position == 0 else coupling[position - 1]
        diag_now = chain_diag(totals[position], chain_prev, link)
        diag_list.append(lax.dynamic_slice_in_dim(diag_now, column * diag_cols, diag_cols, 1))
        chain_prev = diag_now
    diagonals = jnp.stack(diag_list)
    return (jnp.stack(column_list), diagonals)


def swap(value, axis, bit, parts):
    return lax.ppermute(value, axis, [(i, i ^ bit) for i in range(parts)])


def across(value):
    return lax.ppermute(value, "col", [(0, 1), (1, 0)])


def after(values, *events):
    return lax.optimization_barrier((events, values))[1]


def split2(value):
    high = value.astype(bf16)
    return high, (value - high.astype(f32)).astype(bf16)


def nn(a, b):
    return lax.dot_general(a, b, (((1,), (0,)), ((), ())), preferred_element_type=f32)


def nt(a, b):
    return lax.dot_general(a, b, (((1,), (1,)), ((), ())), preferred_element_type=f32)


def nn2(pair, b):
    return nn(pair[0], b) + nn(pair[1], b)


def nn2r(a, pair):
    return nn(a, pair[0]) + nn(a, pair[1])


def owner_of(row, wave, count, j, i):
    return 4 * ((row // 4) ^ (wave * count + i)) + ((row % 4) ^ (3 - j))


def place_kernel(dims, *refs):
    supers, width, rows, span, part = dims
    occ_ref, block_ref = refs[:2]
    f_refs, pt = refs[2:6], refs[6]
    row, col = lax.axis_index("row"), lax.axis_index("col")
    per_side = span // 128
    for side in range(2):
        target = col if side == 0 else 1 - col
        for s in range(supers):
            for b in range(per_side):
                lanes = pl.ds(pl.multiple_of(block_ref[s, target * per_side + b] * 128, 128), 128)
                for wave in range(2):
                    source = f_refs[2 * side + wave]
                    for j in range(4):
                        for i in range(source.shape[1]):
                            first = owner_of(row, wave, source.shape[1], j, i) * part
                            pt[s, pl.ds(pl.multiple_of(first, part), part), lanes] = source[
                                j, i, s * part : (s + 1) * part, b * 128 : (b + 1) * 128
                            ]
    for s in range(supers):
        for b in range(2 * per_side):

            @pl.when(occ_ref[s, b] == 0)
            def _():
                lanes = pl.ds(pl.multiple_of(block_ref[s, b] * 128, 128), 128)
                pt[s, :, lanes] = jnp.zeros((width, 128), bf16)


def load_rows(wave, skip, span, col, row, z_refs, z_all, sem):
    half_rows = z_all.shape[0]
    copies = []
    for side in range(2):
        target = col if side == 0 else 1 - col
        source = z_refs[side]
        local_rows = source.shape[2] - skip
        for j in range(4):
            for i in range(source.shape[1]):
                place = owner_of(row, wave, source.shape[1], j, i) % (half_rows // local_rows)
                copies.append(
                    pltpu.make_async_copy(
                        source.at[j, i, pl.ds(skip, local_rows)],
                        z_all.at[
                            pl.ds(pl.multiple_of(place * local_rows, local_rows), local_rows),
                            pl.ds(pl.multiple_of(target * span, span), span),
                        ],
                        sem,
                    )
                )
    for copy in copies:
        copy.start()
    for copy in copies:
        copy.wait()


def halves(col, half_w):
    return pl.ds(pl.multiple_of(col * half_w, half_w), half_w)


def lanes_of(row, wave, local_rows, half_rows, count):
    half = owner_of(row, wave, count, 0, 0) // (half_rows // local_rows)
    return pl.ds(pl.multiple_of(half * half_rows, half_rows), half_rows)


def row_products(pt, link_ref, zm, c_rows, held, tmp):
    c0h, c0l, p1h, p1l, c1h, c1l, c2h, c2l = held
    cols0 = split2(-nt(zm, pt[0]))
    c0h[...], c0l[...] = cols0
    tmp[...] = nn2(cols0, link_ref[0])
    p1h[...], p1l[...] = split2(tmp[...])
    tmp[...] += nt(zm, pt[1])
    cols1 = split2(-tmp[...])
    c1h[...], c1l[...] = cols1
    cols2 = -(nt(zm, pt[2, c_rows, :]) + nn2(cols1, link_ref[1, :, c_rows]))
    c2h[...], c2l[...] = split2(cols2)


def rows_kernel(dims, skip, *refs):
    width, span = dims
    pt, z_refs, link_ref = refs[0], refs[1:3], refs[3]
    col_out, held, z_all, tmp, sem = refs[4], refs[5:13], refs[13], refs[14], refs[15]
    col, row = lax.axis_index("col"), lax.axis_index("row")
    load_rows(0, skip, span, col, row, z_refs, z_all, sem)
    row_products(pt, link_ref, z_all[...], halves(col, width // 2), held, tmp)
    tile = col_out.shape[1]
    c0h, c0l, _, _, c1h, c1l, _, _ = held
    place = row % (z_all.shape[0] // (2 * tile))
    own = pl.ds(pl.multiple_of(place * 2 * tile, 2 * tile), 2 * tile)
    cols1 = (c1h[own, :], c1l[own, :])
    mine = [
        c0h[own, :].astype(f32) + c0l[own, :].astype(f32),
        cols1[0].astype(f32) + cols1[1].astype(f32),
        -(nt(z_all[own, :], pt[2]) + nn2(cols1, link_ref[1])),
    ]
    for s, value in enumerate(mine):
        col_out[s] = jnp.where(col == 0, value[:tile], value[tile:])


def early_sums_kernel(count, local_rows, *refs):
    pt, c0h, c0l, p1h, p1l, s0, u1 = refs
    lanes = lanes_of(lax.axis_index("row"), 0, local_rows, c0h.shape[0], count)
    s0[...] = nn2r(pt[0, :, lanes], (c0h[...], c0l[...]))
    u1[...] = nn2r(pt[1, :, lanes], (p1h[...], p1l[...]))


def late_sums_kernel(count, local_rows, *refs):
    pt, c1h, c1l, c2h, c2l = refs[:5]
    s1, n2, s2 = refs[5:]
    col, row = lax.axis_index("col"), lax.axis_index("row")
    half_rows, half_w = c2h.shape
    lanes = lanes_of(row, 0, local_rows, half_rows, count)
    s1[...] = nn2r(pt[1, :, lanes], (c1h[...], c1l[...]))
    n2[...] = nn2r(pt[2, halves(col, half_w), lanes], (c1h[...], c1l[...]))
    s2[...] = nn2r(pt[2, :, lanes], (c2h[...], c2l[...]))


def last_kernel(dims, rows, *refs):
    width, span = dims
    pt, z_refs, link_ref, diag_ref, diag_other_ref = refs[0], refs[1:3], refs[3], refs[4], refs[5]
    before, diag_out, held, z_all, tmp, sem = refs[6:11], refs[11], refs[12:20], refs[20], refs[21], refs[22]
    col, row = lax.axis_index("col"), lax.axis_index("row")
    half_w = width // 2
    half_rows = z_all.shape[0]
    c_rows = halves(col, half_w)
    load_rows(1, 0, span, col, row, z_refs, z_all, sem)
    row_products(pt, link_ref, z_all[...], c_rows, held, tmp)
    c0h, c0l, p1h, p1l, c1h, c1l, c2h, c2l = held
    lanes = lanes_of(row, 1, z_refs[0].shape[2], half_rows, z_refs[0].shape[1])
    left = pt[1, :, lanes]
    s0 = before[0][...] + nn2r(pt[0, :, lanes], (c0h[...], c0l[...]))
    u1 = before[1][...] + nn2r(left, (p1h[...], p1l[...]))
    s1 = before[2][...] + nn2r(left, (c1h[...], c1l[...]))
    n2 = before[3][...] + nn2r(pt[2, c_rows, lanes], (c1h[...], c1l[...]))
    s2 = before[4][...] + nn2r(pt[2, :, lanes], (c2h[...], c2l[...]))
    scale = 1.0 / rows

    def whole(s):
        mine, theirs = diag_ref[s], diag_other_ref[s]
        return jnp.concatenate([jnp.where(col == 0, mine, theirs), jnp.where(col == 0, theirs, mine)], axis=1)

    d0 = whole(0) - s0 * scale
    i1 = s1 - u1.T
    d1 = whole(1) - i1 * scale + nn2r(link_ref[0].T, split2(nn2(split2(d0), link_ref[0])))
    i2 = s2 - nn2(split2(n2), link_ref[1]).T
    d2 = diag_ref[2] - i2 * scale + nn2r(link_ref[1].T, split2(nn2(split2(d1), link_ref[1, :, c_rows])))
    diag_out[0] = jnp.where(col == 0, d0[:, :half_w], d0[:, half_w:])
    diag_out[1] = jnp.where(col == 0, d1[:, :half_w], d1[:, half_w:])
    diag_out[2] = d2


def replicated_plan(inverse_block, factor_cols, occupancy, row_block, coupling, diag_inverse):
    row_parts = lax.axis_size("row")
    supers, span, part = factor_cols.shape
    width = part * row_parts
    local_rows = inverse_block.shape[0]
    rows = local_rows * row_parts
    count = row_parts // 8
    any_spec = pl.BlockSpec(memory_space=pl.ANY)
    smem = pl.BlockSpec(memory_space=pltpu.SMEM)
    vmem = pl.BlockSpec(memory_space=pltpu.VMEM)
    shape = jax.ShapeDtypeStruct

    def call(body, name, flops, **kwargs):
        return pl.pallas_call(
            body,
            compiler_params=pltpu.CompilerParams(vmem_limit_bytes=VMEM_LIMIT),
            cost_estimate=pl.CostEstimate(flops=flops, bytes_accessed=8 * 2**20, transcendentals=0),
            name=name,
            **kwargs,
        )

    outer = row_parts // 4
    x = lambda value: swap(value, "row", 1, row_parts)
    y = lambda value: swap(value, "row", 2, row_parts)
    line = lambda value, k: swap(value, "row", 4 * k, row_parts)

    def far(over_x, over_y, i):
        return x(over_y) if i % 2 == 0 else y(over_x)

    def late_wave(parts, *events):
        own = after(jnp.stack(parts), *events)
        return own, x(own), y(own)

    f_own = jnp.transpose(factor_cols, (0, 2, 1)).reshape(supers * part, span)
    f_late = [line(f_own, k) for k in range(count, outer)]
    own = jnp.concatenate([f_own, inverse_block], axis=0)
    own_again = jnp.concatenate(lax.optimization_barrier([f_own, inverse_block]), axis=0)
    early = []
    for k in range(count):
        value = own if k == 0 else line(own_again, k)
        value = after(value, *early[-1][1:3]) if k else value
        over_x, over_y = x(value), y(value)
        early.append([value, over_x, over_y, far(over_x, over_y, k)])
    first = jnp.stack([jnp.stack([p[j] for p in early]) for j in (3, 2, 1, 0)])
    first_other = across(first)
    block = after(inverse_block, *f_late, *early[-1][1:3])
    z_late = [line(block, k) for k in range(count, outer)]
    f_b, f_bx, f_by = late_wave(f_late, *early[-1][1:3], early[0][3])
    f_bx, f_by = after((f_bx, f_by), *z_late)
    f_far = jnp.stack([far(f_bx[i], f_by[i], i) for i in range(count)])
    f_last = jnp.stack([f_far, f_by, f_bx, f_b])
    f_last_other = across(f_last)
    z_b, z_bx, z_by = late_wave(z_late, f_bx, f_by)
    diag_other = across(diag_inverse)

    pt = call(
        functools.partial(place_kernel, (supers, width, rows, span, part)),
        "place", 2 * 10**9,
        out_shape=shape((supers, width, rows), bf16),
        in_specs=[smem] * 2 + [vmem] * 4,
        out_specs=vmem,
    )(occupancy, row_block, first, f_last, first_other, f_last_other)

    dims = (width, span)
    half_rows, half_w = rows // 2, width // 2
    held_shapes = [(half_rows, width)] * 6 + [(half_rows, half_w)] * 2
    work = [pltpu.VMEM((half_rows, 2 * span), bf16), pltpu.VMEM((half_rows, width), f32), pltpu.SemaphoreType.DMA]
    columns, *held = call(
        functools.partial(rows_kernel, dims, supers * part),
        "own_half_rows", 4 * 10**9,
        out_shape=(shape((supers, local_rows // 2, width), f32),) + tuple(shape(v, bf16) for v in held_shapes),
        in_specs=[vmem] + [any_spec] * 2 + [vmem],
        out_specs=(vmem,) * 9,
        scratch_shapes=work,
    )(pt, first, first_other, coupling)
    z_bx, z_by, *held = after((z_bx, z_by, *held), held[0])
    z_far = jnp.stack([far(z_bx[i], z_by[i], i) for i in range(count)])
    c0h, c0l, p1h, p1l, c1h, c1l, c2h, c2l = held
    s0, u1 = call(
        functools.partial(early_sums_kernel, count, local_rows),
        "early_sums", 2 * 10**9,
        out_shape=(shape((width, width), f32),) * 2,
        in_specs=[vmem] * 5,
        out_specs=(vmem,) * 2,
    )(pt, c0h, c0l, p1h, p1l)
    z_far, c1h = after((z_far, c1h), s0)
    z_last = jnp.stack([z_far, z_by, z_bx, z_b])
    z_last_other = across(z_last)
    s1, n2, s2 = call(
        functools.partial(late_sums_kernel, count, local_rows),
        "late_sums", 2 * 10**9,
        out_shape=(shape((width, width), f32), shape((half_w, width), f32), shape((width, half_w), f32)),
        in_specs=[vmem] * 5,
        out_specs=(vmem,) * 3,
    )(pt, c1h, c1l, c2h, c2l)
    sums = [s0, u1, s1, n2, s2]
    diagonals = call(
        functools.partial(last_kernel, dims, rows),
        "other_half", 12 * 10**9,
        out_shape=shape((supers, width, half_w), f32),
        in_specs=[vmem] + [any_spec] * 2 + [vmem] * 8,
        out_specs=vmem,
        scratch_shapes=[pltpu.VMEM(v, bf16) for v in held_shapes] + work,
    )(pt, z_last, z_last_other, coupling, diag_inverse, diag_other, *sums)
    return columns, diagonals


def solution(mesh):
    row_parts, col_parts = mesh.shape["row"], mesh.shape["col"]
    in_specs = (P("row", "col"), P(None, "col", "row"), P(), P(), P(), P(None, None, "col"))
    out_specs = (P(None, ("row", "col"), None), P(None, None, "col"))

    def per_device(inverse_block, factor_cols, *rest):
        held = (inverse_block.size + factor_cols.size) * 2 * row_parts * col_parts
        fits = held <= REPLICATE_BYTES and col_parts == 2 and row_parts in (8, 16)
        plan = replicated_plan if fits else grid_plan
        return plan(inverse_block, factor_cols, *rest)

    return jax.shard_map(
        per_device, mesh=mesh, in_specs=in_specs, out_specs=out_specs, check_vma=False
    )
```

```python
import functools

import jax
import jax.numpy as jnp
from jax import lax
from jax.experimental import pallas as pl
from jax.experimental.pallas import tpu as pltpu
from jax.sharding import PartitionSpec as P

highest = lax.Precision.HIGHEST
f32 = jnp.float32
bf16 = jnp.bfloat16

REPLICATE_BYTES = 12 * 2**20
VMEM_LIMIT = 36 * 2**20


def routed(gathered, occupancy, row_block, nblocks):
    count = gathered.shape[0]
    width_part = gathered.shape[1] // (nblocks * 128)
    blocks = gathered.reshape(count, nblocks, 128, width_part)
    levels = lax.broadcasted_iota(jnp.int32, (count, nblocks, nblocks), 1)
    picks = ((row_block[:, None, :] == levels) & (occupancy[:, None, :] > 0)).astype(jnp.bfloat16)
    placed = jnp.einsum("kqb,kbtx->kxqt", picks, blocks, preferred_element_type=jnp.float32)
    return placed.astype(jnp.bfloat16).reshape(count, width_part, nblocks * 128)


def split_rows(placed, column, row_parts, col_parts, tile):
    count, width_part, total = placed.shape
    span = total // col_parts
    column_part = lax.dynamic_slice_in_dim(placed, column * span, span, 2)
    grid = placed.reshape(count, width_part, row_parts, col_parts, tile)
    mine = lax.dynamic_index_in_dim(grid, column, 3, keepdims=False)
    return (column_part, jnp.transpose(mine, (0, 2, 1, 3)))


def make_term(inverse_block, column_full):
    return lax.dot_general(
        inverse_block, column_full, (((1,), (2,)), ((), ())), preferred_element_type=jnp.float32
    )


def local_step(summed, own_rows, previous, link, diag_part, column, row_first, rows_total):
    if link is None:
        coupled = jnp.zeros_like(summed)
    else:
        coupled = jnp.dot(previous, link.astype(jnp.float32), precision=highest)
    current = -(summed + coupled)
    own = own_rows.astype(jnp.float32)
    inner = jnp.dot(own, current, precision=highest) - jnp.dot(coupled.T, own.T, precision=highest)
    width = summed.shape[1]
    diag_cols = diag_part.shape[1]
    embedded = lax.dynamic_update_slice(
        jnp.zeros((width, width), jnp.float32), diag_part, (0, column * diag_cols)
    )
    return (current, row_first * embedded - inner / rows_total)


def chain_diag(total, chain_prev, link):
    if link is None:
        return total
    link_wide = link.astype(jnp.float32)
    return total + jnp.dot(
        link_wide.T, jnp.dot(chain_prev, link_wide, precision=highest), precision=highest
    )


def grid_plan(inverse_block, factor_cols, occupancy, row_block, coupling, diag_inverse):
    column = lax.axis_index("col")
    row_first = (lax.axis_index("row") == 0).astype(jnp.float32)
    row_parts = lax.axis_size("row")
    col_parts = lax.axis_size("col")
    local_rows = inverse_block.shape[0]
    rows_total = local_rows * row_parts
    supers, span, width_part = factor_cols.shape
    width = width_part * row_parts
    tile = local_rows // col_parts
    nblocks = occupancy.shape[1]
    diag_cols = diag_inverse.shape[2]
    flat = factor_cols.reshape(supers, span * width_part)
    column_list = []
    partial_list = []
    previous = None
    gathered = lax.all_gather(flat, "col", axis=1, tiled=True)
    placed = routed(gathered, occupancy, row_block, nblocks)
    column_part, outgoing = split_rows(placed, column, row_parts, col_parts, tile)
    column_full = lax.all_gather(column_part, "row", axis=1, tiled=True)
    arrived = lax.all_to_all(outgoing, "row", split_axis=1, concat_axis=1, tiled=True)
    own_all = arrived.reshape(supers, width, tile)
    summed = lax.psum_scatter(
        make_term(inverse_block, column_full), "col", scatter_dimension=0, tiled=True
    )
    for position in range(supers):
        link = None if position == 0 else coupling[position - 1]
        current, partial_value = local_step(
            summed[:, position, :],
            own_all[position],
            previous,
            link,
            diag_inverse[position],
            column,
            row_first,
            rows_total,
        )
        column_list.append(current)
        partial_list.append(partial_value)
        previous = current
    diag_list = []
    totals = lax.psum(jnp.stack(partial_list), ("row", "col"))
    chain_prev = None
    for position in range(supers):
        link = None if position == 0 else coupling[position - 1]
        diag_now = chain_diag(totals[position], chain_prev, link)
        diag_list.append(lax.dynamic_slice_in_dim(diag_now, column * diag_cols, diag_cols, 1))
        chain_prev = diag_now
    diagonals = jnp.stack(diag_list)
    return (jnp.stack(column_list), diagonals)


def swap(value, axis, bit, parts):
    return lax.ppermute(value, axis, [(i, i ^ bit) for i in range(parts)])


def across(value):
    return lax.ppermute(value, "col", [(0, 1), (1, 0)])


def after(values, *events):
    return lax.optimization_barrier((events, values))[1]


def split2(value):
    high = value.astype(bf16)
    return high, (value - high.astype(f32)).astype(bf16)


def nn(a, b):
    return lax.dot_general(a, b, (((1,), (0,)), ((), ())), preferred_element_type=f32)


def nt(a, b):
    return lax.dot_general(a, b, (((1,), (1,)), ((), ())), preferred_element_type=f32)


def nn2(pair, b):
    return nn(pair[0], b) + nn(pair[1], b)


def nn2r(a, pair):
    return nn(a, pair[0]) + nn(a, pair[1])


def owner_of(row, wave, count, j, i):
    return 4 * ((row // 4) ^ (wave * count + i)) + ((row % 4) ^ (3 - j))


def place_kernel(dims, *refs):
    supers, width, rows, span, part = dims
    occ_ref, block_ref = refs[:2]
    f_refs, pt = refs[2:6], refs[6]
    row, col = lax.axis_index("row"), lax.axis_index("col")
    per_side = span // 128
    for side in range(2):
        target = col if side == 0 else 1 - col
        for s in range(supers):
            for b in range(per_side):
                lanes = pl.ds(pl.multiple_of(block_ref[s, target * per_side + b] * 128, 128), 128)
                for wave in range(2):
                    source = f_refs[2 * side + wave]
                    for j in range(4):
                        for i in range(source.shape[1]):
                            first = owner_of(row, wave, source.shape[1], j, i) * part
                            pt[s, pl.ds(pl.multiple_of(first, part), part), lanes] = source[
                                j, i, s * part : (s + 1) * part, b * 128 : (b + 1) * 128
                            ]
    for s in range(supers):
        for b in range(2 * per_side):

            @pl.when(occ_ref[s, b] == 0)
            def _():
                lanes = pl.ds(pl.multiple_of(block_ref[s, b] * 128, 128), 128)
                pt[s, :, lanes] = jnp.zeros((width, 128), bf16)


def load_rows(wave, skip, span, col, row, z_refs, z_all, sem):
    half_rows = z_all.shape[0]
    copies = []
    for side in range(2):
        target = col if side == 0 else 1 - col
        source = z_refs[side]
        local_rows = source.shape[2] - skip
        for j in range(4):
            for i in range(source.shape[1]):
                place = owner_of(row, wave, source.shape[1], j, i) % (half_rows // local_rows)
                copies.append(
                    pltpu.make_async_copy(
                        source.at[j, i, pl.ds(skip, local_rows)],
                        z_all.at[
                            pl.ds(pl.multiple_of(place * local_rows, local_rows), local_rows),
                            pl.ds(pl.multiple_of(target * span, span), span),
                        ],
                        sem,
                    )
                )
    for copy in copies:
        copy.start()
    for copy in copies:
        copy.wait()


def halves(col, half_w):
    return pl.ds(pl.multiple_of(col * half_w, half_w), half_w)


def lanes_of(row, wave, local_rows, half_rows, count):
    half = owner_of(row, wave, count, 0, 0) // (half_rows // local_rows)
    return pl.ds(pl.multiple_of(half * half_rows, half_rows), half_rows)


def row_products(pt, link_ref, zm, c_rows, held, tmp):
    c0h, c0l, p1h, p1l, c1h, c1l, c2h, c2l = held
    cols0 = split2(-nt(zm, pt[0]))
    c0h[...], c0l[...] = cols0
    tmp[...] = nn2(cols0, link_ref[0])
    p1h[...], p1l[...] = split2(tmp[...])
    tmp[...] += nt(zm, pt[1])
    cols1 = split2(-tmp[...])
    c1h[...], c1l[...] = cols1
    if c2h is None:
        return
    cols2 = -(nt(zm, pt[2, c_rows, :]) + nn2(cols1, link_ref[1, :, c_rows]))
    c2h[...], c2l[...] = split2(cols2)


def rows_kernel(dims, skip, *refs):
    width, span = dims
    pt, z_refs, link_ref = refs[0], refs[1:3], refs[3]
    z_all, held, tmp, sem = refs[4], refs[5:11], refs[11], refs[12]
    col, row = lax.axis_index("col"), lax.axis_index("row")
    load_rows(0, skip, span, col, row, z_refs, z_all, sem)
    row_products(pt, link_ref, z_all[...], None, (*held, None, None), tmp)


def last_rows_kernel(*refs):
    pt, z_all, c0h, c0l, c1h, c1l, link_ref = refs[:7]
    col_out, c2h, c2l = refs[7:]
    col, row = lax.axis_index("col"), lax.axis_index("row")
    c_rows = halves(col, c2h.shape[1])
    cols1 = (c1h[...], c1l[...])
    cols2 = -(nt(z_all[...], pt[2, c_rows, :]) + nn2(cols1, link_ref[1, :, c_rows]))
    c2h[...], c2l[...] = split2(cols2)
    tile = col_out.shape[1]
    place = row % (z_all.shape[0] // (2 * tile))
    own = pl.ds(pl.multiple_of(place * 2 * tile, 2 * tile), 2 * tile)
    cols1 = (c1h[own, :], c1l[own, :])
    mine = [
        c0h[own, :].astype(f32) + c0l[own, :].astype(f32),
        cols1[0].astype(f32) + cols1[1].astype(f32),
        -(nt(z_all[own, :], pt[2]) + nn2(cols1, link_ref[1])),
    ]
    for s, value in enumerate(mine):
        col_out[s] = jnp.where(col == 0, value[:tile], value[tile:])


def early_sums_kernel(count, local_rows, *refs):
    pt, c0h, c0l, p1h, p1l, s0, u1 = refs
    lanes = lanes_of(lax.axis_index("row"), 0, local_rows, c0h.shape[0], count)
    s0[...] = nn2r(pt[0, :, lanes], (c0h[...], c0l[...]))
    u1[...] = nn2r(pt[1, :, lanes], (p1h[...], p1l[...]))


def late_sums_kernel(count, local_rows, *refs):
    pt, c1h, c1l, c2h, c2l = refs[:5]
    s1, n2, s2 = refs[5:]
    col, row = lax.axis_index("col"), lax.axis_index("row")
    half_rows, half_w = c2h.shape
    lanes = lanes_of(row, 0, local_rows, half_rows, count)
    s1[...] = nn2r(pt[1, :, lanes], (c1h[...], c1l[...]))
    n2[...] = nn2r(pt[2, halves(col, half_w), lanes], (c1h[...], c1l[...]))
    s2[...] = nn2r(pt[2, :, lanes], (c2h[...], c2l[...]))


def last_kernel(dims, rows, *refs):
    width, span = dims
    pt, z_refs, link_ref, diag_ref, diag_other_ref = refs[0], refs[1:3], refs[3], refs[4], refs[5]
    before, diag_out, held, z_all, tmp, sem = refs[6:11], refs[11], refs[12:20], refs[20], refs[21], refs[22]
    col, row = lax.axis_index("col"), lax.axis_index("row")
    half_w = width // 2
    half_rows = z_all.shape[0]
    c_rows = halves(col, half_w)
    load_rows(1, 0, span, col, row, z_refs, z_all, sem)
    row_products(pt, link_ref, z_all[...], c_rows, held, tmp)
    c0h, c0l, p1h, p1l, c1h, c1l, c2h, c2l = held
    lanes = lanes_of(row, 1, z_refs[0].shape[2], half_rows, z_refs[0].shape[1])
    left = pt[1, :, lanes]
    s0 = before[0][...] + nn2r(pt[0, :, lanes], (c0h[...], c0l[...]))
    u1 = before[1][...] + nn2r(left, (p1h[...], p1l[...]))
    s1 = before[2][...] + nn2r(left, (c1h[...], c1l[...]))
    n2 = before[3][...] + nn2r(pt[2, c_rows, lanes], (c1h[...], c1l[...]))
    s2 = before[4][...] + nn2r(pt[2, :, lanes], (c2h[...], c2l[...]))
    scale = 1.0 / rows

    def whole(s):
        mine, theirs = diag_ref[s], diag_other_ref[s]
        return jnp.concatenate([jnp.where(col == 0, mine, theirs), jnp.where(col == 0, theirs, mine)], axis=1)

    d0 = whole(0) - s0 * scale
    i1 = s1 - u1.T
    d1 = whole(1) - i1 * scale + nn2r(link_ref[0].T, split2(nn2(split2(d0), link_ref[0])))
    i2 = s2 - nn2(split2(n2), link_ref[1]).T
    d2 = diag_ref[2] - i2 * scale + nn2r(link_ref[1].T, split2(nn2(split2(d1), link_ref[1, :, c_rows])))
    diag_out[0] = jnp.where(col == 0, d0[:, :half_w], d0[:, half_w:])
    diag_out[1] = jnp.where(col == 0, d1[:, :half_w], d1[:, half_w:])
    diag_out[2] = d2


def replicated_plan(inverse_block, factor_cols, occupancy, row_block, coupling, diag_inverse):
    row_parts = lax.axis_size("row")
    supers, span, part = factor_cols.shape
    width = part * row_parts
    local_rows = inverse_block.shape[0]
    rows = local_rows * row_parts
    count = row_parts // 8
    any_spec = pl.BlockSpec(memory_space=pl.ANY)
    smem = pl.BlockSpec(memory_space=pltpu.SMEM)
    vmem = pl.BlockSpec(memory_space=pltpu.VMEM)
    shape = jax.ShapeDtypeStruct

    def call(body, name, flops, **kwargs):
        return pl.pallas_call(
            body,
            compiler_params=pltpu.CompilerParams(vmem_limit_bytes=VMEM_LIMIT),
            cost_estimate=pl.CostEstimate(flops=flops, bytes_accessed=8 * 2**20, transcendentals=0),
            name=name,
            **kwargs,
        )

    outer = row_parts // 4
    x = lambda value: swap(value, "row", 1, row_parts)
    y = lambda value: swap(value, "row", 2, row_parts)
    line = lambda value, k: swap(value, "row", 4 * k, row_parts)

    def far(over_x, over_y, i):
        return x(over_y) if i % 2 == 0 else y(over_x)

    def late_wave(parts, *events):
        own = after(jnp.stack(parts), *events)
        return own, x(own), y(own)

    f_own = jnp.transpose(factor_cols, (0, 2, 1)).reshape(supers * part, span)
    f_late = [line(f_own, k) for k in range(count, outer)]
    own = jnp.concatenate([f_own, inverse_block], axis=0)
    own_again = jnp.concatenate(lax.optimization_barrier([f_own, inverse_block]), axis=0)
    early = []
    for k in range(count):
        value = own if k == 0 else line(own_again, k)
        value = after(value, *early[-1][1:3]) if k else value
        over_x, over_y = x(value), y(value)
        early.append([value, over_x, over_y, far(over_x, over_y, k)])
    first = jnp.stack([jnp.stack([p[j] for p in early]) for j in (3, 2, 1, 0)])
    first_other = across(first)
    block = after(inverse_block, *f_late, *early[-1][1:3])
    z_late = [line(block, k) for k in range(count, outer)]
    f_b, f_bx, f_by = late_wave(f_late, *early[-1][1:3], early[0][3])
    f_bx, f_by = after((f_bx, f_by), *z_late)
    f_far = jnp.stack([far(f_bx[i], f_by[i], i) for i in range(count)])
    f_last = jnp.stack([f_far, f_by, f_bx, f_b])
    f_last_other = across(f_last)
    z_b, z_bx, z_by = late_wave(z_late, f_bx, f_by)
    diag_other = across(diag_inverse)

    pt = call(
        functools.partial(place_kernel, (supers, width, rows, span, part)),
        "place", 2 * 10**9,
        out_shape=shape((supers, width, rows), bf16),
        in_specs=[smem] * 2 + [vmem] * 4,
        out_specs=vmem,
    )(occupancy, row_block, first, f_last, first_other, f_last_other)

    dims = (width, span)
    half_rows, half_w = rows // 2, width // 2
    held_shapes = [(half_rows, width)] * 6 + [(half_rows, half_w)] * 2
    work = [pltpu.VMEM((half_rows, 2 * span), bf16), pltpu.VMEM((half_rows, width), f32), pltpu.SemaphoreType.DMA]
    z_held, *held = call(
        functools.partial(rows_kernel, dims, supers * part),
        "own_half_rows", 3 * 10**9,
        out_shape=tuple(shape(v, bf16) for v in [(half_rows, 2 * span)] + held_shapes[:6]),
        in_specs=[vmem] + [any_spec] * 2 + [vmem],
        out_specs=(vmem,) * 7,
        scratch_shapes=work[1:],
    )(pt, first, first_other, coupling)
    z_bx, z_by, *held = after((z_bx, z_by, *held), held[0])
    z_far = jnp.stack([far(z_bx[i], z_by[i], i) for i in range(count)])
    c0h, c0l, p1h, p1l, c1h, c1l = held
    columns, c2h, c2l = call(
        last_rows_kernel,
        "last_rows", 2 * 10**9,
        out_shape=(shape((supers, local_rows // 2, width), f32),) + (shape((half_rows, half_w), bf16),) * 2,
        in_specs=[vmem] * 7,
        out_specs=(vmem,) * 3,
    )(pt, z_held, c0h, c0l, c1h, c1l, coupling)
    z_far, c0h = after((z_far, c0h), c2h)
    s0, u1 = call(
        functools.partial(early_sums_kernel, count, local_rows),
        "early_sums", 2 * 10**9,
        out_shape=(shape((width, width), f32),) * 2,
        in_specs=[vmem] * 5,
        out_specs=(vmem,) * 2,
    )(pt, c0h, c0l, p1h, p1l)
    z_last = jnp.stack([z_far, z_by, z_bx, z_b])
    z_last_other = across(z_last)
    s1, n2, s2 = call(
        functools.partial(late_sums_kernel, count, local_rows),
        "late_sums", 2 * 10**9,
        out_shape=(shape((width, width), f32), shape((half_w, width), f32), shape((width, half_w), f32)),
        in_specs=[vmem] * 5,
        out_specs=(vmem,) * 3,
    )(pt, c1h, c1l, c2h, c2l)
    sums = [s0, u1, s1, n2, s2]
    diagonals = call(
        functools.partial(last_kernel, dims, rows),
        "other_half", 12 * 10**9,
        out_shape=shape((supers, width, half_w), f32),
        in_specs=[vmem] + [any_spec] * 2 + [vmem] * 8,
        out_specs=vmem,
        scratch_shapes=[pltpu.VMEM(v, bf16) for v in held_shapes] + work,
    )(pt, z_last, z_last_other, coupling, diag_inverse, diag_other, *sums)
    return columns, diagonals


def solution(mesh):
    row_parts, col_parts = mesh.shape["row"], mesh.shape["col"]
    in_specs = (P("row", "col"), P(None, "col", "row"), P(), P(), P(), P(None, None, "col"))
    out_specs = (P(None, ("row", "col"), None), P(None, None, "col"))

    def per_device(inverse_block, factor_cols, *rest):
        held = (inverse_block.size + factor_cols.size) * 2 * row_parts * col_parts
        fits = held <= REPLICATE_BYTES and col_parts == 2 and row_parts in (8, 16)
        plan = replicated_plan if fits else grid_plan
        return plan(inverse_block, factor_cols, *rest)

    return jax.shard_map(
        per_device, mesh=mesh, in_specs=in_specs, out_specs=out_specs, check_vma=False
    )
```

```python
import functools

import jax
import jax.numpy as jnp
from jax import lax
from jax.experimental import pallas as pl
from jax.experimental.pallas import tpu as pltpu
from jax.sharding import PartitionSpec as P

highest = lax.Precision.HIGHEST
f32 = jnp.float32
bf16 = jnp.bfloat16

REPLICATE_BYTES = 12 * 2**20
VMEM_LIMIT = 36 * 2**20


def routed(gathered, occupancy, row_block, nblocks):
    count = gathered.shape[0]
    width_part = gathered.shape[1] // (nblocks * 128)
    blocks = gathered.reshape(count, nblocks, 128, width_part)
    levels = lax.broadcasted_iota(jnp.int32, (count, nblocks, nblocks), 1)
    picks = ((row_block[:, None, :] == levels) & (occupancy[:, None, :] > 0)).astype(jnp.bfloat16)
    placed = jnp.einsum("kqb,kbtx->kxqt", picks, blocks, preferred_element_type=jnp.float32)
    return placed.astype(jnp.bfloat16).reshape(count, width_part, nblocks * 128)


def split_rows(placed, column, row_parts, col_parts, tile):
    count, width_part, total = placed.shape
    span = total // col_parts
    column_part = lax.dynamic_slice_in_dim(placed, column * span, span, 2)
    grid = placed.reshape(count, width_part, row_parts, col_parts, tile)
    mine = lax.dynamic_index_in_dim(grid, column, 3, keepdims=False)
    return (column_part, jnp.transpose(mine, (0, 2, 1, 3)))


def make_term(inverse_block, column_full):
    return lax.dot_general(
        inverse_block, column_full, (((1,), (2,)), ((), ())), preferred_element_type=jnp.float32
    )


def local_step(summed, own_rows, previous, link, diag_part, column, row_first, rows_total):
    if link is None:
        coupled = jnp.zeros_like(summed)
    else:
        coupled = jnp.dot(previous, link.astype(jnp.float32), precision=highest)
    current = -(summed + coupled)
    own = own_rows.astype(jnp.float32)
    inner = jnp.dot(own, current, precision=highest) - jnp.dot(coupled.T, own.T, precision=highest)
    width = summed.shape[1]
    diag_cols = diag_part.shape[1]
    embedded = lax.dynamic_update_slice(
        jnp.zeros((width, width), jnp.float32), diag_part, (0, column * diag_cols)
    )
    return (current, row_first * embedded - inner / rows_total)


def chain_diag(total, chain_prev, link):
    if link is None:
        return total
    link_wide = link.astype(jnp.float32)
    return total + jnp.dot(
        link_wide.T, jnp.dot(chain_prev, link_wide, precision=highest), precision=highest
    )


def grid_plan(inverse_block, factor_cols, occupancy, row_block, coupling, diag_inverse):
    column = lax.axis_index("col")
    row_first = (lax.axis_index("row") == 0).astype(jnp.float32)
    row_parts = lax.axis_size("row")
    col_parts = lax.axis_size("col")
    local_rows = inverse_block.shape[0]
    rows_total = local_rows * row_parts
    supers, span, width_part = factor_cols.shape
    width = width_part * row_parts
    tile = local_rows // col_parts
    nblocks = occupancy.shape[1]
    diag_cols = diag_inverse.shape[2]
    flat = factor_cols.reshape(supers, span * width_part)
    column_list = []
    partial_list = []
    previous = None
    gathered = lax.all_gather(flat, "col", axis=1, tiled=True)
    placed = routed(gathered, occupancy, row_block, nblocks)
    column_part, outgoing = split_rows(placed, column, row_parts, col_parts, tile)
    column_full = lax.all_gather(column_part, "row", axis=1, tiled=True)
    arrived = lax.all_to_all(outgoing, "row", split_axis=1, concat_axis=1, tiled=True)
    own_all = arrived.reshape(supers, width, tile)
    summed = lax.psum_scatter(
        make_term(inverse_block, column_full), "col", scatter_dimension=0, tiled=True
    )
    for position in range(supers):
        link = None if position == 0 else coupling[position - 1]
        current, partial_value = local_step(
            summed[:, position, :],
            own_all[position],
            previous,
            link,
            diag_inverse[position],
            column,
            row_first,
            rows_total,
        )
        column_list.append(current)
        partial_list.append(partial_value)
        previous = current
    diag_list = []
    totals = lax.psum(jnp.stack(partial_list), ("row", "col"))
    chain_prev = None
    for position in range(supers):
        link = None if position == 0 else coupling[position - 1]
        diag_now = chain_diag(totals[position], chain_prev, link)
        diag_list.append(lax.dynamic_slice_in_dim(diag_now, column * diag_cols, diag_cols, 1))
        chain_prev = diag_now
    diagonals = jnp.stack(diag_list)
    return (jnp.stack(column_list), diagonals)


def swap(value, axis, bit, parts):
    return lax.ppermute(value, axis, [(i, i ^ bit) for i in range(parts)])


def across(value):
    return lax.ppermute(value, "col", [(0, 1), (1, 0)])


def after(values, *events):
    return lax.optimization_barrier((events, values))[1]


def split2(value):
    high = value.astype(bf16)
    return high, (value - high.astype(f32)).astype(bf16)


def nn(a, b):
    return lax.dot_general(a, b, (((1,), (0,)), ((), ())), preferred_element_type=f32)


def nt(a, b):
    return lax.dot_general(a, b, (((1,), (1,)), ((), ())), preferred_element_type=f32)


def nn2(pair, b):
    return nn(pair[0], b) + nn(pair[1], b)


def nn2r(a, pair):
    return nn(a, pair[0]) + nn(a, pair[1])


def owner_of(row, wave, count, j, i):
    return 4 * ((row // 4) ^ (wave * count + i)) + ((row % 4) ^ (3 - j))


def place_kernel(dims, *refs):
    supers, width, rows, span, part = dims
    occ_ref, block_ref = refs[:2]
    f_refs, pt = refs[2:6], refs[6]
    row, col = lax.axis_index("row"), lax.axis_index("col")
    per_side = span // 128
    for side in range(2):
        target = col if side == 0 else 1 - col
        for s in range(supers):
            for b in range(per_side):
                lanes = pl.ds(pl.multiple_of(block_ref[s, target * per_side + b] * 128, 128), 128)
                for wave in range(2):
                    source = f_refs[2 * side + wave]
                    for j in range(4):
                        for i in range(source.shape[1]):
                            first = owner_of(row, wave, source.shape[1], j, i) * part
                            pt[s, pl.ds(pl.multiple_of(first, part), part), lanes] = source[
                                j, i, s * part : (s + 1) * part, b * 128 : (b + 1) * 128
                            ]
    for s in range(supers):
        for b in range(2 * per_side):

            @pl.when(occ_ref[s, b] == 0)
            def _():
                lanes = pl.ds(pl.multiple_of(block_ref[s, b] * 128, 128), 128)
                pt[s, :, lanes] = jnp.zeros((width, 128), bf16)


def load_rows(wave, skip, span, col, row, z_refs, z_all, sem):
    half_rows = z_all.shape[0]
    copies = []
    for side in range(2):
        target = col if side == 0 else 1 - col
        source = z_refs[side]
        local_rows = source.shape[2] - skip
        for j in range(4):
            for i in range(source.shape[1]):
                place = owner_of(row, wave, source.shape[1], j, i) % (half_rows // local_rows)
                copies.append(
                    pltpu.make_async_copy(
                        source.at[j, i, pl.ds(skip, local_rows)],
                        z_all.at[
                            pl.ds(pl.multiple_of(place * local_rows, local_rows), local_rows),
                            pl.ds(pl.multiple_of(target * span, span), span),
                        ],
                        sem,
                    )
                )
    for copy in copies:
        copy.start()
    for copy in copies:
        copy.wait()


def halves(col, half_w):
    return pl.ds(pl.multiple_of(col * half_w, half_w), half_w)


def lanes_of(row, wave, local_rows, half_rows, count):
    half = owner_of(row, wave, count, 0, 0) // (half_rows // local_rows)
    return pl.ds(pl.multiple_of(half * half_rows, half_rows), half_rows)


def row_products(pt, link_ref, zm, c_rows, held, tmp):
    c0h, c0l, p1h, p1l, c1h, c1l, c2h, c2l = held
    cols0 = split2(-nt(zm, pt[0]))
    c0h[...], c0l[...] = cols0
    tmp[...] = nn2(cols0, link_ref[0])
    p1h[...], p1l[...] = split2(tmp[...])
    tmp[...] += nt(zm, pt[1])
    cols1 = split2(-tmp[...])
    c1h[...], c1l[...] = cols1
    if c2h is None:
        return
    cols2 = -(nt(zm, pt[2, c_rows, :]) + nn2(cols1, link_ref[1, :, c_rows]))
    c2h[...], c2l[...] = split2(cols2)


def rows_kernel(dims, skip, *refs):
    width, span = dims
    pt, z_refs, link_ref = refs[0], refs[1:3], refs[3]
    z_all, held, tmp, sem = refs[4], refs[5:11], refs[11], refs[12]
    col, row = lax.axis_index("col"), lax.axis_index("row")
    load_rows(0, skip, span, col, row, z_refs, z_all, sem)
    row_products(pt, link_ref, z_all[...], None, (*held, None, None), tmp)


def last_rows_kernel(*refs):
    pt, z_all, c0h, c0l, c1h, c1l, link_ref = refs[:7]
    col_out, c2h, c2l = refs[7:]
    col, row = lax.axis_index("col"), lax.axis_index("row")
    c_rows = halves(col, c2h.shape[1])
    cols1 = (c1h[...], c1l[...])
    cols2 = -(nt(z_all[...], pt[2, c_rows, :]) + nn2(cols1, link_ref[1, :, c_rows]))
    c2h[...], c2l[...] = split2(cols2)
    tile = col_out.shape[1]
    place = row % (z_all.shape[0] // (2 * tile))
    own = pl.ds(pl.multiple_of(place * 2 * tile, 2 * tile), 2 * tile)
    cols1 = (c1h[own, :], c1l[own, :])
    mine = [
        c0h[own, :].astype(f32) + c0l[own, :].astype(f32),
        cols1[0].astype(f32) + cols1[1].astype(f32),
        -(nt(z_all[own, :], pt[2]) + nn2(cols1, link_ref[1])),
    ]
    for s, value in enumerate(mine):
        col_out[s] = jnp.where(col == 0, value[:tile], value[tile:])


def early_sums_kernel(count, local_rows, *refs):
    pt, c0h, c0l, p1h, p1l, s0, u1 = refs
    lanes = lanes_of(lax.axis_index("row"), 0, local_rows, c0h.shape[0], count)
    s0[...] = nn2r(pt[0, :, lanes], (c0h[...], c0l[...]))
    u1[...] = nn2r(pt[1, :, lanes], (p1h[...], p1l[...]))


def late_sums_kernel(count, local_rows, *refs):
    pt, c1h, c1l, c2h, c2l = refs[:5]
    s1, n2, s2 = refs[5:]
    col, row = lax.axis_index("col"), lax.axis_index("row")
    half_rows, half_w = c2h.shape
    lanes = lanes_of(row, 0, local_rows, half_rows, count)
    s1[...] = nn2r(pt[1, :, lanes], (c1h[...], c1l[...]))
    n2[...] = nn2r(pt[2, halves(col, half_w), lanes], (c1h[...], c1l[...]))
    s2[...] = nn2r(pt[2, :, lanes], (c2h[...], c2l[...]))


def last_kernel(dims, rows, *refs):
    width, span = dims
    pt, z_refs, link_ref, diag_ref, diag_other_ref = refs[0], refs[1:3], refs[3], refs[4], refs[5]
    before, diag_out, held, z_all, tmp, sem = refs[6:11], refs[11], refs[12:20], refs[20], refs[21], refs[22]
    col, row = lax.axis_index("col"), lax.axis_index("row")
    half_w = width // 2
    half_rows = z_all.shape[0]
    c_rows = halves(col, half_w)
    load_rows(1, 0, span, col, row, z_refs, z_all, sem)
    row_products(pt, link_ref, z_all[...], c_rows, held, tmp)
    c0h, c0l, p1h, p1l, c1h, c1l, c2h, c2l = held
    lanes = lanes_of(row, 1, z_refs[0].shape[2], half_rows, z_refs[0].shape[1])
    left = pt[1, :, lanes]
    s0 = before[0][...] + nn2r(pt[0, :, lanes], (c0h[...], c0l[...]))
    u1 = before[1][...] + nn2r(left, (p1h[...], p1l[...]))
    s1 = before[2][...] + nn2r(left, (c1h[...], c1l[...]))
    n2 = before[3][...] + nn2r(pt[2, c_rows, lanes], (c1h[...], c1l[...]))
    s2 = before[4][...] + nn2r(pt[2, :, lanes], (c2h[...], c2l[...]))
    scale = 1.0 / rows

    def whole(s):
        mine, theirs = diag_ref[s], diag_other_ref[s]
        return jnp.concatenate([jnp.where(col == 0, mine, theirs), jnp.where(col == 0, theirs, mine)], axis=1)

    d0 = whole(0) - s0 * scale
    i1 = s1 - u1.T
    d1 = whole(1) - i1 * scale + nn2r(link_ref[0].T, split2(nn2(split2(d0), link_ref[0])))
    i2 = s2 - nn2(split2(n2), link_ref[1]).T
    d2 = diag_ref[2] - i2 * scale + nn2r(link_ref[1].T, split2(nn2(split2(d1), link_ref[1, :, c_rows])))
    diag_out[0] = jnp.where(col == 0, d0[:, :half_w], d0[:, half_w:])
    diag_out[1] = jnp.where(col == 0, d1[:, :half_w], d1[:, half_w:])
    diag_out[2] = d2


def replicated_plan(inverse_block, factor_cols, occupancy, row_block, coupling, diag_inverse):
    row_parts = lax.axis_size("row")
    supers, span, part = factor_cols.shape
    width = part * row_parts
    local_rows = inverse_block.shape[0]
    rows = local_rows * row_parts
    count = row_parts // 8
    any_spec = pl.BlockSpec(memory_space=pl.ANY)
    smem = pl.BlockSpec(memory_space=pltpu.SMEM)
    vmem = pl.BlockSpec(memory_space=pltpu.VMEM)
    shape = jax.ShapeDtypeStruct

    def call(body, name, flops, **kwargs):
        return pl.pallas_call(
            body,
            compiler_params=pltpu.CompilerParams(vmem_limit_bytes=VMEM_LIMIT),
            cost_estimate=pl.CostEstimate(flops=flops, bytes_accessed=8 * 2**20, transcendentals=0),
            name=name,
            **kwargs,
        )

    outer = row_parts // 4
    x = lambda value: swap(value, "row", 1, row_parts)
    y = lambda value: swap(value, "row", 2, row_parts)
    line = lambda value, k: swap(value, "row", 4 * k, row_parts)

    def far(over_x, over_y, i):
        return x(over_y) if i % 2 == 0 else y(over_x)

    def late_wave(parts, *events):
        own = after(jnp.stack(parts), *events)
        return own, x(own), y(own)

    f_own = jnp.transpose(factor_cols, (0, 2, 1)).reshape(supers * part, span)
    f_late = [line(f_own, k) for k in range(count, outer)]
    own = jnp.concatenate([f_own, inverse_block], axis=0)
    own_again = jnp.concatenate(lax.optimization_barrier([f_own, inverse_block]), axis=0)
    early = []
    for k in range(count):
        value = own if k == 0 else line(own_again, k)
        value = after(value, *early[-1][1:3]) if k else value
        over_x, over_y = x(value), y(value)
        early.append([value, over_x, over_y, far(over_x, over_y, k)])
    first = jnp.stack([jnp.stack([p[j] for p in early]) for j in (3, 2, 1, 0)])
    first_other = across(first)
    block = after(inverse_block, *f_late, *early[-1][1:3])
    z_late = [line(block, k) for k in range(count, outer)]
    f_b, f_bx, f_by = late_wave(f_late, *early[-1][1:3], early[0][3])
    f_bx, f_by = after((f_bx, f_by), *z_late)
    f_far = jnp.stack([far(f_bx[i], f_by[i], i) for i in range(count)])
    f_last = jnp.stack([f_far, f_by, f_bx, f_b])
    f_last_other = across(f_last)
    z_b, z_bx, z_by = late_wave(z_late, f_bx, f_by)
    diag_other = across(diag_inverse)

    pt = call(
        functools.partial(place_kernel, (supers, width, rows, span, part)),
        "place", 2 * 10**9,
        out_shape=shape((supers, width, rows), bf16),
        in_specs=[smem] * 2 + [vmem] * 4,
        out_specs=vmem,
    )(occupancy, row_block, first, f_last, first_other, f_last_other)

    dims = (width, span)
    half_rows, half_w = rows // 2, width // 2
    held_shapes = [(half_rows, width)] * 6 + [(half_rows, half_w)] * 2
    work = [pltpu.VMEM((half_rows, 2 * span), bf16), pltpu.VMEM((half_rows, width), f32), pltpu.SemaphoreType.DMA]
    z_held, *held = call(
        functools.partial(rows_kernel, dims, supers * part),
        "own_half_rows", 3 * 10**9,
        out_shape=tuple(shape(v, bf16) for v in [(half_rows, 2 * span)] + held_shapes[:6]),
        in_specs=[vmem] + [any_spec] * 2 + [vmem],
        out_specs=(vmem,) * 7,
        scratch_shapes=work[1:],
    )(pt, first, first_other, coupling)
    z_bx, z_by, *held = after((z_bx, z_by, *held), held[0])
    z_far = jnp.stack([far(z_bx[i], z_by[i], i) for i in range(count)])
    c0h, c0l, p1h, p1l, c1h, c1l = held
    columns, c2h, c2l = call(
        last_rows_kernel,
        "last_rows", 2 * 10**9,
        out_shape=(shape((supers, local_rows // 2, width), f32),) + (shape((half_rows, half_w), bf16),) * 2,
        in_specs=[vmem] * 7,
        out_specs=(vmem,) * 3,
    )(pt, z_held, c0h, c0l, c1h, c1l, coupling)
    s1, n2, s2 = call(
        functools.partial(late_sums_kernel, count, local_rows),
        "late_sums", 2 * 10**9,
        out_shape=(shape((width, width), f32), shape((half_w, width), f32), shape((width, half_w), f32)),
        in_specs=[vmem] * 5,
        out_specs=(vmem,) * 3,
    )(pt, c1h, c1l, c2h, c2l)
    z_far, c0h = after((z_far, c0h), s1)
    z_last = jnp.stack([z_far, z_by, z_bx, z_b])
    z_last_other = across(z_last)
    s0, u1 = call(
        functools.partial(early_sums_kernel, count, local_rows),
        "early_sums", 2 * 10**9,
        out_shape=(shape((width, width), f32),) * 2,
        in_specs=[vmem] * 5,
        out_specs=(vmem,) * 2,
    )(pt, c0h, c0l, p1h, p1l)
    sums = [s0, u1, s1, n2, s2]
    diagonals = call(
        functools.partial(last_kernel, dims, rows),
        "other_half", 12 * 10**9,
        out_shape=shape((supers, width, half_w), f32),
        in_specs=[vmem] + [any_spec] * 2 + [vmem] * 8,
        out_specs=vmem,
        scratch_shapes=[pltpu.VMEM(v, bf16) for v in held_shapes] + work,
    )(pt, z_last, z_last_other, coupling, diag_inverse, diag_other, *sums)
    return columns, diagonals


def solution(mesh):
    row_parts, col_parts = mesh.shape["row"], mesh.shape["col"]
    in_specs = (P("row", "col"), P(None, "col", "row"), P(), P(), P(), P(None, None, "col"))
    out_specs = (P(None, ("row", "col"), None), P(None, None, "col"))

    def per_device(inverse_block, factor_cols, *rest):
        held = (inverse_block.size + factor_cols.size) * 2 * row_parts * col_parts
        fits = held <= REPLICATE_BYTES and col_parts == 2 and row_parts in (8, 16)
        plan = replicated_plan if fits else grid_plan
        return plan(inverse_block, factor_cols, *rest)

    return jax.shard_map(
        per_device, mesh=mesh, in_specs=in_specs, out_specs=out_specs, check_vma=False
    )
```
